32 devices in a mesh: dp: 8 (over y, x, core), group: 4 (over z).
Axes of the slice: x: 2, y: 2, z: 4, core: 2. Of those that a mesh axis runs over, the one named last changes fastest.
Arguments:
- question_tokens: bfloat16 [512, 64, 768], P(('dp', 'group')), may hold values from -6 to 6
- question_lengths: int32 [512], P(('dp', 'group')), may hold values from 16 to 64
- passage_tokens: bfloat16 [128, 256, 768], P(('dp', 'group')), may hold values from -6 to 6
- passage_lengths: int32 [128, 4], P(('dp', 'group')), may hold values from 1 to 128, 256 in all within a row
- positives: int32 [512], P(('dp', 'group')), may hold values from 0 to 511
- w_qkv: bfloat16 [2, 768, 2304], replicated, may hold values from -0.21875 to 0.21875
- qv_bias: float32 [2, 2, 768], replicated, may hold values from -3 to 3
- w_out: bfloat16 [2, 768, 768], replicated, may hold values from -1.5 to 1.5
- out_bias: float32 [2, 768], replicated, may hold values from -3 to 3
- norm_gains: float32 [2, 2, 768], replicated, may hold values from 0.1 to 1.9
- norm_biases: float32 [2, 2, 768], replicated, may hold values from -3 to 3
- w_in: bfloat16 [2, 768, 3072], replicated, may hold values from -0.21875 to 0.21875
- in_bias: float32 [2, 3072], replicated, may hold values from -3 to 3
- w_back: bfloat16 [2, 3072, 768], replicated, may hold values from -0.109375 to 0.109375
- back_bias: float32 [2, 768], replicated, may hold values from -3 to 3
Outputs:
- question_vectors: bfloat16 [512, 768], P(('dp', 'group'))
- passage_vectors: bfloat16 [512, 768], P(('dp', 'group'))
- losses: float32 [512], P(('dp', 'group'))
- grad_question_tokens: float32 [512, 64, 768], P(('dp', 'group'))
- grad_passage_tokens: float32 [128, 256, 768], P(('dp', 'group'))
- grad_w_qkv: float32 [2, 768, 2304], P(None, 'dp')
- grad_qv_bias: float32 [2, 2, 768], replicated
- grad_w_out: float32 [2, 768, 768], P(None, 'dp')
- grad_out_bias: float32 [2, 768], replicated
- grad_norm_gains: float32 [2, 2, 768], replicated
- grad_norm_biases: float32 [2, 2, 768], replicated
- grad_w_in: float32 [2, 768, 3072], P(None, 'dp')
- grad_in_bias: float32 [2, 3072], replicated
- grad_w_back: float32 [2, 3072, 768], P(None, 'dp')
- grad_back_bias: float32 [2, 768], replicated
The draws below stay inside these ranges and needn't reach their ends.
Inputs may be any that keep to these rules, and one draw needn't show every extreme that they name: `question_lengths`: positions at and after a question's length are padding. `passage_lengths`: the 4 lengths of a row sum to 256. `positives`: index among all 512 passages.
All inputs are finite; a program needn't handle non-finite values.
Results may differ from the reference program's by a relative error of at most 0.018.
Values may be sent and summed in bfloat16 or wider, within the bound.
No kernel may reach another device: no remote copies, remote signals or barrier semaphores. Data moves between devices by JAX's collectives and lax.ppermute only.
A program may use at most 384 MiB of HBM per device.

```python
import math
import jax
import jax.numpy as jnp
import numpy as np
from jax import lax

D = 768
HEADS = 12
HEAD_DIM = 64
FF = 3072
QLEN = 64
SEQ = 256
PACK = 4
NQ = 512
NR = 128
NP = 512


def place_ends(drawn, stream_key, low, high):
    longest = drawn.shape.index(max(drawn.shape))
    spots = []
    for shift in (0, 1):
        where = [jax.random.randint(jax.random.fold_in(stream_key, axis), (), 0, length) for axis, length in enumerate(drawn.shape)]
        where[longest] = (where[longest] + shift) % drawn.shape[longest]
        spots.append(tuple(where))
    return drawn.at[spots[0]].set(low).at[spots[1]].set(high)


def block_scale(key, shape, shards, low, top_value):
    def one(axis_at, parts):
        draws = jax.random.uniform(jax.random.fold_in(jax.random.fold_in(key, 6), axis_at), (parts,), jnp.float32, low / len(shards), top_value / len(shards))
        return jnp.repeat(jnp.exp(draws), shape[axis_at] // parts).reshape((-1,) + (1,) * (len(shape) - axis_at - 1))

    level = one(*shards[0])
    for cut in shards[1:]:
        level = level * one(*cut)
    return level


def length_profile(number_of, total, bound, slope):
    weights = [(1 << 20) // math.isqrt(grade ** slope) + 1 for grade in range(2, number_of + 1)]
    rest, given = total - bound - (number_of - 1), [1] * (number_of - 1)
    while rest > 0:
        candidates = [i for i in range(number_of - 1) if given[i] < bound]
        pool, budget = sum([weights[i] for i in candidates]), rest
        for i in candidates:
            extra = min(bound - given[i], max(1, budget * weights[i] // pool), rest)
            given[i] = given[i] + extra
            rest = rest - extra
    return np.array([bound] + given)


def uneven_parts(own_key, amount, total, limit, lean):
    if amount == 2:
        one = jax.random.randint(own_key, (), max(1, total - limit), min(limit, total - 1) + 1)
        return jnp.stack([one, total - one])
    tallies = jnp.asarray(length_profile(amount, total, limit, lean), jnp.int32)
    couples = (amount - 1) // 2
    donor, receiver = tallies[1:1 + 2 * couples:2], tallies[2:2 + 2 * couples:2]
    room = jnp.minimum(donor - 1, limit - receiver)
    passed = jax.random.randint(jax.random.fold_in(own_key, 1), (couples,), 0, 1 << 20) % (room + 1)
    tallies = tallies.at[1:1 + 2 * couples:2].set(donor - passed).at[2:2 + 2 * couples:2].set(receiver + passed)
    return tallies[jax.random.permutation(jax.random.fold_in(own_key, 2), amount)]


def scatter_about(rng, dims, scale, limit, split=(), kind=jnp.bfloat16):
    loudness = block_scale(rng, dims, split, -0.22, 0.18) if split else 1.0
    result = jax.random.normal(rng, dims, jnp.float32) * scale * loudness
    return jnp.minimum(jnp.maximum(result, -limit), limit).astype(kind)


def setup_inputs(seed: int = 0) -> dict:
    splits = jax.random.split(jax.random.key(seed), 16)
    return {
        "question_tokens": scatter_about(splits[0], (NQ, QLEN, D), 1.0, 6.0, ((0, 32),)),
        "question_lengths": place_ends(jax.random.randint(splits[1], (NQ,), QLEN // 4, QLEN + 1), jax.random.fold_in(splits[1], 1), QLEN // 4, QLEN).astype(jnp.int32),
        "passage_tokens": scatter_about(splits[2], (NR, SEQ, D), 1.0, 6.0, ((0, 32),)),
        "passage_lengths": jax.vmap(lambda own: uneven_parts(own, PACK, SEQ, SEQ // 2, 2))(jax.random.split(splits[3], NR)).reshape((NR, PACK)).astype(jnp.int32),
        "positives": place_ends(jax.random.randint(splits[4], (NQ,), 0, NP), jax.random.fold_in(splits[4], 1), 0, NP - 1).astype(jnp.int32),
        "w_qkv": scatter_about(splits[5], (2, D, 3 * D), D ** -0.5, 0.21875),
        "qv_bias": scatter_about(splits[6], (2, 2, D), 0.5, 3.0, (), jnp.float32),
        "w_out": scatter_about(splits[7], (2, D, D), (max(D // 48, 1)) ** -0.5, 1.5),
        "out_bias": scatter_about(splits[8], (2, D), 0.5, 3.0, (), jnp.float32),
        "norm_gains": jnp.clip(1.0 + 0.18 * jax.random.normal(splits[9], (2, 2, D), jnp.float32), 0.1, 1.9),
        "norm_biases": scatter_about(splits[10], (2, 2, D), 0.5, 3.0, (), jnp.float32),
        "w_in": scatter_about(splits[11], (2, D, FF), D ** -0.5, 0.21875),
        "in_bias": scatter_about(splits[12], (2, FF), 0.5, 3.0, (), jnp.float32),
        "w_back": scatter_about(splits[13], (2, FF, D), FF ** -0.5, 0.109375),
        "back_bias": scatter_about(splits[14], (2, D), 0.5, 3.0, (), jnp.float32),
    }


HIGH = lax.Precision.HIGHEST
EPSILON = 1e-12
MASKED = -1000000000.0

@jax.custom_vjp
def low(v):
    return lax.optimization_barrier(v.astype(jnp.bfloat16)).astype(jnp.float32)

@jax.custom_vjp
def low_back(v):
    return v

def low_keep(v):
    return (low(v), None)

def low_pass(kept, grad):
    return (grad,)

def back_keep(v):
    return (v, None)

def back_low(kept, grad):
    return (low(grad),)
low.defvjp(low_keep, low_pass)
low_back.defvjp(back_keep, back_low)

def matmul(left, right):
    return jnp.dot(left, right, precision=HIGH)

def layer_norm(hidden, gain_row, shift_row):
    row_mean = lax.optimization_barrier(jnp.mean(hidden, axis=-1, keepdims=True))
    centred = hidden - row_mean
    variance = lax.optimization_barrier(jnp.mean(centred * centred, axis=-1, keepdims=True))
    return centred * lax.rsqrt(variance + EPSILON) * gain_row + shift_row

def softmax_rows(scores):
    row_peak = lax.optimization_barrier(jnp.max(scores, axis=-1, keepdims=True))
    shifted = jnp.exp(scores - row_peak)
    return shifted / lax.optimization_barrier(jnp.sum(shifted, axis=-1, keepdims=True))

def encoder_layer(tokens_in, allowed, params):
    qkv_weight, qkv_bias, out_weight, out_shift, gain_pair, shift_pair, in_weight, in_shift, back_weight, back_shift = params
    seq_count, length = (tokens_in.shape[0], tokens_in.shape[1])
    token_rows = tokens_in.reshape(seq_count * length, D)
    projected = low(low_back(matmul(token_rows, qkv_weight)) + qkv_bias)
    projected = projected.reshape(seq_count, length, 3, HEADS, HEAD_DIM)
    queries = projected[:, :, 0]
    key_part = projected[:, :, 1]
    value_part = projected[:, :, 2]
    scores = low_back(jnp.einsum('bqhd,bkhd->bhqk', queries, key_part, precision=HIGH) * 0.125)
    scores = jnp.where(allowed[:, None], scores, MASKED)
    attn_probs = low(softmax_rows(scores))
    context = jnp.einsum('bhqk,bkhd->bqhd', attn_probs, value_part, precision=HIGH)
    context = low(low_back(context)).reshape(seq_count * length, D)
    hidden = token_rows + low_back(matmul(context, out_weight)) + out_shift
    normed = layer_norm(hidden, gain_pair[0], shift_pair[0])
    pre_act = low_back(matmul(low(normed), in_weight)) + in_shift
    active = low(jax.nn.gelu(pre_act, approximate=False))
    second = normed + low_back(matmul(active, back_weight)) + back_shift
    return layer_norm(second, gain_pair[1], shift_pair[1]).reshape(seq_count, length, D)

def question_mask(lengths):
    positions = jnp.arange(QLEN, dtype=jnp.int32)
    visible = positions[None, :] < lengths[:, None]
    return jnp.broadcast_to(visible[:, None, :], (lengths.shape[0], QLEN, QLEN))

def passage_layout(lengths):
    positions = jnp.arange(SEQ, dtype=jnp.int32)
    doc_starts = (jnp.cumsum(lengths, axis=-1) - lengths).astype(jnp.int32)
    doc_ids = lax.optimization_barrier(jnp.sum((positions[None, :, None] >= doc_starts[:, None, :]).astype(jnp.int32), axis=-1))
    allowed = doc_ids[:, :, None] == doc_ids[:, None, :]
    selector = (positions[None, None, :] == doc_starts[:, :, None]).astype(jnp.float32)
    return (allowed, selector)

def reference(question_tokens, question_lengths, passage_tokens, passage_lengths, positives, w_qkv, qv_bias, w_out, out_bias, norm_gains, norm_biases, w_in, in_bias, w_back, back_bias):
    q_block = math.gcd(NQ, max(1, 4096 // QLEN))
    r_block = math.gcd(NR, max(1, 4096 // SEQ))
    score_scale = 2.0 / math.sqrt(D)
    q_lengths = question_lengths.reshape(NQ // q_block, q_block)
    p_lengths = passage_lengths.reshape(NR // r_block, r_block, PACK)
    target = (jnp.arange(NP, dtype=jnp.int32)[None, :] == positives[:, None]).astype(jnp.float32)

    def objective(question_in, passage_in, qkv_weight, bias_pair, out_weight, out_shift, gain_pairs, shift_pairs, in_weight, in_shift, back_weight, back_shift):

        def params_of(encoder):
            qkv_bias = jnp.concatenate([bias_pair[encoder, 0], jnp.zeros_like(bias_pair[encoder, 0]), bias_pair[encoder, 1]])
            return (qkv_weight[encoder], qkv_bias, out_weight[encoder], out_shift[encoder], gain_pairs[encoder], shift_pairs[encoder], in_weight[encoder], in_shift[encoder], back_weight[encoder], back_shift[encoder])
        q_params = params_of(0)
        p_params = params_of(1)

        def question_block(inputs):
            block_tokens, block_lengths = inputs
            encoded = encoder_layer(block_tokens, question_mask(block_lengths), q_params)
            return encoded[:, 0, :]

        def passage_block(inputs):
            block_tokens, block_lengths = inputs
            allowed, selector = passage_layout(block_lengths)
            encoded = encoder_layer(block_tokens, allowed, p_params)
            return jnp.einsum('rks,rsd->rkd', selector, encoded, precision=HIGH).reshape(r_block * PACK, D)
        q_cls = lax.map(jax.checkpoint(question_block), (question_in.reshape(NQ // q_block, q_block, QLEN, D), q_lengths)).reshape(NQ, D)
        p_cls = lax.map(jax.checkpoint(passage_block), (passage_in.reshape(NR // r_block, r_block, SEQ, D), p_lengths)).reshape(NP, D)
        q_vec = low(q_cls)
        p_vec = low(p_cls)
        scores = matmul(q_vec, p_vec.T) * score_scale
        row_peak = lax.optimization_barrier(jnp.max(scores, axis=-1, keepdims=True))
        log_total = row_peak[:, 0] + jnp.log(lax.optimization_barrier(jnp.sum(jnp.exp(scores - row_peak), axis=-1)))
        losses = log_total - lax.optimization_barrier(jnp.sum(scores * target, axis=-1))
        return (jnp.sum(losses), (q_vec, p_vec, losses))
    floats = (question_tokens.astype(jnp.float32), passage_tokens.astype(jnp.float32), w_qkv.astype(jnp.float32), qv_bias, w_out.astype(jnp.float32), out_bias, norm_gains, norm_biases, w_in.astype(jnp.float32), in_bias, w_back.astype(jnp.float32), back_bias)
    summed, pullback, extras = jax.vjp(objective, *floats, has_aux=True)
    gradients = pullback(jnp.ones_like(summed))
    q_vec, p_vec, losses = extras
    return (q_vec.astype(jnp.bfloat16), p_vec.astype(jnp.bfloat16), losses, gradients[0], gradients[1], gradients[2], gradients[3], gradients[4], gradients[5], gradients[6], gradients[7], gradients[8], gradients[9], gradients[10], gradients[11])
```

```python
import functools
import math

import jax
import jax.numpy as jnp
from jax import lax
from jax.experimental import pallas as pl
from jax.experimental.pallas import tpu as pltpu
from jax.sharding import PartitionSpec as P

HEAD_DIM = 64
EPSILON = 1e-12
MASKED = -1000000000.0
EXTRA = 128
BF = jnp.bfloat16
F32 = jnp.float32

NT = (((1,), (1,)), ((), ()))
TN = (((0,), (0,)), ((), ()))
NN = (((1,), (0,)), ((), ()))


def mm(left, right, dims=NN):
    return lax.dot_general(left, right, dims, preferred_element_type=F32)


def row_bounds(packed, len_ref, rows, length):
    bounds = []
    for r in range(rows):
        if packed:
            row, k = r // packed, r % packed
            start = row * length
            for earlier in range(k):
                start = start + len_ref[row, earlier]
            bounds.append((start, start + len_ref[row, k]))
        else:
            bounds.append((r * length, r * length + len_ref[r]))
    return bounds


def column(values, rows):
    at = lax.broadcasted_iota(jnp.int32, (rows, 1), 0)
    result = jnp.zeros((rows, 1), jnp.int32)
    for r, value in enumerate(values):
        result = jnp.where(at == r, value, result)
    return result


def head_mask(rows, heads, width):
    row_head = lax.broadcasted_iota(jnp.int32, (rows * heads, width), 0) // rows
    col_head = lax.broadcasted_iota(jnp.int32, (rows * heads, width), 1) // HEAD_DIM
    return row_head == col_head


def spread_heads(values, heads, mask):
    tiled = jnp.concatenate([values] * heads, axis=0)
    return jnp.where(mask, tiled, jnp.zeros_like(tiled))


def gather_heads(full, heads, rows, mask):
    kept = jnp.where(mask, full, jnp.zeros_like(full))
    return jnp.sum(kept.reshape(heads, rows, full.shape[1]), axis=0)


def attend_kernel(encoder, packed, length, rows, heads, len_ref, pos_ref, x_ref, w_ref, bias_ref, wo_ref, ob_ref,
                  pack_ref, bundle_ref, a_ref, p_ref):
    tokens, width = x_ref.shape
    bounds = row_bounds(packed, len_ref, rows, length)
    start = column([b[0] for b in bounds], rows)
    stop = column([b[1] for b in bounds], rows)
    lane = lax.broadcasted_iota(jnp.int32, (rows, tokens), 1)
    x = x_ref[...]
    pick = jnp.where(lane == start, 1.0, 0.0).astype(BF)
    x_cls = mm(pick, x)
    xc = x_cls.astype(BF)
    bias = bias_ref[encoder]
    q = (mm(xc, w_ref[0, :, 0:width]) + bias[0:1, :]).astype(BF)
    mask = head_mask(rows, heads, width)
    a_low = mm(spread_heads(q, heads, mask), w_ref[0, :, width:2 * width], NT).astype(BF)
    a_ref[...] = a_low
    scores = mm(a_low, x, NT) * 0.125
    lane_all = lax.broadcasted_iota(jnp.int32, scores.shape, 1)
    starts = jnp.concatenate([start] * heads, axis=0)
    stops = jnp.concatenate([stop] * heads, axis=0)
    scores = jnp.where((lane_all >= starts) & (lane_all < stops), scores, MASKED)
    peak = jnp.max(scores, axis=1, keepdims=True)
    shifted = jnp.exp(scores - peak)
    p = shifted / jnp.sum(shifted, axis=1, keepdims=True)
    p_ref[...] = p
    p_low = p.astype(BF)
    sums = jnp.sum(p_low.astype(F32), axis=1, keepdims=True)
    pooled = mm(p_low, x).astype(BF)
    full = mm(pooled, w_ref[0, :, 2 * width:3 * width]) + sums * bias[1:2, :]
    ctx = gather_heads(full, heads, rows, mask).astype(BF)
    hidden = x_cls + mm(ctx, wo_ref[0]) + ob_ref[encoder:encoder + 1, :]
    mean = jnp.mean(hidden, axis=1, keepdims=True)
    centred = hidden - mean
    rstd = lax.rsqrt(jnp.mean(centred * centred, axis=1, keepdims=True) + EPSILON)
    pack_ref[:, 0:width] = (centred * rstd).astype(BF)
    rstd_high = rstd.astype(BF).astype(F32)
    pos = column([pos_ref[r] for r in range(rows)], rows)
    lanes = lax.broadcasted_iota(jnp.int32, (rows, EXTRA), 1)
    extra = jnp.where(lanes == 0, rstd_high, 0.0)
    extra = jnp.where(lanes == 1, rstd - rstd_high, extra)
    extra = jnp.where(lanes == 2, (pos // 32).astype(F32), extra)
    extra = jnp.where(lanes == 3, (pos % 32).astype(F32), extra)
    for h in range(heads):
        extra = jnp.where(lanes == 16 + h, sums[h * rows:(h + 1) * rows] - 1.0, extra)
    pack_ref[:, width:] = extra.astype(BF)
    bundle_ref[0:heads * rows, :] = pooled
    bundle_ref[heads * rows:(heads + 1) * rows, :] = xc
    bundle_ref[(heads + 1) * rows:(heads + 2) * rows, :] = ctx
    bundle_ref[(heads + 2) * rows:(heads + 3) * rows, :] = q


def gelu_parts(x):
    cdf = 0.5 * (1.0 + lax.erf(x * math.sqrt(0.5)))
    slope = cdf + x * jnp.exp(-0.5 * x * x) * (1.0 / math.sqrt(2.0 * math.pi))
    return x * cdf, slope


def over_rows(count, tile, work):
    if tile == count:
        work(pl.ds(0, count))
    else:
        def one(t, carry):
            work(pl.ds(pl.multiple_of(t * tile, tile), tile))
            return carry

        lax.fori_loop(0, count // tile, one, 0)


def forward_kernel(chips, depth, rows, steps, tile, ids, *refs):
    blocks = refs[:chips]
    gain_ref, shift_ref, win_ref, inb_ref, wback_ref, backb_ref = refs[chips:chips + 6]
    act_ref, slope_ref, vec_ref, hat2_ref, ex_ref, nl_ref, hat1_ref, total = refs[chips + 6:]
    c, j, z = ids[0], ids[1], ids[2]
    width = nl_ref.shape[1]
    step = pl.program_id(0)

    @pl.when(step == 0)
    def start():
        for kx in range(chips):
            for kz in range(depth):
                for kc in range(2):
                    core = c if kc == 0 else 1 - c
                    place = ((lax.rem(j - kx + chips, chips) * depth + lax.rem(z - kz + depth, depth)) * 2 + core) * rows
                    place = pl.multiple_of(place, rows)
                    at = (kz * 2 + kc) * rows
                    hat1_ref[pl.ds(place, rows), :] = blocks[kx][at:at + rows, 0:width]
                    ex_ref[pl.ds(place, rows), :] = blocks[kx][at:at + rows, width:].astype(F32)
        gain = gain_ref[c]
        shift = shift_ref[c]
        normed = hat1_ref[...].astype(F32) * gain[0:1, :] + shift[0:1, :]
        nl_ref[...] = normed.astype(BF)
        total[...] = normed + backb_ref[pl.ds(c, 1), :]

    columns = win_ref.shape[2]
    pre = mm(nl_ref[...], win_ref[0]) + inb_ref[pl.ds(c, 1), pl.ds(pl.multiple_of(step * columns, columns), columns)]
    active, slope = gelu_parts(pre)
    active = active.astype(BF)
    act_ref[...] = active
    slope_ref[...] = slope.astype(BF)
    total[...] += mm(active, wback_ref[0])

    @pl.when(step == steps - 1)
    def finish():
        gain = gain_ref[c]
        shift = shift_ref[c]

        def normalise(part):
            second = total[part, :]
            mean = jnp.mean(second, axis=1, keepdims=True)
            centred = second - mean
            rstd = lax.rsqrt(jnp.mean(centred * centred, axis=1, keepdims=True) + EPSILON)
            hat = centred * rstd
            hat2_ref[part, :] = hat.astype(BF)
            vec_ref[part, :] = (hat * gain[1:2, :] + shift[1:2, :]).astype(BF)
            ex = ex_ref[part, :]
            lanes = lax.broadcasted_iota(jnp.int32, ex.shape, 1)
            pos = ex[:, 2:3] * 32.0 + ex[:, 3:4]
            ex_ref[part, :] = jnp.where(
                lanes == 0, ex[:, 0:1] + ex[:, 1:2], jnp.where(lanes == 1, rstd, jnp.where(lanes == 2, pos, ex)))

        over_rows(total.shape[0], tile, normalise)


def backward_kernel(chips, depth, rows, steps, tile, ids, own_ref, other_ref, ex_ref, hat2_ref, hat1_ref, slope_ref,
                    wback_ref, win_ref, gain_ref, wout_ref,
                    gsl_ref, gpl_ref, inb_ref, gplane_ref, hplane_ref, loss_ref, mine_ref, sib_ref, small_ref,
                    acc, wide_loss, gfull):
    c, j, z = ids[0], ids[1], ids[2]
    count, width = own_ref.shape
    scale = 2.0 / math.sqrt(width)
    step = pl.program_id(0)

    def softmax_part(questions, passages, pos):
        scores = mm(questions, passages, NT) * scale
        peak = jnp.max(scores, axis=1, keepdims=True)
        shifted = jnp.exp(scores - peak)
        totals = jnp.sum(shifted, axis=1, keepdims=True)
        hit = lax.broadcasted_iota(jnp.int32, scores.shape, 1) == pos.astype(jnp.int32)
        loss = peak + jnp.log(totals) - jnp.sum(jnp.where(hit, scores, 0.0), axis=1, keepdims=True)
        grad = (shifted / totals - jnp.where(hit, 1.0, 0.0)) * scale
        high = grad.astype(BF)
        return loss, high, (grad - high.astype(F32)).astype(BF)

    @pl.when(step == 0)
    def start():
        small_ref[...] = jnp.zeros_like(small_ref)

        @pl.when(c == 0)
        def question_side():
            def work(part):
                loss, high, low = softmax_part(own_ref[part, :], other_ref[...], ex_ref[part, 2:3])
                wide_loss[part, :] = jnp.broadcast_to(loss, (tile, wide_loss.shape[1]))
                acc[part, :] = mm(high, other_ref[...]) + mm(low, other_ref[...])

            over_rows(count, tile, work)

        @pl.when(c == 1)
        def passage_side():
            if tile < count:
                acc[...] = jnp.zeros_like(acc)

            def work(part):
                loss, high, low = softmax_part(other_ref[part, :], own_ref[...], ex_ref[part, 2:3])
                wide_loss[part, :] = jnp.broadcast_to(loss, (tile, wide_loss.shape[1]))
                piece = mm(high, other_ref[part, :], TN) + mm(low, other_ref[part, :], TN)
                acc[...] = piece if tile == count else acc[...] + piece

            over_rows(count, tile, work)

        own_at = pl.multiple_of(((j * depth + z) * 2 + c) * rows, rows)
        loss_ref[...] = wide_loss[pl.ds(own_at, rows), :]

        def norm_back(part):
            grad = acc[part, :]
            hat = hat2_ref[part, :].astype(F32)
            small_ref[1:2, :] += jnp.sum(grad * hat, axis=0, keepdims=True)
            small_ref[3:4, :] += jnp.sum(grad, axis=0, keepdims=True)
            scaled = grad * gain_ref[c][1:2, :]
            inner = jnp.mean(scaled * hat, axis=1, keepdims=True)
            second = ex_ref[part, 1:2] * (scaled - jnp.mean(scaled, axis=1, keepdims=True) - hat * inner)
            small_ref[5:6, :] += jnp.sum(second, axis=0, keepdims=True)
            acc[part, :] = second
            gsl_ref[part, :] = second.astype(BF)

        over_rows(count, tile, norm_back)

    pre = mm(gsl_ref[...], wback_ref[0], NT) * slope_ref[...].astype(F32)
    inb_ref[...] = jnp.sum(pre, axis=0, keepdims=True)
    pre_low = pre.astype(BF)
    gpl_ref[...] = pre_low
    acc[...] += mm(pre_low, win_ref[0], NT)

    @pl.when(step == steps - 1)
    def finish():
        lanes = lax.broadcasted_iota(jnp.int32, (EXTRA, width), 0)
        heads_of = lax.broadcasted_iota(jnp.int32, (EXTRA, width), 1) // HEAD_DIM
        expand = jnp.where(lanes == heads_of + 16, 1.0, 0.0).astype(BF)

        def norm_back(part):
            grad = acc[part, :]
            hat = hat1_ref[part, :].astype(F32)
            small_ref[0:1, :] += jnp.sum(grad * hat, axis=0, keepdims=True)
            small_ref[2:3, :] += jnp.sum(grad, axis=0, keepdims=True)
            scaled = grad * gain_ref[c][0:1, :]
            inner = jnp.mean(scaled * hat, axis=1, keepdims=True)
            hidden = ex_ref[part, 0:1] * (scaled - jnp.mean(scaled, axis=1, keepdims=True) - hat * inner)
            small_ref[4:5, :] += jnp.sum(hidden, axis=0, keepdims=True)
            acc[part, :] = hidden
            ctx = mm(hidden.astype(BF), wout_ref[0], NT).astype(BF)
            sums = mm(ex_ref[part, :].astype(BF), expand) + 1.0
            small_ref[6:7, :] += jnp.sum(sums * ctx.astype(F32), axis=0, keepdims=True)
            gfull[part, :] = ctx

        over_rows(count, tile, norm_back)
        own_at = pl.multiple_of(((j * depth + z) * 2 + c) * rows, rows)
        sib_at = pl.multiple_of(((j * depth + z) * 2 + 1 - c) * rows, rows)
        mine_ref[:, 0:width] = acc[pl.ds(own_at, rows), :]
        sib_ref[:, 0:width] = acc[pl.ds(sib_at, rows), :]
        mine_ref[:, width:] = gfull[pl.ds(own_at, rows), :].astype(F32)
        sib_ref[:, width:] = gfull[pl.ds(sib_at, rows), :].astype(F32)
        for kx in range(chips):
            for kc in range(2):
                core = c if kc == 0 else 1 - c
                place = pl.multiple_of(((lax.rem(j - kx + chips, chips) * depth + z) * 2 + core) * rows, rows)
                at = (kx * 2 + kc) * rows
                gplane_ref[at:at + rows, :] = gfull[pl.ds(place, rows), :]
                hplane_ref[at:at + rows, :] = acc[pl.ds(place, rows), :].astype(BF)


def attend_back_kernel(encoder, packed, length, rows, heads, len_ref, gg_ref, x_ref, w_ref, bias_ref, p_ref, a_ref,
                       gx_ref, late_ref):
    tokens, width = x_ref.shape
    bounds = row_bounds(packed, len_ref, rows, length)
    x = x_ref[...]
    mask = head_mask(rows, heads, width)
    ctx = gg_ref[:, width:]
    blocks = spread_heads(ctx, heads, mask)
    constant = jnp.sum(blocks * bias_ref[encoder][1:2, :], axis=1, keepdims=True)
    b_low = mm(blocks.astype(BF), w_ref[0, :, 2 * width:3 * width], NT).astype(BF)
    p = p_ref[...]
    probs = mm(b_low, x, NT) + constant
    att = (p * (probs - jnp.sum(probs * p, axis=1, keepdims=True))).astype(BF)
    y_low = mm(att, x).astype(BF)
    late_ref[0:heads * rows, :] = y_low
    gq = gather_heads(mm(y_low, w_ref[0, :, width:2 * width]), heads, rows, mask) * 0.125
    gq_low = gq.astype(BF)
    late_ref[heads * rows:(heads + 1) * rows, :] = gq_low
    gx_ref[...] = mm(att, a_ref[...] * jnp.asarray(0.125, BF), TN) + mm(p.astype(BF), b_low, TN)
    first = gg_ref[:, 0:width] + mm(gq_low, w_ref[0, :, 0:width], NT)
    for r in range(rows):
        at = bounds[r][0]
        gx_ref[pl.ds(at, 1), :] += first[r:r + 1, :]


def full_spec(shape):
    return pl.BlockSpec(shape, lambda *_: (0,) * len(shape))


def body(question_tokens, question_lengths, passage_tokens, passage_lengths, positives, w_qkv, qv_bias, w_out, out_bias,
         norm_gains, norm_biases, w_in, in_bias, w_back, back_bias, *, n_dp, depth):
    width = question_tokens.shape[2]
    heads = width // HEAD_DIM
    rows = question_tokens.shape[0]
    pack = passage_lengths.shape[1]
    ff = w_in.shape[2]
    chips = n_dp // 2
    count = n_dp * depth * rows
    part = width // chips
    i = lax.axis_index("dp")
    z = lax.axis_index("group")
    c, j = i % 2, i // 2
    ids = jnp.stack([c, j, z]).astype(jnp.int32)
    first = c == 0

    def mine_other(a, b):
        return jnp.where(first, a, b), jnp.where(first, b, a)

    def swap(x):
        return lax.ppermute(x, "dp", [(k, k ^ 1) for k in range(n_dp)])

    def to_chip(x, k):
        return lax.ppermute(x, "dp", [(s, ((s // 2 + k) % chips) * 2 + s % 2) for s in range(n_dp)])

    def to_depth(x, k):
        return lax.ppermute(x, "group", [(s, (s + k) % depth) for s in range(depth)])

    def canon(rel, me):
        return jnp.roll(rel[::-1], me + 1, axis=0)

    owner = positives // rows
    order = ((owner // depth // 2 * depth + owner % depth) * 2 + owner // depth % 2) * rows + positives % rows

    vmem = pltpu.CompilerParams(vmem_limit_bytes=60 * 1024 * 1024)
    smem = pl.BlockSpec(memory_space=pltpu.SMEM)

    def attend(encoder, x, lengths):
        packed = 0 if encoder == 0 else pack
        tokens = x.shape[0] * x.shape[1]
        return pl.pallas_call(
            functools.partial(attend_kernel, encoder, packed, x.shape[1], rows, heads),
            grid=(1,),
            in_specs=[smem, smem, full_spec((tokens, width)),
                      pl.BlockSpec((1, width, 3 * width), lambda s: (encoder, 0, 0)), full_spec((2, 2, width)),
                      pl.BlockSpec((1, width, width), lambda s: (encoder, 0, 0)), full_spec((2, width))],
            out_specs=[full_spec((rows, width + EXTRA)), full_spec(((heads + 3) * rows, width)),
                       full_spec((heads * rows, width)), full_spec((heads * rows, tokens))],
            out_shape=[jax.ShapeDtypeStruct((rows, width + EXTRA), BF), jax.ShapeDtypeStruct(((heads + 3) * rows, width), BF),
                       jax.ShapeDtypeStruct((heads * rows, width), BF), jax.ShapeDtypeStruct((heads * rows, tokens), F32)],
            compiler_params=vmem, name="attend",
        )(lengths, order, x.reshape(tokens, width), w_qkv, qv_bias, w_out, out_bias)

    pack0, bundle0, a0, p0 = attend(0, question_tokens, question_lengths)
    pack1, bundle1, a1, p1 = attend(1, passage_tokens, passage_lengths)

    mine, other = mine_other(pack0, pack1)
    pair = jnp.concatenate([mine, swap(other)], axis=0)
    column_rows = jnp.concatenate([pair] + [to_depth(pair, k) for k in range(1, depth)], axis=0)
    plane = [column_rows] + [to_chip(column_rows, k) for k in range(1, chips)]

    def by_chip(sliced, whole):
        cut = sliced.reshape(-1, chips, part).transpose(1, 0, 2)
        rest = jnp.broadcast_to(whole.reshape(1, -1, part), (chips, whole.size // part, part))
        return jnp.concatenate([cut, rest], axis=1)

    def exchange(blocks):
        pick = lambda k: lax.dynamic_index_in_dim(blocks, (j + k) % chips, axis=0, keepdims=False)
        return jnp.stack([pick(0)] + [to_chip(pick(k), k) for k in range(1, chips)])

    mine, other = mine_other(bundle0, bundle1)
    bundle = jnp.stack([mine, swap(other)])
    m = (heads + 2) * rows
    early = exchange(by_chip(bundle[:, :m], bundle[:, m:]))
    cut = early[:, :2 * m].reshape(chips, 2, heads + 2, rows, part)
    q_plane = early[:, 2 * m:].reshape(chips, 2, rows, heads, HEAD_DIM)

    fc = 512 if count <= 1024 else 256
    tile = count if count <= 1024 else 128
    steps = ff // fc
    whole_rows = lambda w: full_spec((count, w))
    grid_spec = pltpu.PrefetchScalarGridSpec(
        num_scalar_prefetch=1,
        grid=(steps,),
        in_specs=[full_spec((depth * 2 * rows, width + EXTRA))] * chips + [
            full_spec((2, 2, width)), full_spec((2, 2, width)),
            pl.BlockSpec((1, width, fc), lambda s, ids: (ids[0], 0, s)), full_spec((2, ff)),
            pl.BlockSpec((1, fc, width), lambda s, ids: (ids[0], s, 0)), full_spec((2, width))],
        out_specs=[pl.BlockSpec((count, fc), lambda s, ids: (0, s)), pl.BlockSpec((count, fc), lambda s, ids: (0, s)),
                   whole_rows(width), whole_rows(width), whole_rows(EXTRA), whole_rows(width), whole_rows(width)],
        scratch_shapes=[pltpu.VMEM((count, width), F32)],
    )
    act, slope, vec, hat2, ex, nl, hat1 = pl.pallas_call(
        functools.partial(forward_kernel, chips, depth, rows, steps, tile),
        grid_spec=grid_spec,
        out_shape=[jax.ShapeDtypeStruct((count, ff), BF), jax.ShapeDtypeStruct((count, ff), BF),
                   jax.ShapeDtypeStruct((count, width), BF), jax.ShapeDtypeStruct((count, width), BF),
                   jax.ShapeDtypeStruct((count, EXTRA), F32), jax.ShapeDtypeStruct((count, width), BF),
                   jax.ShapeDtypeStruct((count, width), BF)],
        compiler_params=vmem, name="forward",
    )(ids, *plane, norm_gains, norm_biases, w_in, in_bias, w_back, back_bias)

    vec_other = swap(vec)
    own_at = ((j * depth + z) * 2 + c) * rows
    own = lax.dynamic_slice_in_dim(vec, own_at, rows)
    far = lax.dynamic_slice_in_dim(vec_other, own_at, rows)
    q_vectors, p_vectors = mine_other(own, far)

    grid_spec = pltpu.PrefetchScalarGridSpec(
        num_scalar_prefetch=1,
        grid=(steps,),
        in_specs=[whole_rows(width), whole_rows(width), whole_rows(EXTRA), whole_rows(width), whole_rows(width),
                  pl.BlockSpec((count, fc), lambda s, ids: (0, s)),
                  pl.BlockSpec((1, fc, width), lambda s, ids: (ids[0], s, 0)),
                  pl.BlockSpec((1, width, fc), lambda s, ids: (ids[0], 0, s)), full_spec((2, 2, width)),
                  pl.BlockSpec((1, width, width), lambda s, ids: (ids[0], 0, 0))],
        out_specs=[whole_rows(width), pl.BlockSpec((count, fc), lambda s, ids: (0, s)),
                   pl.BlockSpec((1, fc), lambda s, ids: (0, s)), full_spec((chips * 2 * rows, width)),
                   full_spec((chips * 2 * rows, width)), full_spec((rows, EXTRA)), full_spec((rows, 2 * width)),
                   full_spec((rows, 2 * width)), full_spec((8, width))],
        scratch_shapes=[pltpu.VMEM((count, width), F32), pltpu.VMEM((count, EXTRA), F32), pltpu.VMEM((count, width), BF)],
    )
    gsl, gpl, g_inb, g_plane, h_plane, loss, gg_mine, gg_sib, small = pl.pallas_call(
        functools.partial(backward_kernel, chips, depth, rows, steps, tile),
        grid_spec=grid_spec,
        out_shape=[jax.ShapeDtypeStruct((count, width), BF), jax.ShapeDtypeStruct((count, ff), BF),
                   jax.ShapeDtypeStruct((1, ff), F32), jax.ShapeDtypeStruct((chips * 2 * rows, width), BF),
                   jax.ShapeDtypeStruct((chips * 2 * rows, width), BF), jax.ShapeDtypeStruct((rows, EXTRA), F32),
                   jax.ShapeDtypeStruct((rows, 2 * width), F32), jax.ShapeDtypeStruct((rows, 2 * width), F32),
                   jax.ShapeDtypeStruct((8, width), F32)],
        compiler_params=vmem, name="backward",
    )(ids, vec, vec_other, ex, hat2, hat1, slope, w_back, w_in, norm_gains, w_out)

    gg_other = swap(gg_sib)
    gg0, gg1 = mine_other(gg_mine, gg_other)

    def attend_back(encoder, x, lengths, gg, p, a):
        packed = 0 if encoder == 0 else pack
        tokens = x.shape[0] * x.shape[1]
        gx, late = pl.pallas_call(
            functools.partial(attend_back_kernel, encoder, packed, x.shape[1], rows, heads),
            grid=(1,),
            in_specs=[smem, full_spec((rows, 2 * width)), full_spec((tokens, width)),
                      pl.BlockSpec((1, width, 3 * width), lambda s: (encoder, 0, 0)), full_spec((2, 2, width)),
                      full_spec((heads * rows, tokens)), full_spec((heads * rows, width))],
            out_specs=[full_spec((tokens, width)), full_spec(((heads + 1) * rows, width))],
            out_shape=[jax.ShapeDtypeStruct((tokens, width), F32), jax.ShapeDtypeStruct(((heads + 1) * rows, width), BF)],
            compiler_params=vmem, name="attend_back",
        )(lengths, gg, x.reshape(tokens, width), w_qkv, qv_bias, p, a)
        return gx.reshape(x.shape), late

    gx0, late0 = attend_back(0, question_tokens, question_lengths, gg0, p0, a0)
    gx1, late1 = attend_back(1, passage_tokens, passage_lengths, gg1, p1, a1)

    mine, other = mine_other(late0, late1)
    bundle = jnp.stack([mine, swap(other)])
    m = heads * rows
    late = exchange(by_chip(bundle[:, :m], bundle[:, m:]))
    y_cut = late[:, :2 * m].reshape(chips, 2, heads, rows, part)
    gq_plane = late[:, 2 * m:].reshape(chips, 2, rows, width)

    def per_head(factor, vectors):
        return jnp.einsum("jchrw,jcrhk->whk", factor, vectors, preferred_element_type=F32).reshape(part, width)

    def per_row(factor, vectors):
        return jnp.einsum("jcrw,jcrk->wk", factor, vectors, preferred_element_type=F32)

    g_plane = g_plane.reshape(chips, 2, rows, heads, HEAD_DIM)
    h_plane = h_plane.reshape(chips, 2, rows, width)
    sum_wv = per_head(cut[:, :, :heads], g_plane)
    sum_wo = per_row(cut[:, :, heads + 1], h_plane)
    sum_wk = per_head(y_cut, q_plane) * 0.125
    sum_wq = per_row(cut[:, :, heads], gq_plane)

    def pieces_over_depth(share):
        share = share.astype(BF)
        blocks = share.reshape(depth, part // depth, share.shape[1])
        pick = lambda k: lax.dynamic_index_in_dim(blocks, (z + k) % depth, axis=0, keepdims=False)
        total = pick(0).astype(F32)
        for k in range(1, depth):
            total = total + to_depth(pick(k), k).astype(F32)
        total = total.astype(BF)
        every = jnp.stack([total] + [to_depth(total, k) for k in range(1, depth)])
        return canon(every, z).reshape(share.shape)

    sum_vo = pieces_over_depth(jnp.concatenate([sum_wv, sum_wo], axis=1))
    sum_qk = pieces_over_depth(jnp.concatenate([sum_wq, sum_wk], axis=1))

    gq_sums = jnp.sum(gq_plane.astype(F32), axis=2)
    gq_sums = jnp.where(first, gq_sums, gq_sums[:, ::-1])
    gq_sums = jnp.sum(canon(gq_sums, j), axis=(0, 1)).reshape(1, width)
    every = jnp.stack([gq_sums] + [to_depth(gq_sums, k) for k in range(1, depth)])
    q_bias = jnp.sum(canon(every, z), axis=0)

    nl_cut = lax.dynamic_slice_in_dim(nl, j * part, part, axis=1)
    g_in = jnp.einsum("nd,nf->df", nl_cut, gpl, preferred_element_type=F32)
    fpart = ff // chips
    act_cut = lax.dynamic_slice_in_dim(act, j * fpart, fpart, axis=1)
    g_back = jnp.einsum("nf,nd->fd", act_cut, gsl, preferred_element_type=F32)

    def both(chip_rows):
        half = chip_rows.shape[0] // 2
        own = lax.dynamic_slice_in_dim(chip_rows, c * half, half)
        sib = lax.dynamic_slice_in_dim(chip_rows, (1 - c) * half, half)
        far = swap(sib.astype(BF)).astype(F32)
        return jnp.stack(mine_other(own.astype(F32), far))

    attention = both(jnp.concatenate([sum_qk, sum_vo], axis=1))
    small_all = jnp.concatenate([small, g_inb.reshape(-1, width), q_bias, jnp.zeros((3, width), F32)], axis=0)
    small_all = jnp.stack(mine_other(small_all, swap(small_all)))
    n_in = ff // width
    return (
        q_vectors,
        p_vectors,
        loss[:, 0],
        gx0,
        gx1,
        attention[:, :, :3 * width],
        jnp.stack([small_all[:, 8 + n_in], small_all[:, 6]], axis=1),
        attention[:, :, 3 * width:],
        small_all[:, 4],
        small_all[:, 0:2],
        small_all[:, 2:4],
        both(g_in),
        small_all[:, 8:8 + n_in].reshape(2, ff),
        both(g_back),
        small_all[:, 5],
    )


def solution(mesh):
    split = P(("dp", "group"))
    return jax.shard_map(
        functools.partial(body, n_dp=mesh.shape["dp"], depth=mesh.shape["group"]),
        mesh=mesh,
        in_specs=(split, split, split, split, split) + (P(),) * 10,
        out_specs=(split, split, split, split, split, P(None, "dp", None), P(), P(None, "dp", None), P(), P(), P(),
                   P(None, "dp", None), P(), P(None, "dp", None), P()),
        check_vma=False,
    )
```

```python
import functools
import math

import jax
import jax.numpy as jnp
from jax import lax
from jax.experimental import pallas as pl
from jax.experimental.pallas import tpu as pltpu
from jax.sharding import PartitionSpec as P

HEAD_DIM = 64
EPSILON = 1e-12
MASKED = -1000000000.0
EXTRA = 128
BF = jnp.bfloat16
F32 = jnp.float32

NT = (((1,), (1,)), ((), ()))
TN = (((0,), (0,)), ((), ()))
NN = (((1,), (0,)), ((), ()))


def mm(left, right, dims=NN):
    return lax.dot_general(left, right, dims, preferred_element_type=F32)


def row_bounds(packed, len_ref, rows, length):
    bounds = []
    for r in range(rows):
        if packed:
            row, k = r // packed, r % packed
            start = row * length
            for earlier in range(k):
                start = start + len_ref[row, earlier]
            bounds.append((start, start + len_ref[row, k]))
        else:
            bounds.append((r * length, r * length + len_ref[r]))
    return bounds


def column(values, rows):
    at = lax.broadcasted_iota(jnp.int32, (rows, 1), 0)
    result = jnp.zeros((rows, 1), jnp.int32)
    for r, value in enumerate(values):
        result = jnp.where(at == r, value, result)
    return result


def head_mask(rows, heads, width):
    row_head = lax.broadcasted_iota(jnp.int32, (rows * heads, width), 0) // rows
    col_head = lax.broadcasted_iota(jnp.int32, (rows * heads, width), 1) // HEAD_DIM
    return row_head == col_head


def spread_heads(values, heads, mask):
    tiled = jnp.concatenate([values] * heads, axis=0)
    return jnp.where(mask, tiled, jnp.zeros_like(tiled))


def gather_heads(full, heads, rows, mask):
    kept = jnp.where(mask, full, jnp.zeros_like(full))
    return jnp.sum(kept.reshape(heads, rows, full.shape[1]), axis=0)


def start_all(copies):
    for copy in copies:
        copy.start()


def order_of(positives, rows, depth):
    owner = positives // rows
    dp = owner // depth
    return ((dp // 2 * depth + owner % depth) * 2 + dp % 2) * rows + positives % rows


def attend_kernel(pack, lengths, rows, heads, chips, depth, ids, qlen_ref, plen_ref, pos_ref, xq_hbm, xp_hbm, w_hbm, wo_hbm,
                  bias_ref, ob_ref, pack_mine, pack_other, early_mine, early_other, a_ref, p_ref, x_buf, w_buf, wo_buf, sems):
    c, j = ids[0], ids[1]
    width = wo_buf.shape[2]
    part = width // chips
    tokens = x_buf.shape[1]
    copies = []
    for e in range(2):
        own = [pltpu.make_async_copy(xq_hbm if e == 0 else xp_hbm, x_buf.at[e], sems.at[e * 5])]
        for k in range(3):
            span = pl.ds(k * width, width)
            own.append(pltpu.make_async_copy(w_hbm.at[e, :, span], w_buf.at[e, :, span], sems.at[e * 5 + 1 + k]))
        own.append(pltpu.make_async_copy(wo_hbm.at[e], wo_buf.at[e], sems.at[e * 5 + 4]))
        copies.append(own)
    start_all(copies[0] + copies[1])
    mask = head_mask(rows, heads, width)
    pos = order_of(column([pos_ref[r] for r in range(rows)], rows), rows, depth)
    for e in range(2):
        wait = copies[e]
        bounds = row_bounds(pack if e else 0, plen_ref if e else qlen_ref, rows, lengths[e])
        start = column([b[0] for b in bounds], rows)
        stop = column([b[1] for b in bounds], rows)
        lane = lax.broadcasted_iota(jnp.int32, (rows, tokens), 1)
        bias = bias_ref[e]
        wait[0].wait()
        x = x_buf[e]
        x_cls = mm(jnp.where(lane == start, 1.0, 0.0).astype(BF), x)
        xc = x_cls.astype(BF)
        wait[1].wait()
        q = (mm(xc, w_buf[e, :, 0:width]) + bias[0:1, :]).astype(BF)
        wait[2].wait()
        a_low = mm(spread_heads(q, heads, mask), w_buf[e, :, width:2 * width], NT).astype(BF)
        a_ref[e] = a_low
        scores = mm(a_low, x, NT) * 0.125
        lane_all = lax.broadcasted_iota(jnp.int32, scores.shape, 1)
        starts = jnp.concatenate([start] * heads, axis=0)
        stops = jnp.concatenate([stop] * heads, axis=0)
        scores = jnp.where((lane_all >= starts) & (lane_all < stops), scores, MASKED)
        peak = jnp.max(scores, axis=1, keepdims=True)
        shifted = jnp.exp(scores - peak)
        p = shifted / jnp.sum(shifted, axis=1, keepdims=True)
        p_ref[e] = p
        p_low = p.astype(BF)
        sums = jnp.sum(p_low.astype(F32), axis=1, keepdims=True)
        pooled = mm(p_low, x).astype(BF)
        wait[3].wait()
        full = mm(pooled, w_buf[e, :, 2 * width:3 * width]) + sums * bias[1:2, :]
        ctx = gather_heads(full, heads, rows, mask).astype(BF)
        wait[4].wait()
        hidden = x_cls + mm(ctx, wo_buf[e]) + ob_ref[e:e + 1, :]
        mean = jnp.mean(hidden, axis=1, keepdims=True)
        centred = hidden - mean
        rstd = lax.rsqrt(jnp.mean(centred * centred, axis=1, keepdims=True) + EPSILON)
        hat = (centred * rstd).astype(BF)
        rstd_high = rstd.astype(BF).astype(F32)
        lanes = lax.broadcasted_iota(jnp.int32, (rows, EXTRA), 1)
        extra = jnp.where(lanes == 0, rstd_high, 0.0)
        extra = jnp.where(lanes == 1, rstd - rstd_high, extra)
        extra = jnp.where(lanes == 2, (pos // 32).astype(F32), extra)
        extra = jnp.where(lanes == 3, (pos % 32).astype(F32), extra)
        for h in range(heads):
            extra = jnp.where(lanes == 16 + h, sums[h * rows:(h + 1) * rows] - 1.0, extra)
        extra = extra.astype(BF)

        def put(pack_ref, early_ref):
            pack_ref[:, 0:width] = hat
            pack_ref[:, width:] = extra
            for chip in range(chips):
                slot = lax.rem(chip - j + chips, chips)
                cut = slice(chip * part, (chip + 1) * part)
                pieces = [pooled[h * rows:(h + 1) * rows, cut] for h in range(heads)] + [xc[:, cut], ctx[:, cut], q]
                early_ref[slot] = jnp.concatenate(pieces, axis=1)

        @pl.when(c == e)
        def keep():
            put(pack_mine, early_mine)

        @pl.when(c != e)
        def give():
            put(pack_other, early_other)


def gelu_parts(x):
    bell = jnp.exp(-0.5 * x * x)
    t = 1.0 / (1.0 + (0.3275911 * math.sqrt(0.5)) * jnp.abs(x))
    tail = 1.061405429 * 0.5
    for factor in (-1.453152027, 1.421413741, -0.284496736, 0.254829592):
        tail = tail * t + factor * 0.5
    tail = tail * t * bell
    cdf = jnp.where(x >= 0.0, 1.0 - tail, tail)
    return x * cdf, cdf + x * bell * (1.0 / math.sqrt(2.0 * math.pi))


def relative_places(chips, depth, rows, c, j, z):
    for kx in range(chips):
        for kz in range(depth):
            for kc in range(2):
                core = c if kc == 0 else 1 - c
                place = ((lax.rem(j - kx + chips, chips) * depth + lax.rem(z - kz + depth, depth)) * 2 + core) * rows
                yield kx, kz, kc, pl.multiple_of(place, rows)


def doubling(n, masks):
    found = [0]
    for mask in masks:
        found = found + [k ^ mask for k in found]
    assert sorted(found) == list(range(n))
    return found


def depth_masks(depth):
    return [(1 << k) - 1 for k in range(1, depth.bit_length())]


def chip_masks(chips):
    return [1 << k for k in range(chips.bit_length() - 1)]


def place_of(chip, deep, core, depth, rows):
    return pl.multiple_of(((chip * depth + deep) * 2 + core) * rows, rows)


def crossed_blocks(refs, chips, depth, rows, c, j, z, part):
    near = depth // 2
    for at, dz in enumerate(doubling(depth, depth_masks(depth))):
        for kc in range(2):
            core = c if kc == 0 else 1 - c
            first = ((at % near) * 2 + kc) * rows
            for kx in range(chips):
                place = place_of(lax.rem(j - kx + chips, chips), jnp.bitwise_xor(z, dz), core, depth, rows)
                yield refs[at // near], first, 2 * kx * part, place


def over_rows(count, tile, work):
    if tile == count:
        work(pl.ds(0, count))
    else:
        def one(t, carry):
            work(pl.ds(pl.multiple_of(t * tile, tile), tile))
            return carry

        lax.fori_loop(0, count // tile, one, 0)


def forward_kernel(chips, depth, rows, steps, tile, part, ids, *refs):
    blocks = refs[:chips]
    gain_ref, shift_ref, win_ref, inb_ref, wback_ref, backb_ref = refs[chips:chips + 6]
    act_ref, slope_ref, vec_ref, hat2_ref, ex_ref, cut_ref, hat1_ref, total, nl = refs[chips + 6:]
    c, j, z = ids[0], ids[1], ids[2]
    width = vec_ref.shape[1]
    step = pl.program_id(0)

    @pl.when(step == 0)
    def start():
        for kx, kz, kc, place in relative_places(chips, depth, rows, c, j, z):
            at = (kz * 2 + kc) * rows
            hat1_ref[pl.ds(place, rows), :] = blocks[kx][at:at + rows, 0:width]
            ex_ref[pl.ds(place, rows), :] = blocks[kx][at:at + rows, width:].astype(F32)
        gain = gain_ref[c]
        shift = shift_ref[c]
        normed = hat1_ref[...].astype(F32) * gain[0:1, :] + shift[0:1, :]
        low = normed.astype(BF)
        nl[...] = low
        total[...] = normed + backb_ref[pl.ds(c, 1), :]
        source = lax.broadcasted_iota(jnp.int32, (width, part), 0)
        target = lax.broadcasted_iota(jnp.int32, (width, part), 1) + j * part
        cut_ref[...] = mm(low, jnp.where(source == target, 1.0, 0.0).astype(BF)).astype(BF)

    columns = win_ref.shape[2]
    pre = mm(nl[...], win_ref[0]) + inb_ref[pl.ds(c, 1), pl.ds(pl.multiple_of(step * columns, columns), columns)]
    active, slope = gelu_parts(pre)
    active = active.astype(BF)
    fpart = act_ref.shape[2]
    for s in range(columns // fpart):
        act_ref[s] = active[:, s * fpart:(s + 1) * fpart]
    slope_ref[...] = slope.astype(BF)
    total[...] += mm(active, wback_ref[0])

    @pl.when(step == steps - 1)
    def finish():
        gain = gain_ref[c]
        shift = shift_ref[c]

        def normalise(part):
            second = total[part, :]
            mean = jnp.mean(second, axis=1, keepdims=True)
            centred = second - mean
            rstd = lax.rsqrt(jnp.mean(centred * centred, axis=1, keepdims=True) + EPSILON)
            hat = centred * rstd
            hat2_ref[part, :] = hat.astype(BF)
            vec_ref[part, :] = (hat * gain[1:2, :] + shift[1:2, :]).astype(BF)
            ex = ex_ref[part, :]
            lanes = lax.broadcasted_iota(jnp.int32, ex.shape, 1)
            pos = ex[:, 2:3] * 32.0 + ex[:, 3:4]
            ex_ref[part, :] = jnp.where(
                lanes == 0, ex[:, 0:1] + ex[:, 1:2], jnp.where(lanes == 1, rstd, jnp.where(lanes == 2, pos, ex)))

        over_rows(total.shape[0], tile, normalise)


def norm_back(grad, hat, rstd, gain):
    scaled = grad * gain
    inner = jnp.mean(scaled * hat, axis=1, keepdims=True)
    return rstd * (scaled - jnp.mean(scaled, axis=1, keepdims=True) - hat * inner)


def loss_kernel(depth, rows, tile, ids, own_ref, other_ref, ex_ref, hat2_ref, hat1_ref, slope_ref, gain_ref,
                wback_hbm, win_hbm, wout_hbm, second_ref, loss_ref, mine_ref, sib_ref, small_ref, qvec_ref, pvec_ref,
                wide_loss, wback, win, wout, sems):
    c, j, z = ids[0], ids[1], ids[2]
    count, width = own_ref.shape
    scale = 2.0 / math.sqrt(width)
    copies = [pltpu.make_async_copy(wback_hbm.at[c], wback, sems.at[0]),
              pltpu.make_async_copy(win_hbm.at[c], win, sems.at[1]),
              pltpu.make_async_copy(wout_hbm.at[c], wout, sems.at[2])]
    start_all(copies)
    own_at = pl.multiple_of(((j * depth + z) * 2 + c) * rows, rows)

    def softmax_part(questions, passages, pos):
        scores = mm(questions, passages, NT) * scale
        peak = jnp.max(scores, axis=1, keepdims=True)
        shifted = jnp.exp(scores - peak)
        totals = jnp.sum(shifted, axis=1, keepdims=True)
        hit = lax.broadcasted_iota(jnp.int32, scores.shape, 1) == pos.astype(jnp.int32)
        loss = peak + jnp.log(totals) - jnp.sum(jnp.where(hit, scores, 0.0), axis=1, keepdims=True)
        grad = (shifted / totals - jnp.where(hit, 1.0, 0.0)) * scale
        high = grad.astype(BF)
        return loss, high, (grad - high.astype(F32)).astype(BF)

    @pl.when(c == 0)
    def question_side():
        qvec_ref[...] = own_ref[pl.ds(own_at, rows), :]
        pvec_ref[...] = other_ref[pl.ds(own_at, rows), :]

        def work(part):
            loss, high, low = softmax_part(own_ref[part, :], other_ref[...], ex_ref[part, 2:3])
            wide_loss[part, :] = jnp.broadcast_to(loss, (tile, wide_loss.shape[1]))
            second_ref[part, :] = mm(high, other_ref[...]) + mm(low, other_ref[...])

        over_rows(count, tile, work)

    @pl.when(c == 1)
    def passage_side():
        pvec_ref[...] = own_ref[pl.ds(own_at, rows), :]
        qvec_ref[...] = other_ref[pl.ds(own_at, rows), :]
        if tile < count:
            second_ref[...] = jnp.zeros_like(second_ref)

        def work(part):
            loss, high, low = softmax_part(other_ref[part, :], own_ref[...], ex_ref[part, 2:3])
            wide_loss[part, :] = jnp.broadcast_to(loss, (tile, wide_loss.shape[1]))
            piece = mm(high, other_ref[part, :], TN) + mm(low, other_ref[part, :], TN)
            second_ref[...] = piece if tile == count else second_ref[...] + piece

        over_rows(count, tile, work)

    small_ref[...] = jnp.zeros_like(small_ref)
    loss_ref[...] = wide_loss[pl.ds(own_at, rows), :]

    def late_norm(part):
        grad = second_ref[part, :]
        hat = hat2_ref[part, :].astype(F32)
        small_ref[1:2, :] += jnp.sum(grad * hat, axis=0, keepdims=True)
        small_ref[3:4, :] += jnp.sum(grad, axis=0, keepdims=True)
        second = norm_back(grad, hat, ex_ref[part, 1:2], gain_ref[c][1:2, :])
        small_ref[5:6, :] += jnp.sum(second, axis=0, keepdims=True)
        second_ref[part, :] = second

    over_rows(count, tile, late_norm)

    chip_at = pl.multiple_of((j * depth + z) * 2 * rows, 2 * rows)
    second = second_ref[pl.ds(chip_at, 2 * rows), :]
    copies[0].wait()
    pre = (mm(second.astype(BF), wback[...], NT) * slope_ref[...].astype(F32)).astype(BF)
    copies[1].wait()
    normed = second + mm(pre, win[...], NT)
    hidden = norm_back(normed, hat1_ref[...].astype(F32), ex_ref[pl.ds(chip_at, 2 * rows), 0:1], gain_ref[c][0:1, :])
    copies[2].wait()
    ctx = mm(hidden.astype(BF), wout[...], NT).astype(BF).astype(F32)
    both = jnp.concatenate([hidden, ctx], axis=1)
    is_low = c == 0
    mine_ref[...] = jnp.where(is_low, both[:rows], both[rows:])
    sib_ref[...] = jnp.where(is_low, both[rows:], both[:rows])


def split_halves(value, scratch, c, own_ref_set, sib_ref_set):
    half = value.shape[0] // 2
    scratch[...] = value
    own_ref_set(scratch[pl.ds(pl.multiple_of(c * half, half), half), :])
    sib_ref_set(scratch[pl.ds(pl.multiple_of((1 - c) * half, half), half), :].astype(BF))


def backward_kernel(chips, depth, rows, steps, tile, ids, after_ref, second_ref, ex_ref, hat1_ref, slope_ref, wback_ref, win_ref,
                    gain_ref, wout_ref, small_in, gpl_ref, low_ref, hidden_ref, inb_ref, plane_ref, small_ref, acc, gfull):
    c, j, z = ids[0], ids[1], ids[2]
    count, width = second_ref.shape
    step = pl.program_id(0)

    @pl.when(step == 0)
    def start():
        acc[...] = second_ref[...]
        low_ref[...] = second_ref[...].astype(BF)
        small_ref[...] = small_in[...]

    pre = mm(low_ref[...], wback_ref[0], NT) * slope_ref[...].astype(F32)
    inb_ref[...] = jnp.sum(pre, axis=0, keepdims=True)
    pre_low = pre.astype(BF)
    gpl_ref[...] = pre_low
    acc[...] += mm(pre_low, win_ref[0], NT)

    @pl.when(step == steps - 1)
    def finish():
        lanes = lax.broadcasted_iota(jnp.int32, (EXTRA, width), 0)
        heads_of = lax.broadcasted_iota(jnp.int32, (EXTRA, width), 1) // HEAD_DIM
        expand = jnp.where(lanes == heads_of + 16, 1.0, 0.0).astype(BF)

        def early_norm(part):
            grad = acc[part, :]
            hat = hat1_ref[part, :].astype(F32)
            small_ref[0:1, :] += jnp.sum(grad * hat, axis=0, keepdims=True)
            small_ref[2:3, :] += jnp.sum(grad, axis=0, keepdims=True)
            hidden = norm_back(grad, hat, ex_ref[part, 0:1], gain_ref[c][0:1, :])
            small_ref[4:5, :] += jnp.sum(hidden, axis=0, keepdims=True)
            hidden_low = hidden.astype(BF)
            hidden_ref[part, :] = hidden_low
            ctx = mm(hidden_low, wout_ref[0], NT).astype(BF)
            sums = mm(ex_ref[part, :].astype(BF), expand) + 1.0
            small_ref[6:7, :] += jnp.sum(sums * ctx.astype(F32), axis=0, keepdims=True)
            gfull[part, :] = ctx

        over_rows(count, tile, early_norm)
        for kx in range(chips):
            for kc in range(2):
                core = c if kc == 0 else 1 - c
                place = pl.multiple_of(((lax.rem(j - kx + chips, chips) * depth + z) * 2 + core) * rows, rows)
                at = (kx * 2 + kc) * rows
                plane_ref[at:at + rows, :] = gfull[pl.ds(place, rows), :]


def weight_kernel(chips, depth, rows, part, steps, ids, after_ref, near_ref, far_ref, gpl_ref, low_ref, hidden_ref, act_ref, cut_ref,
                  gin_ref, gback_ref, gout_ref, sib_ref, ctx_all, in_scr, back_scr, out_scr):
    c, j, z = ids[0], ids[1], ids[2]
    step = pl.program_id(0)
    width = low_ref.shape[1]
    half = part // 2
    ghalf = back_scr.shape[0] // 2
    columns = gpl_ref.shape[1]
    in_rows = half * (columns * steps // width)

    def set_own(ref):
        def setter(value):
            ref[0] = value
        return setter

    def set_sib(at, rows, lane, lanes):
        def setter(value):
            sib_ref[at:at + rows, lane:lane + lanes] = value
        return setter

    @pl.when(step == 0)
    def start():
        split_halves(mm(act_ref[0], low_ref[...], TN), back_scr, c, set_own(gback_ref), set_sib(in_rows, ghalf, 0, width))
        for ref, first, lane, place in crossed_blocks((near_ref, far_ref), chips, depth, rows, c, j, z, part):
            ctx_all[pl.ds(place, rows), :] = ref[first:first + rows, lane + part:lane + 2 * part]
        split_halves(mm(ctx_all[...], hidden_ref[...], TN), out_scr, c, set_own(gout_ref), set_sib(in_rows + ghalf, half, 0, width))

    piece = mm(cut_ref[...], gpl_ref[...], TN)
    in_scr[...] = piece
    gin_ref[0] = in_scr[pl.ds(pl.multiple_of(c * half, half), half), :]
    other = in_scr[pl.ds(pl.multiple_of((1 - c) * half, half), half), :].astype(BF)
    for s in range(steps):
        @pl.when(step == s)
        def keep():
            set_sib((s * columns // width) * half, half, s * columns % width, columns)(other)


def attend_back_kernel(rows, heads, chips, ids, mine_ref, far_ref, xq_hbm, xp_hbm, w_hbm, bias_ref, p_ref, *refs):
    early = refs[:chips]
    late_mine, late_other, att_ref, b_ref, first_ref, cross_ref, x_buf, w_buf, sems = refs[chips:]
    c, j = ids[0], ids[1]
    width = bias_ref.shape[2]
    part = width // chips
    copies = []
    for e in range(2):
        own = [pltpu.make_async_copy(w_hbm.at[e, :, pl.ds(k * width, width)], w_buf.at[e, k], sems.at[e * 4 + k])
               for k in (2, 1, 0)]
        own.insert(1, pltpu.make_async_copy(xq_hbm if e == 0 else xp_hbm, x_buf.at[e], sems.at[e * 4 + 3]))
        copies.append(own)
    start_all(copies[0] + copies[1])
    cross_ref[...] = jnp.concatenate([b[:, heads * part:(heads + 2) * part] for b in early], axis=1)
    mask = head_mask(rows, heads, width)
    for e in range(2):
        wait = copies[e]
        gg = jnp.where(c == e, mine_ref[...], far_ref[...])
        blocks = spread_heads(gg[:, width:], heads, mask)
        constant = jnp.sum(blocks * bias_ref[e][1:2, :], axis=1, keepdims=True)
        wait[0].wait()
        b_low = mm(blocks.astype(BF), w_buf[e, 2], NT).astype(BF)
        b_ref[e] = b_low
        p = p_ref[e]
        wait[1].wait()
        x = x_buf[e]
        probs = mm(b_low, x, NT) + constant
        att = (p * (probs - jnp.sum(probs * p, axis=1, keepdims=True))).astype(BF)
        att_ref[e] = att
        y_low = mm(att, x).astype(BF)
        wait[2].wait()
        gq_low = (gather_heads(mm(y_low, w_buf[e, 1]), heads, rows, mask) * 0.125).astype(BF)

        def put(late_ref):
            for chip in range(chips):
                slot = lax.rem(chip - j + chips, chips)
                cut = slice(chip * part, (chip + 1) * part)
                late_ref[slot] = jnp.concatenate([y_low[h * rows:(h + 1) * rows, cut] for h in range(heads)] + [gq_low], axis=1)

        @pl.when(c == e)
        def keep():
            put(late_mine)

        @pl.when(c != e)
        def give():
            put(late_other)

        wait[3].wait()
        first_ref[e] = gg[:, 0:width] + mm(gq_low, w_buf[e, 0], NT)


def token_grad_kernel(pack, lengths, rows, heads, ids, after_ref, qlen_ref, plen_ref, att_ref, p_ref, a_ref, b_ref, first_ref,
                      gq_ref, gp_ref):
    tile = gq_ref.shape[0]
    at = pl.program_id(0) * tile
    lane = lax.broadcasted_iota(jnp.int32, (rows, tile), 1) + at
    for e in range(2):
        bounds = row_bounds(pack if e else 0, plen_ref if e else qlen_ref, rows, lengths[e])
        pick = jnp.where(lane == column([b[0] for b in bounds], rows), 1.0, 0.0).astype(BF)
        first = first_ref[e]
        high = first.astype(BF)
        rest = first - high.astype(F32)
        middle = rest.astype(BF)
        last = (rest - middle.astype(F32)).astype(BF)
        left = jnp.concatenate([att_ref[e], p_ref[e].astype(BF), pick, pick, pick], axis=0)
        right = jnp.concatenate([a_ref[e] * jnp.asarray(0.125, BF), b_ref[e], high, middle, last], axis=0)
        out = gp_ref if e else gq_ref
        out[...] = mm(left, right, TN)


def head_sums(factor, vectors, heads, part):
    width = vectors.shape[1]
    full = mm(factor, vectors, TN)
    row_head = lax.broadcasted_iota(jnp.int32, full.shape, 0) // part
    col_head = lax.broadcasted_iota(jnp.int32, full.shape, 1) // HEAD_DIM
    kept = jnp.where(row_head == col_head, full, 0.0)
    return jnp.sum(kept.reshape(heads, part, width), axis=0)


def share_kernel(heads, chips, depth, part, ids, *refs):
    late = refs[:chips]
    early = refs[chips:2 * chips]
    plane_ref = refs[2 * chips]
    outs = refs[2 * chips + 1:2 * chips + 1 + depth]
    scratch = refs[2 * chips + 1 + depth]
    z = ids[2]
    width = plane_ref.shape[1]
    hp = heads * part
    y = jnp.concatenate([b[:, 0:hp] for b in late], axis=0)
    pooled = jnp.concatenate([b[:, 0:hp] for b in early], axis=0)
    q = jnp.concatenate([b[:, hp + 2 * part:] for b in early], axis=0)
    scratch[:, 0:width] = head_sums(y, q, heads, part) * 0.125
    scratch[:, width:] = head_sums(pooled, plane_ref[...], heads, part)
    span = 2 * width // depth
    for k in range(depth):
        at = pl.multiple_of(lax.rem(z + k, depth) * span, span)
        outs[k][...] = scratch[:, pl.ds(at, span)].astype(BF)


def query_kernel(chips, depth, rows, part, ids, after_ref, near_ref, far_ref, low_chips, high_chips, *refs):
    shares = refs[:depth]
    gw_ref, keep_ref, send_ref, bias_ref, x_all, gq_all, q_scr, share_scr = refs[depth:]
    c, j, z = ids[0], ids[1], ids[2]
    for ref, first, lane, place in crossed_blocks((near_ref, far_ref), chips, depth, rows, c, j, z, part):
        x_all[pl.ds(place, rows), :] = ref[first:first + rows, lane:lane + part]
    few = chips // 2
    for at_chip, dx in enumerate(doubling(chips, chip_masks(chips))):
        for at_depth, dz in enumerate(doubling(depth, depth_masks(depth))):
            for kc in range(2):
                core = c if kc == 0 else 1 - c
                place = place_of(jnp.bitwise_xor(j, dx), jnp.bitwise_xor(z, dz), core, depth, rows)
                at = (((at_chip % few) * depth + at_depth) * 2 + kc) * rows
                gq_all[pl.ds(place, rows), :] = (low_chips, high_chips)[at_chip // few][at:at + rows, :]
    gq = gq_all[...]
    half = part // 2
    width = gq.shape[1]
    span = shares[0].shape[1]
    bias = jnp.sum(gq.astype(F32), axis=0, keepdims=True)
    bias_ref[...] = jnp.broadcast_to(bias, bias_ref.shape)
    total = shares[0][...].astype(F32)
    for k in range(1, depth):
        total = total + shares[k][...].astype(F32)
    share_scr[...] = total
    q_scr[...] = mm(x_all[...], gq, TN)
    own = pl.ds(pl.multiple_of(c * half, half), half)
    sib = pl.ds(pl.multiple_of((1 - c) * half, half), half)
    keep_ref[...] = share_scr[own, :].astype(BF)
    gw_ref[...] = q_scr[own, :]
    send_ref[:, 0:span] = share_scr[sib, :].astype(BF)
    send_ref[:, span:] = q_scr[sib, :].astype(BF)


def assemble_kernel(depth, ids, after_ref, *refs):
    shards = refs[:depth]
    own_ref, far_ref, out_ref = refs[depth:]
    c, z = ids[0], ids[2]
    half, width = own_ref.shape
    span = shards[0].shape[1]
    out_ref[c, :, 0:width] = own_ref[...]
    out_ref[1 - c, :, 0:width] = far_ref[:, span:].astype(F32)
    for k in range(depth):
        at = pl.multiple_of(width + lax.rem(z - k + depth, depth) * span, 128)
        out_ref[c, :, pl.ds(at, span)] = shards[k][0:half, :].astype(F32)
        out_ref[1 - c, :, pl.ds(at, span)] = shards[k][half:, :].astype(F32)


def fill_kernel(in_rows, ids, after_ref, in_hbm, back_hbm, out_hbm, sib_ref, gin_ref, gback_ref, gout_ref):
    half, width = gout_ref.shape[1], gout_ref.shape[2]
    ghalf = gback_ref.shape[1]
    for k in range(in_rows // half):
        gin_ref[0, :, k * width:(k + 1) * width] = sib_ref[k * half:(k + 1) * half, :].astype(F32)
    gback_ref[0] = sib_ref[in_rows:in_rows + ghalf, :].astype(F32)
    gout_ref[0] = sib_ref[in_rows + ghalf:, :].astype(F32)


def full_spec(shape):
    return pl.BlockSpec(tuple(shape), lambda *_: (0,) * len(shape))


def shape_of(shape, dtype):
    return jax.ShapeDtypeStruct(tuple(shape), dtype)


ANY = pl.BlockSpec(memory_space=pl.ANY)
SMEM = pl.BlockSpec(memory_space=pltpu.SMEM)


def kernel_call(name, kernel, ids, args, specs, outs, out_specs, scratch=(), grid=(1,), work=(0, 0), aliases=None, vmem=60):
    specs = [full_spec(a.shape) if s is None else s for a, s in zip(args, specs)]
    out_specs = [full_spec(o.shape) if s is None else s for o, s in zip(outs, out_specs)]
    return pl.pallas_call(
        kernel,
        grid_spec=pltpu.PrefetchScalarGridSpec(num_scalar_prefetch=1, grid=grid, in_specs=specs, out_specs=out_specs,
                                               scratch_shapes=list(scratch)),
        out_shape=list(outs),
        input_output_aliases=aliases or {},
        compiler_params=pltpu.CompilerParams(vmem_limit_bytes=vmem * 1024 * 1024),
        cost_estimate=pl.CostEstimate(flops=int(work[0]), bytes_accessed=int(work[1]), transcendentals=0),
        name=name,
    )(ids, *args)


def body(question_tokens, question_lengths, passage_tokens, passage_lengths, positives, w_qkv, qv_bias, w_out, out_bias,
         norm_gains, norm_biases, w_in, in_bias, w_back, back_bias, *, n_dp, depth):
    width = question_tokens.shape[2]
    heads = width // HEAD_DIM
    rows = question_tokens.shape[0]
    pack = passage_lengths.shape[1]
    lengths = (question_tokens.shape[1], passage_tokens.shape[1])
    tokens = rows * lengths[0]
    ff = w_in.shape[2]
    chips = n_dp // 2
    count = n_dp * depth * rows
    part = width // chips
    half = part // 2
    fpart = ff // chips
    hr = heads * rows
    i = lax.axis_index("dp")
    z = lax.axis_index("group")
    c, j = i % 2, i // 2
    ids = jnp.stack([c, j, z]).astype(jnp.int32)
    first = c == 0
    vm = pltpu.VMEM
    dma = pltpu.SemaphoreType.DMA

    def swap(x):
        return lax.ppermute(x, "dp", [(k, k ^ 1) for k in range(n_dp)])

    def to_chip(x, k):
        return lax.ppermute(x, "dp", [(s, ((s // 2 + k) % chips) * 2 + s % 2) for s in range(n_dp)])

    def to_depth(x, k):
        return lax.ppermute(x, "group", [(s, (s + k) % depth) for s in range(depth)])

    def over_depth(x):
        return [x] + [to_depth(x, k) for k in range(1, depth)]

    def over_plane(x):
        return [x] + [to_chip(x, k) for k in range(1, chips)]

    xq = question_tokens.reshape(tokens, width)
    xp = passage_tokens.reshape(tokens, width)

    wide = (heads + 2) * part + width
    pack_mine, pack_other, early_mine, early_other, a_low, probs = kernel_call(
        "attend", functools.partial(attend_kernel, pack, lengths, rows, heads, chips, depth), ids,
        [question_lengths, passage_lengths, positives, xq, xp, w_qkv, w_out, qv_bias, out_bias],
        [SMEM, SMEM, SMEM, ANY, ANY, ANY, ANY, None, None],
        [shape_of((rows, width + EXTRA), BF)] * 2 + [shape_of((chips, rows, wide), BF)] * 2 + [
            shape_of((2, hr, width), BF), shape_of((2, hr, tokens), F32)],
        [None] * 6,
        [vm((2, tokens, width), BF), vm((2, width, 3 * width), BF), vm((2, width, width), BF), dma((10,))],
        work=(6e9, 13e6))

    pair = jnp.concatenate([pack_mine, swap(pack_other)], axis=0)
    plane = over_plane(jnp.concatenate(over_depth(pair), axis=0))

    fc = max(fpart, 384)
    sub = fc // fpart
    steps = ff // fc
    tile = count if count <= 1024 else 128
    row = lambda w: full_spec((count, w))
    act, slope, vec, hat2, ex, cut, hat1 = kernel_call(
        "forward", functools.partial(forward_kernel, chips, depth, rows, steps, tile, part), ids,
        plane + [norm_gains, norm_biases, w_in, in_bias, w_back, back_bias],
        [None] * chips + [None, None, pl.BlockSpec((1, width, fc), lambda s, ids: (ids[0], 0, s)), None,
                          pl.BlockSpec((1, fc, width), lambda s, ids: (ids[0], s, 0)), None],
        [shape_of((chips, count, fpart), BF), shape_of((count, ff), BF), shape_of((count, width), BF),
         shape_of((count, width), BF), shape_of((count, EXTRA), F32), shape_of((count, part), BF), shape_of((count, width), BF)],
        [pl.BlockSpec((sub, count, fpart), lambda s, ids: (s, 0, 0)), pl.BlockSpec((count, fc), lambda s, ids: (0, s)),
         None, None, None, None, None],
        [vm((count, width), F32), vm((count, width), BF)], grid=(steps,), work=(10e9, 18e6))

    vec_other = swap(vec)
    hp = heads * part

    nothing = vec[0:1, 0:1] * jnp.asarray(0.0, BF)
    early_far = swap(early_other + nothing)
    payload = [jnp.concatenate([early_mine[k], early_far[k]], axis=0) for k in range(chips)]
    early = [payload[0]] + [to_chip(payload[k], k) for k in range(1, chips)]

    chip_block = lambda w: pl.BlockSpec((2 * rows, w), lambda s, ids: (ids[1] * depth + ids[2], 0))
    second, loss, gg_mine, gg_sib, small, q_vectors, p_vectors = kernel_call(
        "loss", functools.partial(loss_kernel, depth, rows, tile), ids,
        [vec, vec_other, ex, hat2, hat1, slope, norm_gains, w_back, w_in, w_out],
        [None, None, None, None, chip_block(width), chip_block(ff), None, ANY, ANY, ANY],
        [shape_of((count, width), F32), shape_of((rows, EXTRA), F32), shape_of((rows, 2 * width), F32),
         shape_of((rows, 2 * width), F32), shape_of((8, width), F32), shape_of((rows, width), BF), shape_of((rows, width), BF)],
        [None] * 7,
        [vm((count, EXTRA), F32), vm((ff, width), BF), vm((width, ff), BF), vm((width, width), BF), dma((3,))],
        work=(8e9, 16e6))

    late_mine, late_other, att, b_low, first_rows, crossed = kernel_call(
        "attend_back", functools.partial(attend_back_kernel, rows, heads, chips), ids,
        [gg_mine, swap(gg_sib), xq, xp, w_qkv, qv_bias, probs] + early,
        [None, None, ANY, ANY, ANY, None, None] + [None] * chips,
        [shape_of((chips, rows, hp + width), BF)] * 2 + [
            shape_of((2, hr, tokens), BF), shape_of((2, hr, width), BF), shape_of((2, rows, width), F32),
            shape_of((2 * rows, 2 * width), BF)],
        [None] * 6,
        [vm((2, tokens, width), BF), vm((2, 3, width, width), BF), dma((8,))], work=(6e9, 16e6))

    late_far = swap(late_other)
    payload = [jnp.concatenate([late_mine[k], late_far[k]], axis=0) for k in range(chips)]
    late = [payload[0]] + [to_chip(payload[k], k) for k in range(1, chips)]

    def xor_depth(x, mask):
        return lax.ppermute(x, "group", [(s, s ^ mask) for s in range(depth)])

    def xor_chip(x, mask):
        return lax.ppermute(x, "dp", [(s, s ^ (2 * mask)) for s in range(n_dp)])

    def double(x, step, masks):
        for mask in masks:
            x = jnp.concatenate([x, step(x, mask)], axis=0)
        return x

    near = double(crossed, xor_depth, depth_masks(depth)[:-1])
    far_z = xor_depth(near, depth_masks(depth)[-1])
    gq_column = double(payload[0][:, hp:], xor_depth, depth_masks(depth))
    gq_low = double(gq_column, xor_chip, chip_masks(chips)[:-1])
    gq_high = xor_chip(gq_low, chip_masks(chips)[-1])

    gpl, low, hidden_low, g_inb, g_plane, small = kernel_call(
        "backward", functools.partial(backward_kernel, chips, depth, rows, steps, tile), ids,
        [late_far, second, ex, hat1, slope, w_back, w_in, norm_gains, w_out, small],
        [ANY, None, None, None, pl.BlockSpec((count, fc), lambda s, ids: (0, s)),
         pl.BlockSpec((1, fc, width), lambda s, ids: (ids[0], s, 0)),
         pl.BlockSpec((1, width, fc), lambda s, ids: (ids[0], 0, s)), None,
         pl.BlockSpec((1, width, width), lambda s, ids: (ids[0], 0, 0)), None],
        [shape_of((count, ff), BF), shape_of((count, width), BF), shape_of((count, width), BF), shape_of((1, ff), F32),
         shape_of((chips * 2 * rows, width), BF), shape_of((8, width), F32)],
        [pl.BlockSpec((count, fc), lambda s, ids: (0, s)), None, None, pl.BlockSpec((1, fc), lambda s, ids: (0, s)), None, None],
        [vm((count, width), F32), vm((count, width), BF)], grid=(steps,), work=(12e9, 18e6))

    span = 2 * width // depth
    shares = kernel_call(
        "share", functools.partial(share_kernel, heads, chips, depth, part), ids,
        late + early + [g_plane], [None] * (2 * chips + 1),
        [shape_of((part, span), BF)] * depth, [None] * depth, [vm((part, 2 * width), F32)], work=(1e9, 3e6))
    shares = [shares[0]] + [to_depth(shares[k], k) for k in range(1, depth)]

    ghalf = fpart // 2
    out_block = lambda r, w: pl.BlockSpec((1, r, w), lambda s, ids: (ids[0], 0, 0))
    in_rows = half * ff // width
    gin, gback, gout, sib = kernel_call(
        "weight", functools.partial(weight_kernel, chips, depth, rows, part, steps), ids,
        [shares[0], near, far_z, gpl, low, hidden_low, act, cut],
        [ANY, None, None, pl.BlockSpec((count, fc), lambda s, ids: (0, s)), None, None,
         pl.BlockSpec((1, count, fpart), lambda s, ids: (ids[1], 0, 0)), None],
        [shape_of((2, half, ff), F32), shape_of((2, ghalf, width), F32), shape_of((2, half, width), F32),
         shape_of((in_rows + ghalf + half, width), BF)],
        [pl.BlockSpec((1, half, fc), lambda s, ids: (ids[0], 0, s)), out_block(ghalf, width), out_block(half, width), None],
        [vm((count, part), BF), vm((part, fc), F32), vm((fpart, width), F32), vm((part, width), F32)],
        grid=(steps,), vmem=28 if count <= 1024 else 60, work=(4e9, 12e6))
    sib_far = swap(sib)

    gw_q, keep, send, q_bias = kernel_call(
        "query", functools.partial(query_kernel, chips, depth, rows, part), ids,
        [sib, near, far_z, gq_low, gq_high] + shares, [ANY] + [None] * (depth + 4),
        [shape_of((half, width), F32), shape_of((half, span), BF), shape_of((half, span + width), BF), shape_of((8, width), F32)],
        [None] * 4,
        [vm((count, part), BF), vm((count, width), BF), vm((part, width), F32), vm((part, span), F32)], vmem=20 if count <= 1024 else 60, work=(1e9, 3e6))
    far = swap(send)
    shards = over_depth(jnp.concatenate([keep, far[:, 0:span]], axis=0))
    gx = kernel_call(
        "token_grad", functools.partial(token_grad_kernel, pack, lengths, rows, heads), ids,
        [far, question_lengths, passage_lengths, att, probs, a_low, b_low, first_rows],
        [ANY, SMEM, SMEM, pl.BlockSpec((2, hr, 256), lambda s, ids: (0, 0, s)),
         pl.BlockSpec((2, hr, 256), lambda s, ids: (0, 0, s)), None, None, None],
        [shape_of((tokens, width), F32)] * 2, [pl.BlockSpec((256, width), lambda s, ids: (s, 0))] * 2,
        grid=(tokens // 256,), vmem=24 if count <= 1024 else 60, work=(2e9, 9e6))

    gin, gback, gout = kernel_call(
        "fill", functools.partial(fill_kernel, in_rows), ids, [gx[0], gin, gback, gout, sib_far], [ANY, ANY, ANY, ANY, None],
        [shape_of(gin.shape, F32), shape_of(gback.shape, F32), shape_of(gout.shape, F32)],
        [pl.BlockSpec((1,) + a.shape[1:], lambda s, ids: (1 - ids[0], 0, 0)) for a in (gin, gback, gout)],
        aliases={2: 0, 3: 1, 4: 2}, vmem=20 if count <= 1024 else 60, work=(1e6, 8e6))

    (g_qkv,) = kernel_call(
        "assemble", functools.partial(assemble_kernel, depth), ids, [gout] + shards + [gw_q, far], [ANY] + [None] * (depth + 2),
        [shape_of((2, half, 3 * width), F32)], [None], vmem=20 if count <= 1024 else 60, work=(1e6, 3e6))

    n_in = ff // width
    small_all = jnp.concatenate([small, g_inb.reshape(-1, width), q_bias[0:4]], axis=0)
    small_far = swap(small_all)
    small_all = jnp.stack([jnp.where(first, small_all, small_far), jnp.where(first, small_far, small_all)])
    return (
        q_vectors,
        p_vectors,
        loss[:, 0],
        gx[0].reshape(question_tokens.shape),
        gx[1].reshape(passage_tokens.shape),
        g_qkv,
        jnp.stack([small_all[:, 8 + n_in], small_all[:, 6]], axis=1),
        gout,
        small_all[:, 4],
        small_all[:, 0:2],
        small_all[:, 2:4],
        gin,
        small_all[:, 8:8 + n_in].reshape(2, ff),
        gback,
        small_all[:, 5],
    )


def solution(mesh):
    split = P(("dp", "group"))
    return jax.shard_map(
        functools.partial(body, n_dp=mesh.shape["dp"], depth=mesh.shape["group"]),
        mesh=mesh,
        in_specs=(split, split, split, split, split) + (P(),) * 10,
        out_specs=(split, split, split, split, split, P(None, "dp", None), P(), P(None, "dp", None), P(), P(), P(),
                   P(None, "dp", None), P(), P(None, "dp", None), P()),
        check_vma=False,
    )
```

```python
import functools
import math

import jax
import jax.numpy as jnp
from jax import lax
from jax.experimental import pallas as pl
from jax.experimental.pallas import tpu as pltpu
from jax.sharding import PartitionSpec as P

HEAD_DIM = 64
EPSILON = 1e-12
MASKED = -1000000000.0
EXTRA = 128
BF = jnp.bfloat16
F32 = jnp.float32

NT = (((1,), (1,)), ((), ()))
TN = (((0,), (0,)), ((), ()))
NN = (((1,), (0,)), ((), ()))


def mm(left, right, dims=NN):
    return lax.dot_general(left, right, dims, preferred_element_type=F32)


def row_bounds(packed, len_ref, rows, length):
    bounds = []
    for r in range(rows):
        if packed:
            row, k = r // packed, r % packed
            start = row * length
            for earlier in range(k):
                start = start + len_ref[row, earlier]
            bounds.append((start, start + len_ref[row, k]))
        else:
            bounds.append((r * length, r * length + len_ref[r]))
    return bounds


def column(values, rows):
    at = lax.broadcasted_iota(jnp.int32, (rows, 1), 0)
    result = jnp.zeros((rows, 1), jnp.int32)
    for r, value in enumerate(values):
        result = jnp.where(at == r, value, result)
    return result


def head_mask(rows, heads, width):
    row_head = lax.broadcasted_iota(jnp.int32, (rows * heads, width), 0) // rows
    col_head = lax.broadcasted_iota(jnp.int32, (rows * heads, width), 1) // HEAD_DIM
    return row_head == col_head


def spread_heads(values, heads, mask):
    tiled = jnp.concatenate([values] * heads, axis=0)
    return jnp.where(mask, tiled, jnp.zeros_like(tiled))


def gather_heads(full, heads, rows, mask):
    kept = jnp.where(mask, full, jnp.zeros_like(full))
    return jnp.sum(kept.reshape(heads, rows, full.shape[1]), axis=0)


def start_all(copies):
    for copy in copies:
        copy.start()


def order_of(positives, rows, depth):
    owner = positives // rows
    dp = owner // depth
    return ((dp // 2 * depth + owner % depth) * 2 + dp % 2) * rows + positives % rows


def attend_kernel(pack, lengths, rows, heads, chips, depth, ids, qlen_ref, plen_ref, pos_ref, xq_hbm, xp_hbm, w_hbm, wo_hbm,
                  bias_ref, ob_ref, pack_mine, pack_other, early_mine, early_other, a_ref, p_ref, x_buf, w_buf, wo_buf, sems):
    c, j = ids[0], ids[1]
    width = wo_buf.shape[2]
    part = width // chips
    tokens = x_buf.shape[1]
    copies = []
    for e in range(2):
        copies.append(pltpu.make_async_copy(xq_hbm if e == 0 else xp_hbm, x_buf.at[e], sems.at[e * 5]))
        for k in range(3):
            copies.append(pltpu.make_async_copy(w_hbm.at[e, :, pl.ds(k * width, width)], w_buf.at[e, k], sems.at[e * 5 + 1 + k]))
        copies.append(pltpu.make_async_copy(wo_hbm.at[e], wo_buf.at[e], sems.at[e * 5 + 4]))
    ahead = 4
    start_all(copies[:ahead])

    def arrive(k):
        copies[k].wait()
        if k + ahead < len(copies):
            copies[k + ahead].start()

    mask = head_mask(rows, heads, width)
    pos = order_of(column([pos_ref[r] for r in range(rows)], rows), rows, depth)
    for e in range(2):
        bounds = row_bounds(pack if e else 0, plen_ref if e else qlen_ref, rows, lengths[e])
        start = column([b[0] for b in bounds], rows)
        stop = column([b[1] for b in bounds], rows)
        lane = lax.broadcasted_iota(jnp.int32, (rows, tokens), 1)
        bias = bias_ref[e]
        arrive(e * 5 + 0)
        x = x_buf[e]
        x_cls = mm(jnp.where(lane == start, 1.0, 0.0).astype(BF), x)
        xc = x_cls.astype(BF)
        arrive(e * 5 + 1)
        q = (mm(xc, w_buf[e, 0]) + bias[0:1, :]).astype(BF)
        arrive(e * 5 + 2)
        a_low = mm(spread_heads(q, heads, mask), w_buf[e, 1], NT).astype(BF)
        a_ref[e] = a_low
        scores = mm(a_low, x, NT) * 0.125
        lane_all = lax.broadcasted_iota(jnp.int32, scores.shape, 1)
        starts = jnp.concatenate([start] * heads, axis=0)
        stops = jnp.concatenate([stop] * heads, axis=0)
        scores = jnp.where((lane_all >= starts) & (lane_all < stops), scores, MASKED)
        peak = jnp.max(scores, axis=1, keepdims=True)
        shifted = jnp.exp(scores - peak)
        p = shifted / jnp.sum(shifted, axis=1, keepdims=True)
        p_ref[e] = p
        p_low = p.astype(BF)
        sums = jnp.sum(p_low.astype(F32), axis=1, keepdims=True)
        pooled = mm(p_low, x).astype(BF)
        arrive(e * 5 + 3)
        full = mm(pooled, w_buf[e, 2]) + sums * bias[1:2, :]
        ctx = gather_heads(full, heads, rows, mask).astype(BF)
        arrive(e * 5 + 4)
        hidden = x_cls + mm(ctx, wo_buf[e]) + ob_ref[e:e + 1, :]
        mean = jnp.mean(hidden, axis=1, keepdims=True)
        centred = hidden - mean
        rstd = lax.rsqrt(jnp.mean(centred * centred, axis=1, keepdims=True) + EPSILON)
        hat = (centred * rstd).astype(BF)
        rstd_high = rstd.astype(BF).astype(F32)
        lanes = lax.broadcasted_iota(jnp.int32, (rows, EXTRA), 1)
        extra = jnp.where(lanes == 0, rstd_high, 0.0)
        extra = jnp.where(lanes == 1, rstd - rstd_high, extra)
        extra = jnp.where(lanes == 2, (pos // 32).astype(F32), extra)
        extra = jnp.where(lanes == 3, (pos % 32).astype(F32), extra)
        for h in range(heads):
            extra = jnp.where(lanes == 16 + h, sums[h * rows:(h + 1) * rows] - 1.0, extra)
        extra = extra.astype(BF)

        def put(pack_ref, early_ref):
            pack_ref[:, 0:width] = hat
            pack_ref[:, width:] = extra
            for chip in range(chips):
                slot = lax.rem(chip - j + chips, chips)
                cut = slice(chip * part, (chip + 1) * part)
                pieces = [pooled[h * rows:(h + 1) * rows, cut] for h in range(heads)] + [xc[:, cut], ctx[:, cut], q]
                early_ref[slot] = jnp.concatenate(pieces, axis=1)

        @pl.when(c == e)
        def keep():
            put(pack_mine, early_mine)

        @pl.when(c != e)
        def give():
            put(pack_other, early_other)


def stage_kernel(ids, after_ref, win_hbm, wback_hbm, wout_hbm, xq_hbm, xp_hbm, w_hbm, win, wback, wout, x_buf, w_buf, sems):
    c = ids[0]
    width = wout.shape[0]
    copies = [pltpu.make_async_copy(win_hbm.at[c], win, sems.at[0]), pltpu.make_async_copy(wback_hbm.at[c], wback, sems.at[1]),
              pltpu.make_async_copy(wout_hbm.at[c], wout, sems.at[2]), pltpu.make_async_copy(xq_hbm, x_buf.at[0], sems.at[3]),
              pltpu.make_async_copy(xp_hbm, x_buf.at[1], sems.at[4])]
    for e in range(2):
        for k in range(3):
            copies.append(pltpu.make_async_copy(w_hbm.at[e, :, pl.ds(k * width, width)], w_buf.at[e, k], sems.at[5 + 3 * e + k]))
    start_all(copies)
    for copy in copies:
        copy.wait()


def gelu_parts(x):
    bell = jnp.exp(-0.5 * x * x)
    t = 1.0 / (1.0 + (0.3275911 * math.sqrt(0.5)) * jnp.abs(x))
    tail = 1.061405429 * 0.5
    for factor in (-1.453152027, 1.421413741, -0.284496736, 0.254829592):
        tail = tail * t + factor * 0.5
    tail = tail * t * bell
    cdf = jnp.where(x >= 0.0, 1.0 - tail, tail)
    return x * cdf, cdf + x * bell * (1.0 / math.sqrt(2.0 * math.pi))


def relative_places(chips, depth, rows, c, j, z):
    for kx in range(chips):
        for kz in range(depth):
            for kc in range(2):
                core = c if kc == 0 else 1 - c
                place = ((lax.rem(j - kx + chips, chips) * depth + lax.rem(z - kz + depth, depth)) * 2 + core) * rows
                yield kx, kz, kc, pl.multiple_of(place, rows)


def doubling(n, masks):
    found = [0]
    for mask in masks:
        found = found + [k ^ mask for k in found]
    assert sorted(found) == list(range(n))
    return found


def depth_masks(depth):
    return [(1 << k) - 1 for k in range(1, depth.bit_length())]


def chip_masks(chips):
    return [1 << k for k in range(chips.bit_length() - 1)]


def place_of(chip, deep, core, depth, rows):
    return pl.multiple_of(((chip * depth + deep) * 2 + core) * rows, rows)


def crossed_blocks(refs, chips, depth, rows, c, j, z, part, lead):
    near = depth // 2
    for at, dz in enumerate(doubling(depth, depth_masks(depth))):
        for kc in range(2):
            core = c if kc == 0 else 1 - c
            first = ((at % near) * 2 + kc) * rows
            for kx in range(chips):
                place = place_of(lax.rem(j - kx + chips, chips), jnp.bitwise_xor(z, dz), core, depth, rows)
                yield refs[at // near], first, lead + 2 * kx * part, place


def over_rows(count, tile, work):
    if tile == count:
        work(pl.ds(0, count))
    else:
        def one(t, carry):
            work(pl.ds(pl.multiple_of(t * tile, tile), tile))
            return carry

        lax.fori_loop(0, count // tile, one, 0)


def forward_kernel(chips, depth, rows, steps, tile, part, ids, *refs):
    blocks = refs[:chips]
    gain_ref, shift_ref, win_ref, inb_ref, wback_ref, backb_ref = refs[chips:chips + 6]
    _, act_ref, slope_ref, vec_ref, hat2_ref, ex_ref, cut_ref, hat1_ref, _, total, nl, chunk = refs[chips + 6:]
    c, j, z = ids[0], ids[1], ids[2]
    width = vec_ref.shape[1]
    step = pl.program_id(0)

    @pl.when(step == 0)
    def start():
        for kx, kz, kc, place in relative_places(chips, depth, rows, c, j, z):
            at = (kz * 2 + kc) * rows
            hat1_ref[pl.ds(place, rows), :] = blocks[kx][at:at + rows, 0:width]
            ex_ref[pl.ds(place, rows), :] = blocks[kx][at:at + rows, width:].astype(F32)
        gain = gain_ref[c]
        shift = shift_ref[c]
        normed = hat1_ref[...].astype(F32) * gain[0:1, :] + shift[0:1, :]
        low = normed.astype(BF)
        nl[...] = low
        total[...] = normed + backb_ref[pl.ds(c, 1), :]
        source = lax.broadcasted_iota(jnp.int32, (width, part), 0)
        target = lax.broadcasted_iota(jnp.int32, (width, part), 1) + j * part
        cut_ref[...] = mm(low, jnp.where(source == target, 1.0, 0.0).astype(BF)).astype(BF)

    columns = slope_ref.shape[1]
    at = pl.multiple_of(step * columns, columns)
    fpart = act_ref.shape[1]
    bias = inb_ref[pl.ds(c, 1), pl.ds(at, columns)]
    strips = 2
    strip = nl.shape[0] // strips
    spans = [slice(k * strip, (k + 1) * strip) for k in range(strips)]

    def up(span):
        return mm(nl[span, :], win_ref[:, pl.ds(at, columns)]) + bias

    def down(span, pre):
        active, slope = gelu_parts(pre)
        active = active.astype(BF)
        chunk[span, :] = active
        slope_ref[span, :] = slope.astype(BF)
        total[span, :] += mm(active, wback_ref[pl.ds(at, columns), :])

    pre = up(spans[0])
    for k in range(strips):
        following = up(spans[k + 1]) if k + 1 < strips else None
        down(spans[k], pre)
        pre = following
    for q in range(columns // fpart):
        @pl.when(step * (columns // fpart) + q == j)
        def keep():
            act_ref[...] = chunk[:, q * fpart:(q + 1) * fpart]

    @pl.when(step == steps - 1)
    def finish():
        gain = gain_ref[c]
        shift = shift_ref[c]

        def normalise(part):
            second = total[part, :]
            mean = jnp.mean(second, axis=1, keepdims=True)
            centred = second - mean
            rstd = lax.rsqrt(jnp.mean(centred * centred, axis=1, keepdims=True) + EPSILON)
            hat = centred * rstd
            hat2_ref[part, :] = hat.astype(BF)
            vec_ref[part, :] = (hat * gain[1:2, :] + shift[1:2, :]).astype(BF)
            ex = ex_ref[part, :]
            lanes = lax.broadcasted_iota(jnp.int32, ex.shape, 1)
            pos = ex[:, 2:3] * 32.0 + ex[:, 3:4]
            ex_ref[part, :] = jnp.where(
                lanes == 0, ex[:, 0:1] + ex[:, 1:2], jnp.where(lanes == 1, rstd, jnp.where(lanes == 2, pos, ex)))

        over_rows(total.shape[0], tile, normalise)


def norm_back(grad, hat, rstd, gain):
    scaled = grad * gain
    inner = jnp.mean(scaled * hat, axis=1, keepdims=True)
    return rstd * (scaled - jnp.mean(scaled, axis=1, keepdims=True) - hat * inner)


def loss_kernel(depth, rows, tile, ids, own_ref, other_ref, ex_ref, hat2_ref, hat1_ref, slope_ref, gain_ref,
                wback, win, wout, second_ref, loss_ref, mine_ref, sib_ref, small_ref, qvec_ref, pvec_ref,
                wide_loss):
    c, j, z = ids[0], ids[1], ids[2]
    count, width = own_ref.shape
    scale = 2.0 / math.sqrt(width)
    own_at = pl.multiple_of(((j * depth + z) * 2 + c) * rows, rows)

    def softmax_part(questions, passages, pos):
        scores = mm(questions, passages, NT) * scale
        peak = jnp.max(scores, axis=1, keepdims=True)
        shifted = jnp.exp(scores - peak)
        totals = jnp.sum(shifted, axis=1, keepdims=True)
        hit = lax.broadcasted_iota(jnp.int32, scores.shape, 1) == pos.astype(jnp.int32)
        loss = peak + jnp.log(totals) - jnp.sum(jnp.where(hit, scores, 0.0), axis=1, keepdims=True)
        grad = (shifted / totals - jnp.where(hit, 1.0, 0.0)) * scale
        high = grad.astype(BF)
        return loss, high, (grad - high.astype(F32)).astype(BF)

    @pl.when(c == 0)
    def question_side():
        qvec_ref[...] = own_ref[pl.ds(own_at, rows), :]
        pvec_ref[...] = other_ref[pl.ds(own_at, rows), :]

        def work(part):
            loss, high, low = softmax_part(own_ref[part, :], other_ref[...], ex_ref[part, 2:3])
            wide_loss[part, :] = jnp.broadcast_to(loss, (tile, wide_loss.shape[1]))
            second_ref[part, :] = mm(high, other_ref[...]) + mm(low, other_ref[...])

        over_rows(count, tile, work)

    @pl.when(c == 1)
    def passage_side():
        pvec_ref[...] = own_ref[pl.ds(own_at, rows), :]
        qvec_ref[...] = other_ref[pl.ds(own_at, rows), :]
        if tile < count:
            second_ref[...] = jnp.zeros_like(second_ref)

        def work(part):
            loss, high, low = softmax_part(other_ref[part, :], own_ref[...], ex_ref[part, 2:3])
            wide_loss[part, :] = jnp.broadcast_to(loss, (tile, wide_loss.shape[1]))
            piece = mm(high, other_ref[part, :], TN) + mm(low, other_ref[part, :], TN)
            second_ref[...] = piece if tile == count else second_ref[...] + piece

        over_rows(count, tile, work)

    small_ref[...] = jnp.zeros_like(small_ref)
    losses = wide_loss[pl.ds(own_at, rows), :]
    diagonal = lax.broadcasted_iota(jnp.int32, losses.shape, 0) == lax.broadcasted_iota(jnp.int32, losses.shape, 1)
    loss_ref[...] = jnp.sum(jnp.where(diagonal, losses, 0.0), axis=0, keepdims=True)[:, 0:rows]

    def late_norm(part):
        grad = second_ref[part, :]
        hat = hat2_ref[part, :].astype(F32)
        small_ref[1:2, :] += jnp.sum(grad * hat, axis=0, keepdims=True)
        small_ref[3:4, :] += jnp.sum(grad, axis=0, keepdims=True)
        second = norm_back(grad, hat, ex_ref[part, 1:2], gain_ref[c][1:2, :])
        small_ref[5:6, :] += jnp.sum(second, axis=0, keepdims=True)
        second_ref[part, :] = second

    over_rows(count, tile, late_norm)

    chip_at = pl.multiple_of((j * depth + z) * 2 * rows, 2 * rows)
    second = second_ref[pl.ds(chip_at, 2 * rows), :]
    pre = (mm(second.astype(BF), wback[...], NT) * slope_ref[...].astype(F32)).astype(BF)
    normed = second + mm(pre, win[...], NT)
    hidden = norm_back(normed, hat1_ref[...].astype(F32), ex_ref[pl.ds(chip_at, 2 * rows), 0:1], gain_ref[c][0:1, :])
    ctx = mm(hidden.astype(BF), wout[...], NT).astype(BF).astype(F32)
    both = jnp.concatenate([hidden, ctx], axis=1)
    is_low = c == 0
    mine_ref[...] = jnp.where(is_low, both[:rows], both[rows:])
    sib_ref[...] = jnp.where(is_low, both[rows:], both[:rows])


def split_halves(value, scratch, c, own_ref_set, sib_ref_set):
    half = value.shape[0] // 2
    scratch[...] = value
    own_ref_set(scratch[pl.ds(pl.multiple_of(c * half, half), half), :])
    sib_ref_set(scratch[pl.ds(pl.multiple_of((1 - c) * half, half), half), :].astype(BF))


def backward_kernel(chips, depth, rows, steps, tile, ids, near_ref, second_ref, ex_ref, hat1_ref, slope_ref, wback_ref, win_ref,
                    gain_ref, wout_ref, small_in, gpl_ref, low_ref, hidden_ref, plane_ref, small_ref, column_ref, acc, gfull):
    c, j, z = ids[0], ids[1], ids[2]
    count, width = second_ref.shape
    step = pl.program_id(0)

    @pl.when(step == 0)
    def start():
        acc[...] = second_ref[...]
        low_ref[...] = second_ref[...].astype(BF)
        column_ref[...] = near_ref[:, 0:width]
        small_ref[0:8, :] = small_in[...]
        small_ref[8:, :] = jnp.zeros((8, width), F32)

    columns = slope_ref.shape[1]
    at = pl.multiple_of(step * columns, columns)
    pre = mm(low_ref[...], wback_ref[pl.ds(at, columns), :], NT) * slope_ref[...].astype(F32)
    bias = jnp.sum(pre, axis=0, keepdims=True)
    pre_low = pre.astype(BF)
    gpl_ref[...] = pre_low
    acc[...] += mm(pre_low, win_ref[:, pl.ds(at, columns)], NT)
    for s in range(steps):
        @pl.when(step == s)
        def keep_bias():
            line, lane = 8 + s * columns // width, s * columns % width
            small_ref[line:line + 1, lane:lane + columns] = bias

    @pl.when(step == steps - 1)
    def finish():
        lanes = lax.broadcasted_iota(jnp.int32, (EXTRA, width), 0)
        heads_of = lax.broadcasted_iota(jnp.int32, (EXTRA, width), 1) // HEAD_DIM
        expand = jnp.where(lanes == heads_of + 16, 1.0, 0.0).astype(BF)

        def early_norm(part):
            grad = acc[part, :]
            hat = hat1_ref[part, :].astype(F32)
            small_ref[0:1, :] += jnp.sum(grad * hat, axis=0, keepdims=True)
            small_ref[2:3, :] += jnp.sum(grad, axis=0, keepdims=True)
            hidden = norm_back(grad, hat, ex_ref[part, 0:1], gain_ref[c][0:1, :])
            small_ref[4:5, :] += jnp.sum(hidden, axis=0, keepdims=True)
            hidden_low = hidden.astype(BF)
            hidden_ref[part, :] = hidden_low
            ctx = mm(hidden_low, wout_ref[...], NT).astype(BF)
            sums = mm(ex_ref[part, :].astype(BF), expand) + 1.0
            small_ref[6:7, :] += jnp.sum(sums * ctx.astype(F32), axis=0, keepdims=True)
            gfull[part, :] = ctx

        over_rows(count, tile, early_norm)
        for kx in range(chips):
            for kc in range(2):
                core = c if kc == 0 else 1 - c
                place = pl.multiple_of(((lax.rem(j - kx + chips, chips) * depth + z) * 2 + core) * rows, rows)
                at = (kx * 2 + kc) * rows
                plane_ref[at:at + rows, :] = gfull[pl.ds(place, rows), :]


def weight_kernel(chips, depth, rows, part, steps, ids, after_ref, near_ref, far_ref, gpl_ref, low_ref, hidden_ref, act_ref, cut_ref,
                  gin_ref, gback_ref, gout_ref, sib_ref, ctx_all, in_scr, back_scr, out_scr):
    c, j, z = ids[0], ids[1], ids[2]
    step = pl.program_id(0)
    width = low_ref.shape[1]
    half = part // 2
    ghalf = back_scr.shape[0] // 2
    columns = gpl_ref.shape[1]
    in_rows = half * (columns * steps // width)

    def set_own(ref):
        def setter(value):
            ref[0] = value
        return setter

    def set_sib(at, rows, lane, lanes):
        def setter(value):
            sib_ref[at:at + rows, lane:lane + lanes] = value
        return setter

    @pl.when(step == 0)
    def start():
        split_halves(mm(act_ref[...], low_ref[...], TN), back_scr, c, set_own(gback_ref), set_sib(in_rows, ghalf, 0, width))
        for ref, first, lane, place in crossed_blocks((near_ref, far_ref), chips, depth, rows, c, j, z, part, chips * part):
            ctx_all[pl.ds(place, rows), :] = ref[first:first + rows, lane + part:lane + 2 * part]
        split_halves(mm(ctx_all[...], hidden_ref[...], TN), out_scr, c, set_own(gout_ref), set_sib(in_rows + ghalf, half, 0, width))

    piece = mm(cut_ref[...], gpl_ref[...], TN)
    in_scr[...] = piece
    gin_ref[0] = in_scr[pl.ds(pl.multiple_of(c * half, half), half), :]
    other = in_scr[pl.ds(pl.multiple_of((1 - c) * half, half), half), :].astype(BF)
    for s in range(steps):
        @pl.when(step == s)
        def keep():
            set_sib((s * columns // width) * half, half, s * columns % width, columns)(other)


def attend_back_kernel(rows, heads, chips, ids, mine_ref, far_ref, x_buf, w_buf, bias_ref, p_ref, *refs):
    early = refs[:chips]
    late_mine, late_other, att_ref, b_ref, first_ref, cross_ref = refs[chips:]
    c, j = ids[0], ids[1]
    width = bias_ref.shape[2]
    part = width // chips
    cross_ref[...] = jnp.concatenate([b[:, heads * part:(heads + 2) * part] for b in early], axis=1)
    mask = head_mask(rows, heads, width)
    for e in range(2):
        gg = jnp.where(c == e, mine_ref[...], far_ref[...])
        blocks = spread_heads(gg[:, width:], heads, mask)
        constant = jnp.sum(blocks * bias_ref[e][1:2, :], axis=1, keepdims=True)
        b_low = mm(blocks.astype(BF), w_buf[e, 2], NT).astype(BF)
        b_ref[e] = b_low
        p = p_ref[e]
        x = x_buf[e]
        probs = mm(b_low, x, NT) + constant
        att = (p * (probs - jnp.sum(probs * p, axis=1, keepdims=True))).astype(BF)
        att_ref[e] = att
        y_low = mm(att, x).astype(BF)
        gq_low = (gather_heads(mm(y_low, w_buf[e, 1]), heads, rows, mask) * 0.125).astype(BF)

        def put(late_ref):
            for chip in range(chips):
                slot = lax.rem(chip - j + chips, chips)
                cut = slice(chip * part, (chip + 1) * part)
                late_ref[slot] = jnp.concatenate([y_low[h * rows:(h + 1) * rows, cut] for h in range(heads)] + [gq_low], axis=1)

        @pl.when(c == e)
        def keep():
            put(late_mine)

        @pl.when(c != e)
        def give():
            put(late_other)

        first_ref[e] = gg[:, 0:width] + mm(gq_low, w_buf[e, 0], NT)


def token_grad_kernel(pack, lengths, rows, heads, ids, after_ref, qlen_ref, plen_ref, att_ref, p_ref, a_ref, b_ref, first_ref,
                      gq_ref, gp_ref):
    tile = gq_ref.shape[0]
    at = pl.program_id(0) * tile
    lane = lax.broadcasted_iota(jnp.int32, (rows, tile), 1) + at
    for e in range(2):
        bounds = row_bounds(pack if e else 0, plen_ref if e else qlen_ref, rows, lengths[e])
        pick = jnp.where(lane == column([b[0] for b in bounds], rows), 1.0, 0.0).astype(BF)
        first = first_ref[e]
        high = first.astype(BF)
        rest = first - high.astype(F32)
        middle = rest.astype(BF)
        last = (rest - middle.astype(F32)).astype(BF)
        left = jnp.concatenate([att_ref[e], p_ref[e].astype(BF), pick, pick, pick], axis=0)
        right = jnp.concatenate([a_ref[e] * jnp.asarray(0.125, BF), b_ref[e], high, middle, last], axis=0)
        out = gp_ref if e else gq_ref
        out[...] = mm(left, right, TN)


def head_sums(factor, vectors, heads, part):
    width = vectors.shape[1]
    full = mm(factor, vectors, TN)
    row_head = lax.broadcasted_iota(jnp.int32, full.shape, 0) // part
    col_head = lax.broadcasted_iota(jnp.int32, full.shape, 1) // HEAD_DIM
    kept = jnp.where(row_head == col_head, full, 0.0)
    return jnp.sum(kept.reshape(heads, part, width), axis=0)


def share_kernel(heads, chips, depth, part, ids, *refs):
    late = refs[:chips]
    early = refs[chips:2 * chips]
    plane_ref = refs[2 * chips]
    outs = refs[2 * chips + 2:2 * chips + 2 + depth]
    column_ref, scratch = refs[-2:]
    column_ref[...] = refs[2 * chips + 1][...]
    z = ids[2]
    width = plane_ref.shape[1]
    hp = heads * part
    y = jnp.concatenate([b[:, 0:hp] for b in late], axis=0)
    pooled = jnp.concatenate([b[:, 0:hp] for b in early], axis=0)
    q = jnp.concatenate([b[:, hp + 2 * part:] for b in early], axis=0)
    scratch[:, 0:width] = head_sums(y, q, heads, part) * 0.125
    scratch[:, width:] = head_sums(pooled, plane_ref[...], heads, part)
    span = 2 * width // depth
    for k in range(depth):
        at = pl.multiple_of(lax.rem(z + k, depth) * span, span)
        outs[k][...] = scratch[:, pl.ds(at, span)].astype(BF)


def query_kernel(chips, depth, rows, part, ids, sib_in, near_ref, far_ref, low_chips, high_chips, *refs):
    shares = refs[:depth]
    small_in, gw_ref, keep_ref, send_ref, small_ref, sib_out, x_all, gq_all, q_scr, share_scr = refs[depth:]
    c, j, z = ids[0], ids[1], ids[2]
    for ref, first, lane, place in crossed_blocks((near_ref, far_ref), chips, depth, rows, c, j, z, part, chips * part):
        x_all[pl.ds(place, rows), :] = ref[first:first + rows, lane:lane + part]
    few = chips // 2
    for at_chip, dx in enumerate(doubling(chips, chip_masks(chips))):
        for at_depth, dz in enumerate(doubling(depth, depth_masks(depth))):
            for kc in range(2):
                core = c if kc == 0 else 1 - c
                place = place_of(jnp.bitwise_xor(j, dx), jnp.bitwise_xor(z, dz), core, depth, rows)
                at = (((at_chip % few) * depth + at_depth) * 2 + kc) * rows
                gq_all[pl.ds(place, rows), :] = (low_chips, high_chips)[at_chip // few][at:at + rows, :]
    gq = gq_all[...]
    half = part // 2
    width = gq.shape[1]
    span = shares[0].shape[1]
    bias = jnp.sum(gq.astype(F32), axis=0, keepdims=True)
    small_ref[...] = small_in[...]
    small_ref[7:8, :] = bias
    total = shares[0][...].astype(F32)
    for k in range(1, depth):
        total = total + shares[k][...].astype(F32)
    share_scr[...] = total
    q_scr[...] = mm(x_all[...], gq, TN)
    own = pl.ds(pl.multiple_of(c * half, half), half)
    sib = pl.ds(pl.multiple_of((1 - c) * half, half), half)
    keep_ref[...] = share_scr[own, :].astype(BF)
    gw_ref[...] = q_scr[own, :]
    send_ref[:, 0:span] = share_scr[sib, :].astype(BF)
    send_ref[:, span:] = q_scr[sib, :].astype(BF)


def assemble_kernel(depth, ids, after_ref, *refs):
    shards = refs[:depth]
    own_ref, far_ref, out_ref = refs[depth:]
    c, z = ids[0], ids[2]
    half, width = own_ref.shape
    span = shards[0].shape[1]
    out_ref[c, :, 0:width] = own_ref[...]
    out_ref[1 - c, :, 0:width] = far_ref[:, span:].astype(F32)
    for k in range(depth):
        at = pl.multiple_of(width + lax.rem(z - k + depth, depth) * span, 128)
        out_ref[c, :, pl.ds(at, span)] = shards[k][0:half, :].astype(F32)
        out_ref[1 - c, :, pl.ds(at, span)] = shards[k][half:, :].astype(F32)


def fill_kernel(in_rows, ids, after_ref, in_hbm, back_hbm, out_hbm, sib_ref, own_ref, other_ref, gin_ref, gback_ref, gout_ref,
                qv_ref, outb_ref, gains_ref, shifts_ref, inb_ref, backb_ref):
    c = ids[0]
    half, width = gout_ref.shape[1], gout_ref.shape[2]
    ghalf = gback_ref.shape[1]
    for k in range(in_rows // half):
        gin_ref[0, :, k * width:(k + 1) * width] = sib_ref[k * half:(k + 1) * half, :].astype(F32)
    gback_ref[0] = sib_ref[in_rows:in_rows + ghalf, :].astype(F32)
    gout_ref[0] = sib_ref[in_rows + ghalf:, :].astype(F32)
    for e in range(2):
        small = jnp.where(c == e, own_ref[...], other_ref[...])
        gains_ref[e] = small[0:2]
        shifts_ref[e] = small[2:4]
        outb_ref[e:e + 1, :] = small[4:5]
        backb_ref[e:e + 1, :] = small[5:6]
        qv_ref[e, 0:1, :] = small[7:8]
        qv_ref[e, 1:2, :] = small[6:7]
        for k in range(inb_ref.shape[1] // width):
            inb_ref[e:e + 1, k * width:(k + 1) * width] = small[8 + k:9 + k]


def full_spec(shape):
    return pl.BlockSpec(tuple(shape), lambda *_: (0,) * len(shape))


def shape_of(shape, dtype):
    return jax.ShapeDtypeStruct(tuple(shape), dtype)


ANY = pl.BlockSpec(memory_space=pl.ANY)
SMEM = pl.BlockSpec(memory_space=pltpu.SMEM)


def kernel_call(name, kernel, ids, args, specs, outs, out_specs, scratch=(), grid=(1,), work=(0, 0), aliases=None, vmem=60):
    specs = [full_spec(a.shape) if s is None else s for a, s in zip(args, specs)]
    out_specs = [full_spec(o.shape) if s is None else s for o, s in zip(outs, out_specs)]
    return pl.pallas_call(
        kernel,
        grid_spec=pltpu.PrefetchScalarGridSpec(num_scalar_prefetch=1, grid=grid, in_specs=specs, out_specs=out_specs,
                                               scratch_shapes=list(scratch)),
        out_shape=list(outs),
        input_output_aliases=aliases or {},
        compiler_params=pltpu.CompilerParams(vmem_limit_bytes=vmem * 1024 * 1024),
        cost_estimate=pl.CostEstimate(flops=int(work[0]), bytes_accessed=int(work[1]), transcendentals=0),
        name=name,
    )(ids, *args)


def body(question_tokens, question_lengths, passage_tokens, passage_lengths, positives, w_qkv, qv_bias, w_out, out_bias,
         norm_gains, norm_biases, w_in, in_bias, w_back, back_bias, *, n_dp, depth):
    width = question_tokens.shape[2]
    heads = width // HEAD_DIM
    rows = question_tokens.shape[0]
    pack = passage_lengths.shape[1]
    lengths = (question_tokens.shape[1], passage_tokens.shape[1])
    tokens = rows * lengths[0]
    ff = w_in.shape[2]
    chips = n_dp // 2
    count = n_dp * depth * rows
    part = width // chips
    half = part // 2
    fpart = ff // chips
    hr = heads * rows
    i = lax.axis_index("dp")
    z = lax.axis_index("group")
    c, j = i % 2, i // 2
    ids = jnp.stack([c, j, z]).astype(jnp.int32)
    vm = pltpu.VMEM
    dma = pltpu.SemaphoreType.DMA

    def swap(x):
        return lax.ppermute(x, "dp", [(k, k ^ 1) for k in range(n_dp)])

    def to_chip(x, k):
        return lax.ppermute(x, "dp", [(s, ((s // 2 + k) % chips) * 2 + s % 2) for s in range(n_dp)])

    def to_depth(x, k):
        return lax.ppermute(x, "group", [(s, (s + k) % depth) for s in range(depth)])

    def over_depth(x):
        return [x] + [to_depth(x, k) for k in range(1, depth)]

    def over_plane(x):
        return [x] + [to_chip(x, k) for k in range(1, chips)]

    small_enough = count <= 1024
    kept = pl.BlockSpec(memory_space=pltpu.VMEM) if small_enough else None
    keep_shape = (lambda shape: pltpu.VMEM(shape, BF)) if small_enough else (lambda shape: shape_of(shape, BF))

    xq = question_tokens.reshape(tokens, width)
    xp = passage_tokens.reshape(tokens, width)

    wide = (heads + 2) * part + width
    pack_mine, pack_other, early_mine, early_other, a_low, probs = kernel_call(
        "attend", functools.partial(attend_kernel, pack, lengths, rows, heads, chips, depth), ids,
        [question_lengths, passage_lengths, positives, xq, xp, w_qkv, w_out, qv_bias, out_bias],
        [SMEM, SMEM, SMEM, ANY, ANY, ANY, ANY, None, None],
        [shape_of((rows, width + EXTRA), BF)] * 2 + [shape_of((chips, rows, wide), BF)] * 2 + [
            shape_of((2, hr, width), BF), shape_of((2, hr, tokens), F32)],
        [None] * 6,
        [vm((2, tokens, width), BF), vm((2, 3, width, width), BF), vm((2, width, width), BF), dma((10,))],
        vmem=60 if count <= 1024 else 60, work=(6e9, 13e6))

    pair = jnp.concatenate([pack_mine, swap(pack_other)], axis=0)
    column_rows = jnp.concatenate(over_depth(pair), axis=0)
    plane = over_plane(column_rows)
    win_kept, wback_kept, wout_kept, x_kept, w_kept = kernel_call(
        "stage", stage_kernel, ids, [column_rows, w_in, w_back, w_out, xq, xp, w_qkv], [ANY] * 7,
        [keep_shape((width, ff)), keep_shape((ff, width)), keep_shape((width, width)), keep_shape((2, tokens, width)),
         keep_shape((2, 3, width, width))], [kept] * 5, [dma((11,))],
        vmem=24 if count <= 1024 else 60, work=(5e9, 10e6))

    fc = max(fpart, 384)
    steps = ff // fc
    tile = count if count <= 1024 else 128
    row = lambda w: full_spec((count, w))
    act, slope, vec, hat2, ex, cut, hat1, early_other = kernel_call(
        "forward", functools.partial(forward_kernel, chips, depth, rows, steps, tile, part), ids,
        plane + [norm_gains, norm_biases, win_kept, in_bias, wback_kept, back_bias, early_other],
        [None] * chips + [None, None, kept, None, kept, None, ANY],
        [shape_of((count, fpart), BF), shape_of((count, ff), BF), shape_of((count, width), BF),
         shape_of((count, width), BF), shape_of((count, EXTRA), F32), shape_of((count, part), BF), shape_of((count, width), BF),
         shape_of(early_other.shape, BF)],
        [None, pl.BlockSpec((count, fc), lambda s, ids: (0, s)), None, None, None, None, None, ANY],
        [vm((count, width), F32), vm((count, width), BF), vm((count, fc), BF)], grid=(steps,), vmem=24 if count <= 1024 else 60, work=(10e9, 18e6),
        aliases={1 + chips + 6: 7})

    vec_other = swap(vec)
    hp = heads * part

    early_far = swap(early_other)
    payload = [jnp.concatenate([early_mine[k], early_far[k]], axis=0) for k in range(chips)]
    early = [payload[0]] + [to_chip(payload[k], k) for k in range(1, chips)]

    chip_block = lambda w: pl.BlockSpec((2 * rows, w), lambda s, ids: (ids[1] * depth + ids[2], 0))
    second, loss, gg_mine, gg_sib, small, q_vectors, p_vectors = kernel_call(
        "loss", functools.partial(loss_kernel, depth, rows, tile), ids,
        [vec, vec_other, ex, hat2, hat1, slope, norm_gains, wback_kept, win_kept, wout_kept],
        [None, None, None, None, chip_block(width), chip_block(ff), None, kept, kept, kept],
        [shape_of((count, width), F32), shape_of((1, rows), F32), shape_of((rows, 2 * width), F32),
         shape_of((rows, 2 * width), F32), shape_of((8, width), F32), shape_of((rows, width), BF), shape_of((rows, width), BF)],
        [None] * 7,
        [vm((count, EXTRA), F32)],
        vmem=24 if count <= 1024 else 60, work=(8e9, 16e6))

    late_mine, late_other, att, b_low, first_rows, crossed = kernel_call(
        "attend_back", functools.partial(attend_back_kernel, rows, heads, chips), ids,
        [gg_mine, swap(gg_sib), x_kept, w_kept, qv_bias, probs] + early,
        [None, None, kept, kept, None, None] + [None] * chips,
        [shape_of((chips, rows, hp + width), BF)] * 2 + [
            shape_of((2, hr, tokens), BF), shape_of((2, hr, width), BF), shape_of((2, rows, width), F32),
            shape_of((2 * rows, 2 * width), BF)],
        [None] * 6,
        vmem=24 if count <= 1024 else 60, work=(6e9, 16e6))

    late_far = swap(late_other)
    payload = [jnp.concatenate([late_mine[k], late_far[k]], axis=0) for k in range(chips)]
    late = [payload[0]] + [to_chip(payload[k], k) for k in range(1, chips)]

    def xor_depth(x, mask):
        return lax.ppermute(x, "group", [(s, s ^ mask) for s in range(depth)])

    def xor_chip(x, mask):
        return lax.ppermute(x, "dp", [(s, s ^ (2 * mask)) for s in range(n_dp)])

    def double(x, step, masks):
        for mask in masks:
            x = jnp.concatenate([x, step(x, mask)], axis=0)
        return x

    near = double(jnp.concatenate([payload[0][:, hp:], crossed], axis=1), xor_depth, depth_masks(depth)[:-1])
    far_z = xor_depth(near, depth_masks(depth)[-1])
    gpl, low, hidden_low, g_plane, small, gq_near = kernel_call(
        "backward", functools.partial(backward_kernel, chips, depth, rows, steps, tile), ids,
        [near, second, ex, hat1, slope, wback_kept, win_kept, norm_gains, wout_kept, small],
        [None, None, None, None, pl.BlockSpec((count, fc), lambda s, ids: (0, s)),
         kept, kept, None, kept, None],
        [shape_of((count, ff), BF), shape_of((count, width), BF), shape_of((count, width), BF),
         shape_of((chips * 2 * rows, width), BF), shape_of((16, width), F32), shape_of((near.shape[0], width), BF)],
        [pl.BlockSpec((count, fc), lambda s, ids: (0, s)), None, None, None, None, None],
        [vm((count, width), F32), vm((count, width), BF)], grid=(steps,), vmem=36 if count <= 1024 else 60, work=(12e9, 18e6))

    gq_column = jnp.concatenate([gq_near, far_z[:, 0:width]], axis=0)

    span = 2 * width // depth
    *shares, gq_first = kernel_call(
        "share", functools.partial(share_kernel, heads, chips, depth, part), ids,
        late + early + [g_plane, gq_column], [None] * (2 * chips + 2),
        [shape_of((part, span), BF)] * depth + [shape_of(gq_column.shape, BF)], [None] * (depth + 1),
        [vm((part, 2 * width), F32)], vmem=40 if count <= 1024 else 60, work=(1e9, 3e6))
    masks = chip_masks(chips)
    gq_low = jnp.concatenate([gq_first, xor_chip(gq_column, masks[0])], axis=0)
    gq_low = double(gq_low, xor_chip, masks[1:-1])
    gq_high = xor_chip(gq_low, masks[-1])
    shares = [shares[0]] + [to_depth(shares[k], k) for k in range(1, depth)]

    ghalf = fpart // 2
    out_block = lambda r, w: pl.BlockSpec((1, r, w), lambda s, ids: (ids[0], 0, 0))
    in_rows = half * ff // width
    gin, gback, gout, sib = kernel_call(
        "weight", functools.partial(weight_kernel, chips, depth, rows, part, steps), ids,
        [shares[0], near, far_z, gpl, low, hidden_low, act, cut],
        [ANY, None, None, pl.BlockSpec((count, fc), lambda s, ids: (0, s)), None, None,
         None, None],
        [shape_of((2, half, ff), F32), shape_of((2, ghalf, width), F32), shape_of((2, half, width), F32),
         shape_of((in_rows + ghalf + half, width), BF)],
        [pl.BlockSpec((1, half, fc), lambda s, ids: (ids[0], 0, s)), out_block(ghalf, width), out_block(half, width), None],
        [vm((count, part), BF), vm((part, fc), F32), vm((fpart, width), F32), vm((part, width), F32)],
        grid=(steps,), vmem=44 if count <= 1024 else 60, work=(4e9, 12e6))
    gw_q, keep, send, small, sib = kernel_call(
        "query", functools.partial(query_kernel, chips, depth, rows, part), ids,
        [sib, near, far_z, gq_low, gq_high] + shares + [small], [ANY] + [None] * (depth + 5),
        [shape_of((half, width), F32), shape_of((half, span), BF), shape_of((half, span + width), BF), shape_of((16, width), F32),
         shape_of(sib.shape, BF)],
        [None] * 4 + [ANY],
        [vm((count, part), BF), vm((count, width), BF), vm((part, width), F32), vm((part, span), F32)], vmem=20 if count <= 1024 else 60, aliases={1: 4}, work=(1e9, 3e6))
    sib_far = swap(sib)
    far = swap(send)
    shards = over_depth(jnp.concatenate([keep, far[:, 0:span]], axis=0))
    gx = kernel_call(
        "token_grad", functools.partial(token_grad_kernel, pack, lengths, rows, heads), ids,
        [far, question_lengths, passage_lengths, att, probs, a_low, b_low, first_rows],
        [ANY, SMEM, SMEM, pl.BlockSpec((2, hr, 256), lambda s, ids: (0, 0, s)),
         pl.BlockSpec((2, hr, 256), lambda s, ids: (0, 0, s)), None, None, None],
        [shape_of((tokens, width), F32)] * 2, [pl.BlockSpec((256, width), lambda s, ids: (s, 0))] * 2,
        grid=(tokens // 256,), vmem=24 if count <= 1024 else 60, work=(2e9, 9e6))

    gin, gback, gout, g_qv, g_outb, g_gains, g_shifts, g_inb, g_backb = kernel_call(
        "fill", functools.partial(fill_kernel, in_rows), ids, [gx[0], gin, gback, gout, sib_far, small, swap(small)],
        [ANY, ANY, ANY, ANY, None, None, None],
        [shape_of(gin.shape, F32), shape_of(gback.shape, F32), shape_of(gout.shape, F32), shape_of((2, 2, width), F32),
         shape_of((2, width), F32), shape_of((2, 2, width), F32), shape_of((2, 2, width), F32), shape_of((2, ff), F32),
         shape_of((2, width), F32)],
        [pl.BlockSpec((1,) + a.shape[1:], lambda s, ids: (1 - ids[0], 0, 0)) for a in (gin, gback, gout)] + [None] * 6,
        aliases={2: 0, 3: 1, 4: 2}, vmem=20 if count <= 1024 else 60, work=(1e6, 8e6))

    (g_qkv,) = kernel_call(
        "assemble", functools.partial(assemble_kernel, depth), ids, [gout] + shards + [gw_q, far], [ANY] + [None] * (depth + 2),
        [shape_of((2, half, 3 * width), F32)], [None], vmem=20 if count <= 1024 else 60, work=(1e6, 3e6))

    return (
        q_vectors,
        p_vectors,
        loss.reshape(rows),
        gx[0].reshape(question_tokens.shape),
        gx[1].reshape(passage_tokens.shape),
        g_qkv,
        g_qv,
        gout,
        g_outb,
        g_gains,
        g_shifts,
        gin,
        g_inb,
        gback,
        g_backb,
    )


def solution(mesh):
    split = P(("dp", "group"))
    return jax.shard_map(
        functools.partial(body, n_dp=mesh.shape["dp"], depth=mesh.shape["group"]),
        mesh=mesh,
        in_specs=(split, split, split, split, split) + (P(),) * 10,
        out_specs=(split, split, split, split, split, P(None, "dp", None), P(), P(None, "dp", None), P(), P(), P(),
                   P(None, "dp", None), P(), P(None, "dp", None), P()),
        check_vma=False,
    )
```

```python
import functools
import math

import jax
import jax.numpy as jnp
from jax import lax
from jax.experimental import pallas as pl
from jax.experimental.pallas import tpu as pltpu
from jax.sharding import PartitionSpec as P

HEAD_DIM = 64
EPSILON = 1e-12
MASKED = -1000000000.0
EXTRA = 128
BF = jnp.bfloat16
F32 = jnp.float32

NT = (((1,), (1,)), ((), ()))
TN = (((0,), (0,)), ((), ()))
NN = (((1,), (0,)), ((), ()))


def mm(left, right, dims=NN):
    return lax.dot_general(left, right, dims, preferred_element_type=F32)


def row_bounds(packed, len_ref, rows, length):
    bounds = []
    for r in range(rows):
        if packed:
            row, k = r // packed, r % packed
            start = row * length
            for earlier in range(k):
                start = start + len_ref[row, earlier]
            bounds.append((start, start + len_ref[row, k]))
        else:
            bounds.append((r * length, r * length + len_ref[r]))
    return bounds


def column(values, rows):
    at = lax.broadcasted_iota(jnp.int32, (rows, 1), 0)
    result = jnp.zeros((rows, 1), jnp.int32)
    for r, value in enumerate(values):
        result = jnp.where(at == r, value, result)
    return result


def head_mask(rows, heads, width):
    row_head = lax.broadcasted_iota(jnp.int32, (rows * heads, width), 0) // rows
    col_head = lax.broadcasted_iota(jnp.int32, (rows * heads, width), 1) // HEAD_DIM
    return row_head == col_head


def spread_heads(values, heads, mask):
    tiled = jnp.concatenate([values] * heads, axis=0)
    return jnp.where(mask, tiled, jnp.zeros_like(tiled))


def gather_heads(full, heads, rows, mask):
    kept = jnp.where(mask, full, jnp.zeros_like(full))
    return jnp.sum(kept.reshape(heads, rows, full.shape[1]), axis=0)


def start_all(copies):
    for copy in copies:
        copy.start()


def order_of(positives, rows, depth):
    owner = positives // rows
    dp = owner // depth
    return ((dp // 2 * depth + owner % depth) * 2 + dp % 2) * rows + positives % rows


def attend_kernel(pack, lengths, rows, heads, chips, depth, qlen_ref, plen_ref, pos_ref, xq_hbm, xp_hbm, w_hbm, wo_hbm,
                  bias_ref, ob_ref, pack_mine, pack_other, early_mine, early_other, a_ref, p_ref, x_buf, w_buf, wo_buf, sems):
    i = lax.axis_index("dp")
    c, j = lax.rem(i, 2), i // 2
    width = wo_buf.shape[2]
    part = width // chips
    tokens = x_buf.shape[1]
    both = range(2)

    def weight_copy(e, k):
        return pltpu.make_async_copy(w_hbm.at[e, :, pl.ds(k * width, width)], w_buf.at[e, k], sems.at[e * 5 + 1 + k])

    copies = []
    for e in both:
        copies += [pltpu.make_async_copy(xq_hbm if e == 0 else xp_hbm, x_buf.at[e], sems.at[e * 5]), weight_copy(e, 0)]
    copies += [weight_copy(e, k) for k in (1, 2) for e in both]
    copies += [pltpu.make_async_copy(wo_hbm.at[e], wo_buf.at[e], sems.at[e * 5 + 4]) for e in both]
    ahead = 10
    start_all(copies[:ahead])

    def arrive(k):
        copies[k].wait()
        if k + ahead < len(copies):
            copies[k + ahead].start()

    mask = head_mask(rows, heads, width)
    pos = order_of(column([pos_ref[r] for r in range(rows)], rows), rows, depth)
    bounds = [row_bounds(pack if e else 0, plen_ref if e else qlen_ref, rows, lengths[e]) for e in both]
    start = [column([b[0] for b in bounds[e]], rows) for e in both]
    stop = [column([b[1] for b in bounds[e]], rows) for e in both]
    lane = lax.broadcasted_iota(jnp.int32, (rows, tokens), 1)
    pick = [jnp.where(lane == start[e], 1.0, 0.0).astype(BF) for e in both]
    x_cls, xc, q = [], [], []
    for e in both:
        arrive(2 * e)
        x_cls.append(mm(pick[e], x_buf[e]))
        xc.append(x_cls[e].astype(BF))
        arrive(2 * e + 1)
        q.append((mm(xc[e], w_buf[e, 0]) + bias_ref[e][0:1, :]).astype(BF))
    arrive(4)
    arrive(5)
    a_low = [mm(spread_heads(q[e], heads, mask), w_buf[e, 1], NT).astype(BF) for e in both]
    scores = [mm(a_low[e], x_buf[e], NT) * 0.125 for e in both]
    p_low, sums = [], []
    for e in both:
        a_ref[e] = a_low[e]
        lane_all = lax.broadcasted_iota(jnp.int32, scores[e].shape, 1)
        starts = jnp.concatenate([start[e]] * heads, axis=0)
        stops = jnp.concatenate([stop[e]] * heads, axis=0)
        allowed = jnp.where((lane_all >= starts) & (lane_all < stops), scores[e], MASKED)
        shifted = jnp.exp(allowed - jnp.max(allowed, axis=1, keepdims=True))
        p = shifted / jnp.sum(shifted, axis=1, keepdims=True)
        p_ref[e] = p
        p_low.append(p.astype(BF))
        sums.append(jnp.sum(p_low[e].astype(F32), axis=1, keepdims=True))
    pooled = [mm(p_low[e], x_buf[e]).astype(BF) for e in both]
    arrive(6)
    arrive(7)
    full = [mm(pooled[e], w_buf[e, 2]) + sums[e] * bias_ref[e][1:2, :] for e in both]
    ctx = [gather_heads(full[e], heads, rows, mask).astype(BF) for e in both]
    arrive(8)
    arrive(9)
    hidden = [x_cls[e] + mm(ctx[e], wo_buf[e]) + ob_ref[e:e + 1, :] for e in both]
    lanes = lax.broadcasted_iota(jnp.int32, (rows, EXTRA), 1)
    hat, extra = [], []
    for e in both:
        centred = hidden[e] - jnp.mean(hidden[e], axis=1, keepdims=True)
        rstd = lax.rsqrt(jnp.mean(centred * centred, axis=1, keepdims=True) + EPSILON)
        hat.append((centred * rstd).astype(BF))
        rstd_high = rstd.astype(BF).astype(F32)
        more = jnp.where(lanes == 0, rstd_high, 0.0)
        more = jnp.where(lanes == 1, rstd - rstd_high, more)
        more = jnp.where(lanes == 2, (pos // 32).astype(F32), more)
        more = jnp.where(lanes == 3, (pos % 32).astype(F32), more)
        for h in range(heads):
            more = jnp.where(lanes == 16 + h, sums[e][h * rows:(h + 1) * rows] - 1.0, more)
        extra.append(more.astype(BF))

    def put(e, pack_ref, early_ref):
        pack_ref[:, 0:width] = hat[e]
        pack_ref[:, width:] = extra[e]
        for chip in range(chips):
            slot = lax.rem(chip - j + chips, chips)
            cut = slice(chip * part, (chip + 1) * part)
            pieces = [pooled[e][h * rows:(h + 1) * rows, cut] for h in range(heads)] + [xc[e][:, cut], ctx[e][:, cut], q[e]]
            early_ref[slot] = jnp.concatenate(pieces, axis=1)

    @pl.when(c == 0)
    def even():
        put(0, pack_mine, early_mine)
        put(1, pack_other, early_other)

    @pl.when(c == 1)
    def odd():
        put(1, pack_mine, early_mine)
        put(0, pack_other, early_other)


def stage_kernel(ids, after_ref, win_hbm, wback_hbm, wout_hbm, xq_hbm, xp_hbm, w_hbm, win, wback, wout, x_buf, w_buf, sems):
    c = ids[0]
    width = wout.shape[0]
    copies = [pltpu.make_async_copy(win_hbm.at[c], win, sems.at[0]), pltpu.make_async_copy(wback_hbm.at[c], wback, sems.at[1]),
              pltpu.make_async_copy(wout_hbm.at[c], wout, sems.at[2]), pltpu.make_async_copy(xq_hbm, x_buf.at[0], sems.at[3]),
              pltpu.make_async_copy(xp_hbm, x_buf.at[1], sems.at[4])]
    for e in range(2):
        for k in range(3):
            copies.append(pltpu.make_async_copy(w_hbm.at[e, :, pl.ds(k * width, width)], w_buf.at[e, k], sems.at[5 + 3 * e + k]))
    start_all(copies)
    for copy in copies:
        copy.wait()


def gelu_parts(x):
    bell = jnp.exp(-0.5 * x * x)
    t = 1.0 / (1.0 + (0.3275911 * math.sqrt(0.5)) * jnp.abs(x))
    tail = 1.061405429 * 0.5
    for factor in (-1.453152027, 1.421413741, -0.284496736, 0.254829592):
        tail = tail * t + factor * 0.5
    tail = tail * t * bell
    cdf = jnp.where(x >= 0.0, 1.0 - tail, tail)
    return x * cdf, cdf + x * bell * (1.0 / math.sqrt(2.0 * math.pi))


def relative_places(chips, depth, rows, c, j, z):
    for kx in range(chips):
        for kz in range(depth):
            for kc in range(2):
                core = c if kc == 0 else 1 - c
                place = ((lax.rem(j - kx + chips, chips) * depth + lax.rem(z - kz + depth, depth)) * 2 + core) * rows
                yield kx, kz, kc, pl.multiple_of(place, rows)


def doubling(n, masks):
    found = [0]
    for mask in masks:
        found = found + [k ^ mask for k in found]
    assert sorted(found) == list(range(n))
    return found


def depth_masks(depth):
    return [(1 << k) - 1 for k in range(1, depth.bit_length())]


def chip_masks(chips):
    return [1 << k for k in range(chips.bit_length() - 1)]


def place_of(chip, deep, core, depth, rows):
    return pl.multiple_of(((chip * depth + deep) * 2 + core) * rows, rows)


def crossed_blocks(refs, chips, depth, rows, c, j, z, part, lead):
    near = depth // 2
    for at, dz in enumerate(doubling(depth, depth_masks(depth))):
        for kc in range(2):
            core = c if kc == 0 else 1 - c
            first = ((at % near) * 2 + kc) * rows
            for kx in range(chips):
                place = place_of(lax.rem(j - kx + chips, chips), jnp.bitwise_xor(z, dz), core, depth, rows)
                yield refs[at // near], first, lead + 2 * kx * part, place


def over_rows(count, tile, work):
    if tile == count:
        work(pl.ds(0, count))
    else:
        def one(t, carry):
            work(pl.ds(pl.multiple_of(t * tile, tile), tile))
            return carry

        lax.fori_loop(0, count // tile, one, 0)


def forward_kernel(chips, depth, rows, steps, tile, part, ids, *refs):
    blocks = refs[:chips]
    gain_ref, shift_ref, win_ref, inb_ref, wback_ref, backb_ref = refs[chips:chips + 6]
    _, act_ref, slope_ref, vec_ref, hat2_ref, ex_ref, cut_ref, hat1_ref, _, total, nl, chunk = refs[chips + 6:]
    c, j, z = ids[0], ids[1], ids[2]
    width = vec_ref.shape[1]
    step = pl.program_id(0)

    @pl.when(step == 0)
    def start():
        for kx, kz, kc, place in relative_places(chips, depth, rows, c, j, z):
            at = (kz * 2 + kc) * rows
            hat1_ref[pl.ds(place, rows), :] = blocks[kx][at:at + rows, 0:width]
            ex_ref[pl.ds(place, rows), :] = blocks[kx][at:at + rows, width:].astype(F32)
        gain = gain_ref[c]
        shift = shift_ref[c]
        normed = hat1_ref[...].astype(F32) * gain[0:1, :] + shift[0:1, :]
        low = normed.astype(BF)
        nl[...] = low
        total[...] = normed + backb_ref[pl.ds(c, 1), :]
        source = lax.broadcasted_iota(jnp.int32, (width, part), 0)
        target = lax.broadcasted_iota(jnp.int32, (width, part), 1) + j * part
        cut_ref[...] = mm(low, jnp.where(source == target, 1.0, 0.0).astype(BF)).astype(BF)

    columns = slope_ref.shape[1]
    at = pl.multiple_of(step * columns, columns)
    fpart = act_ref.shape[1]
    bias = inb_ref[pl.ds(c, 1), pl.ds(at, columns)]
    strips = 2
    strip = nl.shape[0] // strips
    spans = [slice(k * strip, (k + 1) * strip) for k in range(strips)]

    def up(span):
        return mm(nl[span, :], win_ref[:, pl.ds(at, columns)]) + bias

    def down(span, pre):
        active, slope = gelu_parts(pre)
        active = active.astype(BF)
        chunk[span, :] = active
        slope_ref[span, :] = slope.astype(BF)
        total[span, :] += mm(active, wback_ref[pl.ds(at, columns), :])

    pre = up(spans[0])
    for k in range(strips):
        following = up(spans[k + 1]) if k + 1 < strips else None
        down(spans[k], pre)
        pre = following
    for q in range(columns // fpart):
        @pl.when(step * (columns // fpart) + q == j)
        def keep():
            act_ref[...] = chunk[:, q * fpart:(q + 1) * fpart]

    @pl.when(step == steps - 1)
    def finish():
        gain = gain_ref[c]
        shift = shift_ref[c]

        def normalise(part):
            second = total[part, :]
            mean = jnp.mean(second, axis=1, keepdims=True)
            centred = second - mean
            rstd = lax.rsqrt(jnp.mean(centred * centred, axis=1, keepdims=True) + EPSILON)
            hat = centred * rstd
            hat2_ref[part, :] = hat.astype(BF)
            vec_ref[part, :] = (hat * gain[1:2, :] + shift[1:2, :]).astype(BF)
            ex = ex_ref[part, :]
            lanes = lax.broadcasted_iota(jnp.int32, ex.shape, 1)
            pos = ex[:, 2:3] * 32.0 + ex[:, 3:4]
            ex_ref[part, :] = jnp.where(
                lanes == 0, ex[:, 0:1] + ex[:, 1:2], jnp.where(lanes == 1, rstd, jnp.where(lanes == 2, pos, ex)))

        over_rows(total.shape[0], tile, normalise)


def norm_back(grad, hat, rstd, gain):
    scaled = grad * gain
    inner = jnp.mean(scaled * hat, axis=1, keepdims=True)
    return rstd * (scaled - jnp.mean(scaled, axis=1, keepdims=True) - hat * inner)


def loss_kernel(depth, rows, tile, ids, own_ref, other_ref, ex_ref, hat2_ref, hat1_ref, slope_ref, gain_ref,
                wback, win, wout, second_ref, loss_ref, mine_ref, sib_ref, small_ref, qvec_ref, pvec_ref,
                wide_loss):
    c, j, z = ids[0], ids[1], ids[2]
    count, width = own_ref.shape
    scale = 2.0 / math.sqrt(width)
    own_at = pl.multiple_of(((j * depth + z) * 2 + c) * rows, rows)

    def softmax_part(questions, passages, pos):
        scores = mm(questions, passages, NT) * scale
        peak = jnp.max(scores, axis=1, keepdims=True)
        shifted = jnp.exp(scores - peak)
        totals = jnp.sum(shifted, axis=1, keepdims=True)
        hit = lax.broadcasted_iota(jnp.int32, scores.shape, 1) == pos.astype(jnp.int32)
        loss = peak + jnp.log(totals) - jnp.sum(jnp.where(hit, scores, 0.0), axis=1, keepdims=True)
        grad = (shifted / totals - jnp.where(hit, 1.0, 0.0)) * scale
        high = grad.astype(BF)
        return loss, high, (grad - high.astype(F32)).astype(BF)

    @pl.when(c == 0)
    def question_side():
        qvec_ref[...] = own_ref[pl.ds(own_at, rows), :]
        pvec_ref[...] = other_ref[pl.ds(own_at, rows), :]

        def work(part):
            loss, high, low = softmax_part(own_ref[part, :], other_ref[...], ex_ref[part, 2:3])
            wide_loss[part, :] = jnp.broadcast_to(loss, (tile, wide_loss.shape[1]))
            second_ref[part, :] = mm(high, other_ref[...]) + mm(low, other_ref[...])

        over_rows(count, tile, work)

    @pl.when(c == 1)
    def passage_side():
        pvec_ref[...] = own_ref[pl.ds(own_at, rows), :]
        qvec_ref[...] = other_ref[pl.ds(own_at, rows), :]
        if tile < count:
            second_ref[...] = jnp.zeros_like(second_ref)

        def work(part):
            loss, high, low = softmax_part(other_ref[part, :], own_ref[...], ex_ref[part, 2:3])
            wide_loss[part, :] = jnp.broadcast_to(loss, (tile, wide_loss.shape[1]))
            piece = mm(high, other_ref[part, :], TN) + mm(low, other_ref[part, :], TN)
            second_ref[...] = piece if tile == count else second_ref[...] + piece

        over_rows(count, tile, work)

    small_ref[...] = jnp.zeros_like(small_ref)
    losses = wide_loss[pl.ds(own_at, rows), :]
    diagonal = lax.broadcasted_iota(jnp.int32, losses.shape, 0) == lax.broadcasted_iota(jnp.int32, losses.shape, 1)
    loss_ref[...] = jnp.sum(jnp.where(diagonal, losses, 0.0), axis=0, keepdims=True)[:, 0:rows]

    def late_norm(part):
        grad = second_ref[part, :]
        hat = hat2_ref[part, :].astype(F32)
        small_ref[1:2, :] += jnp.sum(grad * hat, axis=0, keepdims=True)
        small_ref[3:4, :] += jnp.sum(grad, axis=0, keepdims=True)
        second = norm_back(grad, hat, ex_ref[part, 1:2], gain_ref[c][1:2, :])
        small_ref[5:6, :] += jnp.sum(second, axis=0, keepdims=True)
        second_ref[part, :] = second

    over_rows(count, tile, late_norm)

    chip_at = pl.multiple_of((j * depth + z) * 2 * rows, 2 * rows)
    second = second_ref[pl.ds(chip_at, 2 * rows), :]
    pre = (mm(second.astype(BF), wback[...], NT) * slope_ref[...].astype(F32)).astype(BF)
    normed = second + mm(pre, win[...], NT)
    hidden = norm_back(normed, hat1_ref[...].astype(F32), ex_ref[pl.ds(chip_at, 2 * rows), 0:1], gain_ref[c][0:1, :])
    ctx = mm(hidden.astype(BF), wout[...], NT).astype(BF).astype(F32)
    both = jnp.concatenate([hidden, ctx], axis=1)
    is_low = c == 0
    mine_ref[...] = jnp.where(is_low, both[:rows], both[rows:])
    sib_ref[...] = jnp.where(is_low, both[rows:], both[:rows])


def split_halves(value, scratch, c, own_ref_set, sib_ref_set):
    half = value.shape[0] // 2
    scratch[...] = value
    own_ref_set(scratch[pl.ds(pl.multiple_of(c * half, half), half), :])
    sib_ref_set(scratch[pl.ds(pl.multiple_of((1 - c) * half, half), half), :].astype(BF))


def backward_kernel(chips, depth, rows, steps, tile, ids, near_ref, second_ref, ex_ref, hat1_ref, slope_ref, wback_ref, win_ref,
                    gain_ref, wout_ref, small_in, gpl_ref, low_ref, hidden_ref, plane_ref, small_ref, column_ref, acc, gfull):
    c, j, z = ids[0], ids[1], ids[2]
    count, width = second_ref.shape
    step = pl.program_id(0)

    @pl.when(step == 0)
    def start():
        acc[...] = second_ref[...]
        low_ref[...] = second_ref[...].astype(BF)
        column_ref[...] = near_ref[:, 0:width]
        small_ref[0:8, :] = small_in[...]
        small_ref[8:, :] = jnp.zeros((8, width), F32)

    columns = slope_ref.shape[1]
    at = pl.multiple_of(step * columns, columns)
    pre = mm(low_ref[...], wback_ref[pl.ds(at, columns), :], NT) * slope_ref[...].astype(F32)
    bias = jnp.sum(pre, axis=0, keepdims=True)
    pre_low = pre.astype(BF)
    gpl_ref[...] = pre_low
    acc[...] += mm(pre_low, win_ref[:, pl.ds(at, columns)], NT)
    for s in range(steps):
        @pl.when(step == s)
        def keep_bias():
            line, lane = 8 + s * columns // width, s * columns % width
            small_ref[line:line + 1, lane:lane + columns] = bias

    @pl.when(step == steps - 1)
    def finish():
        lanes = lax.broadcasted_iota(jnp.int32, (EXTRA, width), 0)
        heads_of = lax.broadcasted_iota(jnp.int32, (EXTRA, width), 1) // HEAD_DIM
        expand = jnp.where(lanes == heads_of + 16, 1.0, 0.0).astype(BF)

        def early_norm(part):
            grad = acc[part, :]
            hat = hat1_ref[part, :].astype(F32)
            small_ref[0:1, :] += jnp.sum(grad * hat, axis=0, keepdims=True)
            small_ref[2:3, :] += jnp.sum(grad, axis=0, keepdims=True)
            hidden = norm_back(grad, hat, ex_ref[part, 0:1], gain_ref[c][0:1, :])
            small_ref[4:5, :] += jnp.sum(hidden, axis=0, keepdims=True)
            hidden_low = hidden.astype(BF)
            hidden_ref[part, :] = hidden_low
            ctx = mm(hidden_low, wout_ref[...], NT).astype(BF)
            sums = mm(ex_ref[part, :].astype(BF), expand) + 1.0
            small_ref[6:7, :] += jnp.sum(sums * ctx.astype(F32), axis=0, keepdims=True)
            gfull[part, :] = ctx

        over_rows(count, tile, early_norm)
        for kx in range(chips):
            for kc in range(2):
                core = c if kc == 0 else 1 - c
                place = pl.multiple_of(((lax.rem(j - kx + chips, chips) * depth + z) * 2 + core) * rows, rows)
                at = (kx * 2 + kc) * rows
                plane_ref[at:at + rows, :] = gfull[pl.ds(place, rows), :]


def weight_kernel(chips, depth, rows, part, steps, ids, after_ref, near_ref, far_ref, gpl_ref, low_ref, hidden_ref, act_ref, cut_ref,
                  gin_ref, gback_ref, gout_ref, sib_ref, ctx_all, in_scr, back_scr, out_scr):
    c, j, z = ids[0], ids[1], ids[2]
    step = pl.program_id(0)
    width = low_ref.shape[1]
    half = part // 2
    ghalf = back_scr.shape[0] // 2
    columns = gpl_ref.shape[1]
    in_rows = half * (columns * steps // width)

    def set_own(ref):
        def setter(value):
            ref[0] = value
        return setter

    def set_sib(at, rows, lane, lanes):
        def setter(value):
            sib_ref[at:at + rows, lane:lane + lanes] = value
        return setter

    @pl.when(step == 0)
    def start():
        split_halves(mm(act_ref[...], low_ref[...], TN), back_scr, c, set_own(gback_ref), set_sib(in_rows, ghalf, 0, width))
        for ref, first, lane, place in crossed_blocks((near_ref, far_ref), chips, depth, rows, c, j, z, part, chips * part):
            ctx_all[pl.ds(place, rows), :] = ref[first:first + rows, lane + part:lane + 2 * part]
        split_halves(mm(ctx_all[...], hidden_ref[...], TN), out_scr, c, set_own(gout_ref), set_sib(in_rows + ghalf, half, 0, width))

    piece = mm(cut_ref[...], gpl_ref[...], TN)
    in_scr[...] = piece
    gin_ref[0] = in_scr[pl.ds(pl.multiple_of(c * half, half), half), :]
    other = in_scr[pl.ds(pl.multiple_of((1 - c) * half, half), half), :].astype(BF)
    for s in range(steps):
        @pl.when(step == s)
        def keep():
            set_sib((s * columns // width) * half, half, s * columns % width, columns)(other)


def attend_back_kernel(rows, heads, chips, ids, mine_ref, far_ref, x_buf, w_buf, bias_ref, p_ref, *refs):
    early = refs[:chips]
    late_mine, late_other, att_ref, b_ref, first_ref, cross_ref = refs[chips:]
    c, j = ids[0], ids[1]
    width = bias_ref.shape[2]
    part = width // chips
    cross_ref[...] = jnp.concatenate([b[:, heads * part:(heads + 2) * part] for b in early], axis=1)
    mask = head_mask(rows, heads, width)
    both = range(2)
    gg = [jnp.where(c == e, mine_ref[...], far_ref[...]) for e in both]
    blocks = [spread_heads(gg[e][:, width:], heads, mask) for e in both]
    constant = [jnp.sum(blocks[e] * bias_ref[e][1:2, :], axis=1, keepdims=True) for e in both]
    b_low = [mm(blocks[e].astype(BF), w_buf[e, 2], NT).astype(BF) for e in both]
    probs = [mm(b_low[e], x_buf[e], NT) + constant[e] for e in both]
    att = []
    for e in both:
        b_ref[e] = b_low[e]
        p = p_ref[e]
        att.append((p * (probs[e] - jnp.sum(probs[e] * p, axis=1, keepdims=True))).astype(BF))
        att_ref[e] = att[e]
    y_low = [mm(att[e], x_buf[e]).astype(BF) for e in both]
    gq_low = [(gather_heads(mm(y_low[e], w_buf[e, 1]), heads, rows, mask) * 0.125).astype(BF) for e in both]
    for e in both:
        first_ref[e] = gg[e][:, 0:width] + mm(gq_low[e], w_buf[e, 0], NT)

    def put(e, late_ref):
        for chip in range(chips):
            slot = lax.rem(chip - j + chips, chips)
            cut = slice(chip * part, (chip + 1) * part)
            pieces = [y_low[e][h * rows:(h + 1) * rows, cut] for h in range(heads)] + [gq_low[e]]
            late_ref[slot] = jnp.concatenate(pieces, axis=1)

    @pl.when(c == 0)
    def even():
        put(0, late_mine)
        put(1, late_other)

    @pl.when(c == 1)
    def odd():
        put(1, late_mine)
        put(0, late_other)


def token_grad_kernel(pack, lengths, rows, heads, ids, after_ref, qlen_ref, plen_ref, att_ref, p_ref, a_ref, b_ref, first_ref,
                      gq_ref, gp_ref):
    tile = gq_ref.shape[0]
    at = pl.program_id(0) * tile
    lane = lax.broadcasted_iota(jnp.int32, (rows, tile), 1) + at
    for e in range(2):
        bounds = row_bounds(pack if e else 0, plen_ref if e else qlen_ref, rows, lengths[e])
        pick = jnp.where(lane == column([b[0] for b in bounds], rows), 1.0, 0.0).astype(BF)
        first = first_ref[e]
        high = first.astype(BF)
        rest = first - high.astype(F32)
        middle = rest.astype(BF)
        last = (rest - middle.astype(F32)).astype(BF)
        left = jnp.concatenate([att_ref[e], p_ref[e].astype(BF), pick, pick, pick], axis=0)
        right = jnp.concatenate([a_ref[e] * jnp.asarray(0.125, BF), b_ref[e], high, middle, last], axis=0)
        out = gp_ref if e else gq_ref
        out[...] = mm(left, right, TN)


def head_sums(factor, vectors, heads, part):
    width = vectors.shape[1]
    full = mm(factor, vectors, TN)
    row_head = lax.broadcasted_iota(jnp.int32, full.shape, 0) // part
    col_head = lax.broadcasted_iota(jnp.int32, full.shape, 1) // HEAD_DIM
    kept = jnp.where(row_head == col_head, full, 0.0)
    return jnp.sum(kept.reshape(heads, part, width), axis=0)


def share_kernel(heads, chips, depth, part, ids, *refs):
    late = refs[:chips]
    early = refs[chips:2 * chips]
    plane_ref = refs[2 * chips]
    outs = refs[2 * chips + 2:2 * chips + 2 + depth]
    column_ref, scratch = refs[-2:]
    column_ref[...] = refs[2 * chips + 1][...]
    z = ids[2]
    width = plane_ref.shape[1]
    hp = heads * part
    y = jnp.concatenate([b[:, 0:hp] for b in late], axis=0)
    pooled = jnp.concatenate([b[:, 0:hp] for b in early], axis=0)
    q = jnp.concatenate([b[:, hp + 2 * part:] for b in early], axis=0)
    scratch[:, 0:width] = head_sums(y, q, heads, part) * 0.125
    scratch[:, width:] = head_sums(pooled, plane_ref[...], heads, part)
    span = 2 * width // depth
    for k in range(depth):
        at = pl.multiple_of(lax.rem(z + k, depth) * span, span)
        outs[k][...] = scratch[:, pl.ds(at, span)].astype(BF)


def query_kernel(chips, depth, rows, part, ids, sib_in, near_ref, far_ref, low_chips, high_chips, *refs):
    shares = refs[:depth]
    small_in, gw_ref, keep_ref, send_ref, small_ref, sib_out, x_all, gq_all, q_scr, share_scr = refs[depth:]
    c, j, z = ids[0], ids[1], ids[2]
    for ref, first, lane, place in crossed_blocks((near_ref, far_ref), chips, depth, rows, c, j, z, part, chips * part):
        x_all[pl.ds(place, rows), :] = ref[first:first + rows, lane:lane + part]
    few = chips // 2
    for at_chip, dx in enumerate(doubling(chips, chip_masks(chips))):
        for at_depth, dz in enumerate(doubling(depth, depth_masks(depth))):
            for kc in range(2):
                core = c if kc == 0 else 1 - c
                place = place_of(jnp.bitwise_xor(j, dx), jnp.bitwise_xor(z, dz), core, depth, rows)
                at = (((at_chip % few) * depth + at_depth) * 2 + kc) * rows
                gq_all[pl.ds(place, rows), :] = (low_chips, high_chips)[at_chip // few][at:at + rows, :]
    gq = gq_all[...]
    half = part // 2
    width = gq.shape[1]
    span = shares[0].shape[1]
    bias = jnp.sum(gq.astype(F32), axis=0, keepdims=True)
    small_ref[...] = small_in[...]
    small_ref[7:8, :] = bias
    total = shares[0][...].astype(F32)
    for k in range(1, depth):
        total = total + shares[k][...].astype(F32)
    share_scr[...] = total
    q_scr[...] = mm(x_all[...], gq, TN)
    own = pl.ds(pl.multiple_of(c * half, half), half)
    sib = pl.ds(pl.multiple_of((1 - c) * half, half), half)
    keep_ref[...] = share_scr[own, :].astype(BF)
    gw_ref[...] = q_scr[own, :]
    send_ref[:, 0:span] = share_scr[sib, :].astype(BF)
    send_ref[:, span:] = q_scr[sib, :].astype(BF)


def assemble_kernel(depth, ids, after_ref, *refs):
    shards = refs[:depth]
    own_ref, far_ref, out_ref = refs[depth:]
    c, z = ids[0], ids[2]
    half, width = own_ref.shape
    span = shards[0].shape[1]
    out_ref[c, :, 0:width] = own_ref[...]
    out_ref[1 - c, :, 0:width] = far_ref[:, span:].astype(F32)
    for k in range(depth):
        at = pl.multiple_of(width + lax.rem(z - k + depth, depth) * span, 128)
        out_ref[c, :, pl.ds(at, span)] = shards[k][0:half, :].astype(F32)
        out_ref[1 - c, :, pl.ds(at, span)] = shards[k][half:, :].astype(F32)


def fill_kernel(in_rows, ids, after_ref, in_hbm, back_hbm, out_hbm, sib_ref, own_ref, other_ref, gin_ref, gback_ref, gout_ref,
                qv_ref, outb_ref, gains_ref, shifts_ref, inb_ref, backb_ref):
    c = ids[0]
    half, width = gout_ref.shape[1], gout_ref.shape[2]
    ghalf = gback_ref.shape[1]
    for k in range(in_rows // half):
        gin_ref[0, :, k * width:(k + 1) * width] = sib_ref[k * half:(k + 1) * half, :].astype(F32)
    gback_ref[0] = sib_ref[in_rows:in_rows + ghalf, :].astype(F32)
    gout_ref[0] = sib_ref[in_rows + ghalf:, :].astype(F32)
    for e in range(2):
        small = jnp.where(c == e, own_ref[...], other_ref[...])
        gains_ref[e] = small[0:2]
        shifts_ref[e] = small[2:4]
        outb_ref[e:e + 1, :] = small[4:5]
        backb_ref[e:e + 1, :] = small[5:6]
        qv_ref[e, 0:1, :] = small[7:8]
        qv_ref[e, 1:2, :] = small[6:7]
        for k in range(inb_ref.shape[1] // width):
            inb_ref[e:e + 1, k * width:(k + 1) * width] = small[8 + k:9 + k]


def full_spec(shape):
    return pl.BlockSpec(tuple(shape), lambda *_: (0,) * len(shape))


def shape_of(shape, dtype):
    return jax.ShapeDtypeStruct(tuple(shape), dtype)


ANY = pl.BlockSpec(memory_space=pl.ANY)
SMEM = pl.BlockSpec(memory_space=pltpu.SMEM)


def kernel_call(name, kernel, ids, args, specs, outs, out_specs, scratch=(), grid=(1,), work=(0, 0), aliases=None, vmem=60):
    specs = [full_spec(a.shape) if s is None else s for a, s in zip(args, specs)]
    out_specs = [full_spec(o.shape) if s is None else s for o, s in zip(outs, out_specs)]
    return pl.pallas_call(
        kernel,
        grid_spec=pltpu.PrefetchScalarGridSpec(num_scalar_prefetch=1, grid=grid, in_specs=specs, out_specs=out_specs,
                                               scratch_shapes=list(scratch)),
        out_shape=list(outs),
        input_output_aliases=aliases or {},
        compiler_params=pltpu.CompilerParams(vmem_limit_bytes=vmem * 1024 * 1024),
        cost_estimate=pl.CostEstimate(flops=int(work[0]), bytes_accessed=int(work[1]), transcendentals=0),
        name=name,
    )(ids, *args)


def body(question_tokens, question_lengths, passage_tokens, passage_lengths, positives, w_qkv, qv_bias, w_out, out_bias,
         norm_gains, norm_biases, w_in, in_bias, w_back, back_bias, *, n_dp, depth):
    width = question_tokens.shape[2]
    heads = width // HEAD_DIM
    rows = question_tokens.shape[0]
    pack = passage_lengths.shape[1]
    lengths = (question_tokens.shape[1], passage_tokens.shape[1])
    tokens = rows * lengths[0]
    ff = w_in.shape[2]
    chips = n_dp // 2
    count = n_dp * depth * rows
    part = width // chips
    half = part // 2
    fpart = ff // chips
    hr = heads * rows
    i = lax.axis_index("dp")
    z = lax.axis_index("group")
    c, j = i % 2, i // 2
    ids = jnp.stack([c, j, z]).astype(jnp.int32)
    vm = pltpu.VMEM
    dma = pltpu.SemaphoreType.DMA

    def swap(x):
        return lax.ppermute(x, "dp", [(k, k ^ 1) for k in range(n_dp)])

    def to_chip(x, k):
        return lax.ppermute(x, "dp", [(s, ((s // 2 + k) % chips) * 2 + s % 2) for s in range(n_dp)])

    def to_depth(x, k):
        return lax.ppermute(x, "group", [(s, (s + k) % depth) for s in range(depth)])

    def over_depth(x):
        return [x] + [to_depth(x, k) for k in range(1, depth)]

    def over_plane(x):
        return [x] + [to_chip(x, k) for k in range(1, chips)]

    small_enough = count <= 1024
    kept = pl.BlockSpec(memory_space=pltpu.VMEM) if small_enough else None
    keep_shape = (lambda shape: pltpu.VMEM(shape, BF)) if small_enough else (lambda shape: shape_of(shape, BF))

    xq = question_tokens.reshape(tokens, width)
    xp = passage_tokens.reshape(tokens, width)

    wide = (heads + 2) * part + width
    pack_mine, pack_other, early_mine, early_other, a_low, probs = kernel_call(
        "attend", functools.partial(attend_kernel, pack, lengths, rows, heads, chips, depth), question_lengths,
        [passage_lengths, positives, xq, xp, w_qkv, w_out, qv_bias, out_bias],
        [SMEM, SMEM, ANY, ANY, ANY, ANY, None, None],
        [shape_of((rows, width + EXTRA), BF)] * 2 + [shape_of((chips, rows, wide), BF)] * 2 + [
            shape_of((2, hr, width), BF), shape_of((2, hr, tokens), F32)],
        [None] * 6,
        [vm((2, tokens, width), BF), vm((2, 3, width, width), BF), vm((2, width, width), BF), dma((10,))],
        vmem=60 if count <= 1024 else 60, work=(6e9, 13e6))

    pair = jnp.concatenate([pack_mine, swap(pack_other)], axis=0)
    column_rows = jnp.concatenate(over_depth(pair), axis=0)
    plane = over_plane(column_rows)
    win_kept, wback_kept, wout_kept, x_kept, w_kept = kernel_call(
        "stage", stage_kernel, ids, [column_rows, w_in, w_back, w_out, xq, xp, w_qkv], [ANY] * 7,
        [keep_shape((width, ff)), keep_shape((ff, width)), keep_shape((width, width)), keep_shape((2, tokens, width)),
         keep_shape((2, 3, width, width))], [kept] * 5, [dma((11,))],
        vmem=24 if count <= 1024 else 60, work=(5e9, 10e6))

    fc = max(fpart, 384)
    steps = ff // fc
    tile = count if count <= 1024 else 128
    row = lambda w: full_spec((count, w))
    act, slope, vec, hat2, ex, cut, hat1, early_other = kernel_call(
        "forward", functools.partial(forward_kernel, chips, depth, rows, steps, tile, part), ids,
        plane + [norm_gains, norm_biases, win_kept, in_bias, wback_kept, back_bias, early_other],
        [None] * chips + [None, None, kept, None, kept, None, ANY],
        [shape_of((count, fpart), BF), shape_of((count, ff), BF), shape_of((count, width), BF),
         shape_of((count, width), BF), shape_of((count, EXTRA), F32), shape_of((count, part), BF), shape_of((count, width), BF),
         shape_of(early_other.shape, BF)],
        [None, pl.BlockSpec((count, fc), lambda s, ids: (0, s)), None, None, None, None, None, ANY],
        [vm((count, width), F32), vm((count, width), BF), vm((count, fc), BF)], grid=(steps,), vmem=24 if count <= 1024 else 60, work=(10e9, 18e6),
        aliases={1 + chips + 6: 7})

    vec_other = swap(vec)
    hp = heads * part

    early_far = swap(early_other)
    payload = [jnp.concatenate([early_mine[k], early_far[k]], axis=0) for k in range(chips)]
    early = [payload[0]] + [to_chip(payload[k], k) for k in range(1, chips)]

    chip_block = lambda w: pl.BlockSpec((2 * rows, w), lambda s, ids: (ids[1] * depth + ids[2], 0))
    second, loss, gg_mine, gg_sib, small, q_vectors, p_vectors = kernel_call(
        "loss", functools.partial(loss_kernel, depth, rows, tile), ids,
        [vec, vec_other, ex, hat2, hat1, slope, norm_gains, wback_kept, win_kept, wout_kept],
        [None, None, None, None, chip_block(width), chip_block(ff), None, kept, kept, kept],
        [shape_of((count, width), F32), shape_of((1, rows), F32), shape_of((rows, 2 * width), F32),
         shape_of((rows, 2 * width), F32), shape_of((8, width), F32), shape_of((rows, width), BF), shape_of((rows, width), BF)],
        [None] * 7,
        [vm((count, EXTRA), F32)],
        vmem=24 if count <= 1024 else 60, work=(8e9, 16e6))

    late_mine, late_other, att, b_low, first_rows, crossed = kernel_call(
        "attend_back", functools.partial(attend_back_kernel, rows, heads, chips), ids,
        [gg_mine, swap(gg_sib), x_kept, w_kept, qv_bias, probs] + early,
        [None, None, kept, kept, None, None] + [None] * chips,
        [shape_of((chips, rows, hp + width), BF)] * 2 + [
            shape_of((2, hr, tokens), BF), shape_of((2, hr, width), BF), shape_of((2, rows, width), F32),
            shape_of((2 * rows, 2 * width), BF)],
        [None] * 6,
        vmem=24 if count <= 1024 else 60, work=(6e9, 16e6))

    late_far = swap(late_other)
    payload = [jnp.concatenate([late_mine[k], late_far[k]], axis=0) for k in range(chips)]
    late = [payload[0]] + [to_chip(payload[k], k) for k in range(1, chips)]

    def xor_depth(x, mask):
        return lax.ppermute(x, "group", [(s, s ^ mask) for s in range(depth)])

    def xor_chip(x, mask):
        return lax.ppermute(x, "dp", [(s, s ^ (2 * mask)) for s in range(n_dp)])

    def double(x, step, masks):
        for mask in masks:
            x = jnp.concatenate([x, step(x, mask)], axis=0)
        return x

    near = double(jnp.concatenate([payload[0][:, hp:], crossed], axis=1), xor_depth, depth_masks(depth)[:-1])
    far_z = xor_depth(near, depth_masks(depth)[-1])
    gpl, low, hidden_low, g_plane, small, gq_near = kernel_call(
        "backward", functools.partial(backward_kernel, chips, depth, rows, steps, tile), ids,
        [near, second, ex, hat1, slope, wback_kept, win_kept, norm_gains, wout_kept, small],
        [None, None, None, None, pl.BlockSpec((count, fc), lambda s, ids: (0, s)),
         kept, kept, None, kept, None],
        [shape_of((count, ff), BF), shape_of((count, width), BF), shape_of((count, width), BF),
         shape_of((chips * 2 * rows, width), BF), shape_of((16, width), F32), shape_of((near.shape[0], width), BF)],
        [pl.BlockSpec((count, fc), lambda s, ids: (0, s)), None, None, None, None, None],
        [vm((count, width), F32), vm((count, width), BF)], grid=(steps,), vmem=30 if count <= 1024 else 60, work=(12e9, 18e6))

    gq_column = jnp.concatenate([gq_near, far_z[:, 0:width]], axis=0)

    span = 2 * width // depth
    *shares, gq_first = kernel_call(
        "share", functools.partial(share_kernel, heads, chips, depth, part), ids,
        late + early + [g_plane, gq_column], [None] * (2 * chips + 2),
        [shape_of((part, span), BF)] * depth + [shape_of(gq_column.shape, BF)], [None] * (depth + 1),
        [vm((part, 2 * width), F32)], vmem=28 if count <= 1024 else 60, work=(1e9, 3e6))
    masks = chip_masks(chips)
    gq_low = jnp.concatenate([gq_first, xor_chip(gq_column, masks[0])], axis=0)
    gq_low = double(gq_low, xor_chip, masks[1:-1])
    gq_high = xor_chip(gq_low, masks[-1])
    shares = [shares[0]] + [to_depth(shares[k], k) for k in range(1, depth)]

    ghalf = fpart // 2
    out_block = lambda r, w: pl.BlockSpec((1, r, w), lambda s, ids: (ids[0], 0, 0))
    in_rows = half * ff // width
    gin, gback, gout, sib = kernel_call(
        "weight", functools.partial(weight_kernel, chips, depth, rows, part, steps), ids,
        [shares[0], near, far_z, gpl, low, hidden_low, act, cut],
        [ANY, None, None, pl.BlockSpec((count, fc), lambda s, ids: (0, s)), None, None,
         None, None],
        [shape_of((2, half, ff), F32), shape_of((2, ghalf, width), F32), shape_of((2, half, width), F32),
         shape_of((in_rows + ghalf + half, width), BF)],
        [pl.BlockSpec((1, half, fc), lambda s, ids: (ids[0], 0, s)), out_block(ghalf, width), out_block(half, width), None],
        [vm((count, part), BF), vm((part, fc), F32), vm((fpart, width), F32), vm((part, width), F32)],
        grid=(steps,), vmem=28 if count <= 1024 else 60, work=(4e9, 12e6))
    gw_q, keep, send, small, sib = kernel_call(
        "query", functools.partial(query_kernel, chips, depth, rows, part), ids,
        [sib, near, far_z, gq_low, gq_high] + shares + [small], [ANY] + [None] * (depth + 5),
        [shape_of((half, width), F32), shape_of((half, span), BF), shape_of((half, span + width), BF), shape_of((16, width), F32),
         shape_of(sib.shape, BF)],
        [None] * 4 + [ANY],
        [vm((count, part), BF), vm((count, width), BF), vm((part, width), F32), vm((part, span), F32)], vmem=20 if count <= 1024 else 60, aliases={1: 4}, work=(1e9, 3e6))
    sib_far = swap(sib)
    far = swap(send)
    shards = over_depth(jnp.concatenate([keep, far[:, 0:span]], axis=0))
    gx = kernel_call(
        "token_grad", functools.partial(token_grad_kernel, pack, lengths, rows, heads), ids,
        [far, question_lengths, passage_lengths, att, probs, a_low, b_low, first_rows],
        [ANY, SMEM, SMEM, pl.BlockSpec((2, hr, 256), lambda s, ids: (0, 0, s)),
         pl.BlockSpec((2, hr, 256), lambda s, ids: (0, 0, s)), None, None, None],
        [shape_of((tokens, width), F32)] * 2, [pl.BlockSpec((256, width), lambda s, ids: (s, 0))] * 2,
        grid=(tokens // 256,), vmem=24 if count <= 1024 else 60, work=(2e9, 9e6))

    gin, gback, gout, g_qv, g_outb, g_gains, g_shifts, g_inb, g_backb = kernel_call(
        "fill", functools.partial(fill_kernel, in_rows), ids, [gx[0], gin, gback, gout, sib_far, small, swap(small)],
        [ANY, ANY, ANY, ANY, None, None, None],
        [shape_of(gin.shape, F32), shape_of(gback.shape, F32), shape_of(gout.shape, F32), shape_of((2, 2, width), F32),
         shape_of((2, width), F32), shape_of((2, 2, width), F32), shape_of((2, 2, width), F32), shape_of((2, ff), F32),
         shape_of((2, width), F32)],
        [pl.BlockSpec((1,) + a.shape[1:], lambda s, ids: (1 - ids[0], 0, 0)) for a in (gin, gback, gout)] + [None] * 6,
        aliases={2: 0, 3: 1, 4: 2}, vmem=20 if count <= 1024 else 60, work=(1e6, 8e6))

    (g_qkv,) = kernel_call(
        "assemble", functools.partial(assemble_kernel, depth), ids, [gout] + shards + [gw_q, far], [ANY] + [None] * (depth + 2),
        [shape_of((2, half, 3 * width), F32)], [None], vmem=20 if count <= 1024 else 60, work=(1e6, 3e6))

    return (
        q_vectors,
        p_vectors,
        loss.reshape(rows),
        gx[0].reshape(question_tokens.shape),
        gx[1].reshape(passage_tokens.shape),
        g_qkv,
        g_qv,
        gout,
        g_outb,
        g_gains,
        g_shifts,
        gin,
        g_inb,
        gback,
        g_backb,
    )


def solution(mesh):
    split = P(("dp", "group"))
    return jax.shard_map(
        functools.partial(body, n_dp=mesh.shape["dp"], depth=mesh.shape["group"]),
        mesh=mesh,
        in_specs=(split, split, split, split, split) + (P(),) * 10,
        out_specs=(split, split, split, split, split, P(None, "dp", None), P(), P(None, "dp", None), P(), P(), P(),
                   P(None, "dp", None), P(), P(None, "dp", None), P()),
        check_vma=False,
    )
```

```python
import functools
import math

import jax
import jax.numpy as jnp
from jax import lax
from jax.experimental import pallas as pl
from jax.experimental.pallas import tpu as pltpu
from jax.sharding import PartitionSpec as P

HEAD_DIM = 64
EPSILON = 1e-12
MASKED = -1000000000.0
EXTRA = 128
BF = jnp.bfloat16
F32 = jnp.float32

NT = (((1,), (1,)), ((), ()))
TN = (((0,), (0,)), ((), ()))
NN = (((1,), (0,)), ((), ()))


def mm(left, right, dims=NN):
    return lax.dot_general(left, right, dims, preferred_element_type=F32)


def row_bounds(packed, len_ref, rows, length):
    bounds = []
    for r in range(rows):
        if packed:
            row, k = r // packed, r % packed
            start = row * length
            for earlier in range(k):
                start = start + len_ref[row, earlier]
            bounds.append((start, start + len_ref[row, k]))
        else:
            bounds.append((r * length, r * length + len_ref[r]))
    return bounds


def column(values, rows):
    at = lax.broadcasted_iota(jnp.int32, (rows, 1), 0)
    result = jnp.zeros((rows, 1), jnp.int32)
    for r, value in enumerate(values):
        result = jnp.where(at == r, value, result)
    return result


def head_mask(rows, heads, width):
    row_head = lax.broadcasted_iota(jnp.int32, (rows * heads, width), 0) // rows
    col_head = lax.broadcasted_iota(jnp.int32, (rows * heads, width), 1) // HEAD_DIM
    return row_head == col_head


def spread_heads(values, heads, mask):
    tiled = jnp.concatenate([values] * heads, axis=0)
    return jnp.where(mask, tiled, jnp.zeros_like(tiled))


def gather_heads(full, heads, rows, mask):
    kept = jnp.where(mask, full, jnp.zeros_like(full))
    return jnp.sum(kept.reshape(heads, rows, full.shape[1]), axis=0)


def start_all(copies):
    for copy in copies:
        copy.start()


def order_of(positives, rows, depth):
    owner = positives // rows
    dp = owner // depth
    return ((dp // 2 * depth + owner % depth) * 2 + dp % 2) * rows + positives % rows


def attend_kernel(pack, lengths, rows, heads, chips, depth, qlen_ref, plen_ref, pos_ref, xq_hbm, xp_hbm, w_hbm, wo_hbm,
                  bias_ref, ob_ref, pack_mine, pack_other, early_mine, early_other, a_ref, p_ref, x_buf, w_buf, wo_buf, sems):
    i = lax.axis_index("dp")
    c, j = lax.rem(i, 2), i // 2
    width = wo_buf.shape[2]
    part = width // chips
    tokens = x_buf.shape[1]
    both = range(2)

    def weight_copy(e, k):
        return pltpu.make_async_copy(w_hbm.at[e, :, pl.ds(k * width, width)], w_buf.at[e, k], sems.at[e * 5 + 1 + k])

    copies = []
    for e in both:
        copies += [pltpu.make_async_copy(xq_hbm if e == 0 else xp_hbm, x_buf.at[e], sems.at[e * 5]), weight_copy(e, 0)]
    copies += [weight_copy(e, k) for k in (1, 2) for e in both]
    copies += [pltpu.make_async_copy(wo_hbm.at[e], wo_buf.at[e], sems.at[e * 5 + 4]) for e in both]
    ahead = 10
    start_all(copies[:ahead])

    def arrive(k):
        copies[k].wait()
        if k + ahead < len(copies):
            copies[k + ahead].start()

    mask = head_mask(rows, heads, width)
    pos = order_of(column([pos_ref[r] for r in range(rows)], rows), rows, depth)
    bounds = [row_bounds(pack if e else 0, plen_ref if e else qlen_ref, rows, lengths[e]) for e in both]
    start = [column([b[0] for b in bounds[e]], rows) for e in both]
    stop = [column([b[1] for b in bounds[e]], rows) for e in both]
    lane = lax.broadcasted_iota(jnp.int32, (rows, tokens), 1)
    pick = [jnp.where(lane == start[e], 1.0, 0.0).astype(BF) for e in both]
    x_cls, xc, q = [], [], []
    for e in both:
        arrive(2 * e)
        x_cls.append(mm(pick[e], x_buf[e]))
        xc.append(x_cls[e].astype(BF))
        arrive(2 * e + 1)
        q.append((mm(xc[e], w_buf[e, 0]) + bias_ref[e][0:1, :]).astype(BF))
    arrive(4)
    arrive(5)
    a_low = [mm(spread_heads(q[e], heads, mask), w_buf[e, 1], NT).astype(BF) for e in both]
    scores = [mm(a_low[e], x_buf[e], NT) * 0.125 for e in both]
    p_low, sums = [], []
    for e in both:
        a_ref[e] = a_low[e]
        lane_all = lax.broadcasted_iota(jnp.int32, scores[e].shape, 1)
        starts = jnp.concatenate([start[e]] * heads, axis=0)
        stops = jnp.concatenate([stop[e]] * heads, axis=0)
        allowed = jnp.where((lane_all >= starts) & (lane_all < stops), scores[e], MASKED)
        shifted = jnp.exp(allowed - jnp.max(allowed, axis=1, keepdims=True))
        p = shifted / jnp.sum(shifted, axis=1, keepdims=True)
        p_ref[e] = p
        p_low.append(p.astype(BF))
        sums.append(jnp.sum(p_low[e].astype(F32), axis=1, keepdims=True))
    pooled = [mm(p_low[e], x_buf[e]).astype(BF) for e in both]
    arrive(6)
    arrive(7)
    full = [mm(pooled[e], w_buf[e, 2]) + sums[e] * bias_ref[e][1:2, :] for e in both]
    ctx = [gather_heads(full[e], heads, rows, mask).astype(BF) for e in both]
    arrive(8)
    arrive(9)
    hidden = [x_cls[e] + mm(ctx[e], wo_buf[e]) + ob_ref[e:e + 1, :] for e in both]
    lanes = lax.broadcasted_iota(jnp.int32, (rows, EXTRA), 1)
    hat, extra = [], []
    for e in both:
        centred = hidden[e] - jnp.mean(hidden[e], axis=1, keepdims=True)
        rstd = lax.rsqrt(jnp.mean(centred * centred, axis=1, keepdims=True) + EPSILON)
        hat.append((centred * rstd).astype(BF))
        rstd_high = rstd.astype(BF).astype(F32)
        more = jnp.where(lanes == 0, rstd_high, 0.0)
        more = jnp.where(lanes == 1, rstd - rstd_high, more)
        more = jnp.where(lanes == 2, (pos // 32).astype(F32), more)
        more = jnp.where(lanes == 3, (pos % 32).astype(F32), more)
        for h in range(heads):
            more = jnp.where(lanes == 16 + h, sums[e][h * rows:(h + 1) * rows] - 1.0, more)
        extra.append(more.astype(BF))

    def put(e, pack_ref, early_ref):
        pack_ref[:, 0:width] = hat[e]
        pack_ref[:, width:] = extra[e]
        for chip in range(chips):
            slot = lax.rem(chip - j + chips, chips)
            cut = slice(chip * part, (chip + 1) * part)
            pieces = [pooled[e][h * rows:(h + 1) * rows, cut] for h in range(heads)] + [xc[e][:, cut], ctx[e][:, cut], q[e]]
            early_ref[slot] = jnp.concatenate(pieces, axis=1)

    @pl.when(c == 0)
    def even():
        put(0, pack_mine, early_mine)
        put(1, pack_other, early_other)

    @pl.when(c == 1)
    def odd():
        put(1, pack_mine, early_mine)
        put(0, pack_other, early_other)


def stage_kernel(ids, after_ref, win_hbm, wback_hbm, wout_hbm, xq_hbm, xp_hbm, w_hbm, win, wback, wout, x_buf, w_buf, sems):
    c = ids[0]
    width = wout.shape[0]
    copies = [pltpu.make_async_copy(win_hbm.at[c], win, sems.at[0]), pltpu.make_async_copy(wback_hbm.at[c], wback, sems.at[1]),
              pltpu.make_async_copy(wout_hbm.at[c], wout, sems.at[2]), pltpu.make_async_copy(xq_hbm, x_buf.at[0], sems.at[3]),
              pltpu.make_async_copy(xp_hbm, x_buf.at[1], sems.at[4])]
    for e in range(2):
        for k in range(3):
            copies.append(pltpu.make_async_copy(w_hbm.at[e, :, pl.ds(k * width, width)], w_buf.at[e, k], sems.at[5 + 3 * e + k]))
    start_all(copies)
    for copy in copies:
        copy.wait()


def gelu_parts(x):
    bell = jnp.exp(-0.5 * x * x)
    t = 1.0 / (1.0 + (0.3275911 * math.sqrt(0.5)) * jnp.abs(x))
    tail = 1.061405429 * 0.5
    for factor in (-1.453152027, 1.421413741, -0.284496736, 0.254829592):
        tail = tail * t + factor * 0.5
    tail = tail * t * bell
    cdf = jnp.where(x >= 0.0, 1.0 - tail, tail)
    return x * cdf, cdf + x * bell * (1.0 / math.sqrt(2.0 * math.pi))


def relative_places(chips, depth, rows, c, j, z):
    for kx in range(chips):
        for kz in range(depth):
            for kc in range(2):
                core = c if kc == 0 else 1 - c
                place = ((lax.rem(j - kx + chips, chips) * depth + lax.rem(z - kz + depth, depth)) * 2 + core) * rows
                yield kx, kz, kc, pl.multiple_of(place, rows)


def doubling(n, masks):
    found = [0]
    for mask in masks:
        found = found + [k ^ mask for k in found]
    assert sorted(found) == list(range(n))
    return found


def depth_masks(depth):
    return [(1 << k) - 1 for k in range(1, depth.bit_length())]


def chip_masks(chips):
    return [1 << k for k in range(chips.bit_length() - 1)]


def place_of(chip, deep, core, depth, rows):
    return pl.multiple_of(((chip * depth + deep) * 2 + core) * rows, rows)


def crossed_blocks(refs, chips, depth, rows, c, j, z, part, lead):
    near = depth // 2
    for at, dz in enumerate(doubling(depth, depth_masks(depth))):
        for kc in range(2):
            core = c if kc == 0 else 1 - c
            first = ((at % near) * 2 + kc) * rows
            for kx in range(chips):
                place = place_of(lax.rem(j - kx + chips, chips), jnp.bitwise_xor(z, dz), core, depth, rows)
                yield refs[at // near], first, lead + 2 * kx * part, place


def over_rows(count, tile, work):
    if tile == count:
        work(pl.ds(0, count))
    else:
        def one(t, carry):
            work(pl.ds(pl.multiple_of(t * tile, tile), tile))
            return carry

        lax.fori_loop(0, count // tile, one, 0)


def forward_kernel(chips, depth, rows, steps, tile, part, ids, *refs):
    blocks = refs[:chips]
    gain_ref, shift_ref, win_ref, inb_ref, wback_ref, backb_ref = refs[chips:chips + 6]
    _, act_ref, slope_ref, vec_ref, hat2_ref, ex_ref, cut_ref, hat1_ref, _, total, nl, chunk = refs[chips + 6:]
    c, j, z = ids[0], ids[1], ids[2]
    width = vec_ref.shape[1]
    step = pl.program_id(0)

    @pl.when(step == 0)
    def start():
        for kx, kz, kc, place in relative_places(chips, depth, rows, c, j, z):
            at = (kz * 2 + kc) * rows
            hat1_ref[pl.ds(place, rows), :] = blocks[kx][at:at + rows, 0:width]
            ex_ref[pl.ds(place, rows), :] = blocks[kx][at:at + rows, width:].astype(F32)
        gain = gain_ref[c]
        shift = shift_ref[c]
        normed = hat1_ref[...].astype(F32) * gain[0:1, :] + shift[0:1, :]
        low = normed.astype(BF)
        nl[...] = low
        total[...] = normed + backb_ref[pl.ds(c, 1), :]
        source = lax.broadcasted_iota(jnp.int32, (width, part), 0)
        target = lax.broadcasted_iota(jnp.int32, (width, part), 1) + j * part
        cut_ref[...] = mm(low, jnp.where(source == target, 1.0, 0.0).astype(BF)).astype(BF)

    columns = slope_ref.shape[1]
    at = pl.multiple_of(step * columns, columns)
    fpart = act_ref.shape[1]
    bias = inb_ref[pl.ds(c, 1), pl.ds(at, columns)]
    strips = 2
    strip = nl.shape[0] // strips
    spans = [slice(k * strip, (k + 1) * strip) for k in range(strips)]

    def up(span):
        return mm(nl[span, :], win_ref[:, pl.ds(at, columns)]) + bias

    def down(span, pre):
        active, slope = gelu_parts(pre)
        active = active.astype(BF)
        chunk[span, :] = active
        slope_ref[span, :] = slope.astype(BF)
        total[span, :] += mm(active, wback_ref[pl.ds(at, columns), :])

    pre = up(spans[0])
    for k in range(strips):
        following = up(spans[k + 1]) if k + 1 < strips else None
        down(spans[k], pre)
        pre = following
    for q in range(columns // fpart):
        @pl.when(step * (columns // fpart) + q == j)
        def keep():
            act_ref[...] = chunk[:, q * fpart:(q + 1) * fpart]

    @pl.when(step == steps - 1)
    def finish():
        gain = gain_ref[c]
        shift = shift_ref[c]

        def normalise(part):
            second = total[part, :]
            mean = jnp.mean(second, axis=1, keepdims=True)
            centred = second - mean
            rstd = lax.rsqrt(jnp.mean(centred * centred, axis=1, keepdims=True) + EPSILON)
            hat = centred * rstd
            hat2_ref[part, :] = hat.astype(BF)
            vec_ref[part, :] = (hat * gain[1:2, :] + shift[1:2, :]).astype(BF)
            ex = ex_ref[part, :]
            lanes = lax.broadcasted_iota(jnp.int32, ex.shape, 1)
            pos = ex[:, 2:3] * 32.0 + ex[:, 3:4]
            ex_ref[part, :] = jnp.where(
                lanes == 0, ex[:, 0:1] + ex[:, 1:2], jnp.where(lanes == 1, rstd, jnp.where(lanes == 2, pos, ex)))

        over_rows(total.shape[0], tile, normalise)


def norm_back(grad, hat, rstd, gain):
    scaled = grad * gain
    inner = jnp.mean(scaled * hat, axis=1, keepdims=True)
    return rstd * (scaled - jnp.mean(scaled, axis=1, keepdims=True) - hat * inner)


def loss_kernel(depth, rows, tile, ids, own_ref, other_ref, ex_ref, hat2_ref, hat1_ref, slope_ref, gain_ref,
                wback, win, wout, second_ref, loss_ref, mine_ref, sib_ref, small_ref, qvec_ref, pvec_ref,
                wide_loss):
    c, j, z = ids[0], ids[1], ids[2]
    count, width = own_ref.shape
    scale = 2.0 / math.sqrt(width)
    own_at = pl.multiple_of(((j * depth + z) * 2 + c) * rows, rows)

    def softmax_part(questions, passages, pos):
        scores = mm(questions, passages, NT) * scale
        peak = jnp.max(scores, axis=1, keepdims=True)
        shifted = jnp.exp(scores - peak)
        totals = jnp.sum(shifted, axis=1, keepdims=True)
        hit = lax.broadcasted_iota(jnp.int32, scores.shape, 1) == pos.astype(jnp.int32)
        loss = peak + jnp.log(totals) - jnp.sum(jnp.where(hit, scores, 0.0), axis=1, keepdims=True)
        grad = (shifted / totals - jnp.where(hit, 1.0, 0.0)) * scale
        high = grad.astype(BF)
        return loss, high, (grad - high.astype(F32)).astype(BF)

    @pl.when(c == 0)
    def question_side():
        qvec_ref[...] = own_ref[pl.ds(own_at, rows), :]
        pvec_ref[...] = other_ref[pl.ds(own_at, rows), :]

        def work(part):
            loss, high, low = softmax_part(own_ref[part, :], other_ref[...], ex_ref[part, 2:3])
            wide_loss[part, :] = jnp.broadcast_to(loss, (tile, wide_loss.shape[1]))
            second_ref[part, :] = mm(high, other_ref[...]) + mm(low, other_ref[...])

        over_rows(count, tile, work)

    @pl.when(c == 1)
    def passage_side():
        pvec_ref[...] = own_ref[pl.ds(own_at, rows), :]
        qvec_ref[...] = other_ref[pl.ds(own_at, rows), :]
        if tile < count:
            second_ref[...] = jnp.zeros_like(second_ref)

        def work(part):
            loss, high, low = softmax_part(other_ref[part, :], own_ref[...], ex_ref[part, 2:3])
            wide_loss[part, :] = jnp.broadcast_to(loss, (tile, wide_loss.shape[1]))
            piece = mm(high, other_ref[part, :], TN) + mm(low, other_ref[part, :], TN)
            second_ref[...] = piece if tile == count else second_ref[...] + piece

        over_rows(count, tile, work)

    small_ref[...] = jnp.zeros_like(small_ref)
    losses = wide_loss[pl.ds(own_at, rows), :]
    diagonal = lax.broadcasted_iota(jnp.int32, losses.shape, 0) == lax.broadcasted_iota(jnp.int32, losses.shape, 1)
    loss_ref[...] = jnp.sum(jnp.where(diagonal, losses, 0.0), axis=0, keepdims=True)[:, 0:rows]

    def late_norm(part):
        grad = second_ref[part, :]
        hat = hat2_ref[part, :].astype(F32)
        small_ref[1:2, :] += jnp.sum(grad * hat, axis=0, keepdims=True)
        small_ref[3:4, :] += jnp.sum(grad, axis=0, keepdims=True)
        second = norm_back(grad, hat, ex_ref[part, 1:2], gain_ref[c][1:2, :])
        small_ref[5:6, :] += jnp.sum(second, axis=0, keepdims=True)
        second_ref[part, :] = second

    over_rows(count, tile, late_norm)

    chip_at = pl.multiple_of((j * depth + z) * 2 * rows, 2 * rows)
    second = second_ref[pl.ds(chip_at, 2 * rows), :]
    pre = (mm(second.astype(BF), wback[...], NT) * slope_ref[...].astype(F32)).astype(BF)
    normed = second + mm(pre, win[...], NT)
    hidden = norm_back(normed, hat1_ref[...].astype(F32), ex_ref[pl.ds(chip_at, 2 * rows), 0:1], gain_ref[c][0:1, :])
    ctx = mm(hidden.astype(BF), wout[...], NT).astype(BF).astype(F32)
    both = jnp.concatenate([hidden, ctx], axis=1)
    is_low = c == 0
    mine_ref[...] = jnp.where(is_low, both[:rows], both[rows:])
    sib_ref[...] = jnp.where(is_low, both[rows:], both[:rows])


def split_halves(value, scratch, c, own_ref_set, sib_ref_set):
    half = value.shape[0] // 2
    scratch[...] = value
    own_ref_set(scratch[pl.ds(pl.multiple_of(c * half, half), half), :])
    sib_ref_set(scratch[pl.ds(pl.multiple_of((1 - c) * half, half), half), :].astype(BF))


def backward_kernel(chips, depth, rows, steps, tile, ids, near_ref, second_ref, ex_ref, hat1_ref, slope_ref, wback_ref, win_ref,
                    gain_ref, wout_ref, small_in, gpl_ref, low_ref, hidden_ref, plane_ref, small_ref, column_ref, acc, gfull):
    c, j, z = ids[0], ids[1], ids[2]
    count, width = second_ref.shape
    step = pl.program_id(0)

    @pl.when(step == 0)
    def start():
        acc[...] = second_ref[...]
        low_ref[...] = second_ref[...].astype(BF)
        column_ref[...] = near_ref[:, 0:width]
        small_ref[0:8, :] = small_in[...]
        small_ref[8:, :] = jnp.zeros((8, width), F32)

    columns = slope_ref.shape[1]
    at = pl.multiple_of(step * columns, columns)
    strip = count // 2
    bias = jnp.zeros((1, columns), F32)
    spans = [slice(k * strip, (k + 1) * strip) for k in range(2)]
    rising = [mm(low_ref[span, :], wback_ref[pl.ds(at, columns), :], NT) for span in spans]
    for span, grown in zip(spans, rising):
        pre = grown * slope_ref[span, :].astype(F32)
        bias = bias + jnp.sum(pre, axis=0, keepdims=True)
        pre_low = pre.astype(BF)
        gpl_ref[span, :] = pre_low
        acc[span, :] += mm(pre_low, win_ref[:, pl.ds(at, columns)], NT)
    for s in range(steps):
        @pl.when(step == s)
        def keep_bias():
            line, lane = 8 + s * columns // width, s * columns % width
            small_ref[line:line + 1, lane:lane + columns] = bias

    @pl.when(step == steps - 1)
    def finish():
        lanes = lax.broadcasted_iota(jnp.int32, (EXTRA, width), 0)
        heads_of = lax.broadcasted_iota(jnp.int32, (EXTRA, width), 1) // HEAD_DIM
        expand = jnp.where(lanes == heads_of + 16, 1.0, 0.0).astype(BF)

        def early_norm(part):
            grad = acc[part, :]
            hat = hat1_ref[part, :].astype(F32)
            small_ref[0:1, :] += jnp.sum(grad * hat, axis=0, keepdims=True)
            small_ref[2:3, :] += jnp.sum(grad, axis=0, keepdims=True)
            hidden = norm_back(grad, hat, ex_ref[part, 0:1], gain_ref[c][0:1, :])
            small_ref[4:5, :] += jnp.sum(hidden, axis=0, keepdims=True)
            hidden_low = hidden.astype(BF)
            hidden_ref[part, :] = hidden_low
            ctx = mm(hidden_low, wout_ref[...], NT).astype(BF)
            sums = mm(ex_ref[part, :].astype(BF), expand) + 1.0
            small_ref[6:7, :] += jnp.sum(sums * ctx.astype(F32), axis=0, keepdims=True)
            gfull[part, :] = ctx

        over_rows(count, tile, early_norm)
        for kx in range(chips):
            for kc in range(2):
                core = c if kc == 0 else 1 - c
                place = pl.multiple_of(((lax.rem(j - kx + chips, chips) * depth + z) * 2 + core) * rows, rows)
                at = (kx * 2 + kc) * rows
                plane_ref[at:at + rows, :] = gfull[pl.ds(place, rows), :]


def weight_kernel(chips, depth, rows, part, steps, ids, after_ref, near_ref, far_ref, gpl_ref, low_ref, hidden_ref, act_ref, cut_ref,
                  gin_ref, gback_ref, gout_ref, sib_ref, ctx_all, in_scr, back_scr, out_scr):
    c, j, z = ids[0], ids[1], ids[2]
    step = pl.program_id(0)
    width = low_ref.shape[1]
    half = part // 2
    ghalf = back_scr.shape[0] // 2
    columns = gpl_ref.shape[1]
    in_rows = half * (columns * steps // width)

    def set_own(ref):
        def setter(value):
            ref[0] = value
        return setter

    def set_sib(at, rows, lane, lanes):
        def setter(value):
            sib_ref[at:at + rows, lane:lane + lanes] = value
        return setter

    @pl.when(step == 0)
    def start():
        split_halves(mm(act_ref[...], low_ref[...], TN), back_scr, c, set_own(gback_ref), set_sib(in_rows, ghalf, 0, width))
        for ref, first, lane, place in crossed_blocks((near_ref, far_ref), chips, depth, rows, c, j, z, part, chips * part):
            ctx_all[pl.ds(place, rows), :] = ref[first:first + rows, lane + part:lane + 2 * part]
        split_halves(mm(ctx_all[...], hidden_ref[...], TN), out_scr, c, set_own(gout_ref), set_sib(in_rows + ghalf, half, 0, width))

    piece = mm(cut_ref[...], gpl_ref[...], TN)
    in_scr[...] = piece
    gin_ref[0] = in_scr[pl.ds(pl.multiple_of(c * half, half), half), :]
    other = in_scr[pl.ds(pl.multiple_of((1 - c) * half, half), half), :].astype(BF)
    for s in range(steps):
        @pl.when(step == s)
        def keep():
            set_sib((s * columns // width) * half, half, s * columns % width, columns)(other)


def attend_back_kernel(rows, heads, chips, ids, mine_ref, far_ref, x_buf, w_buf, bias_ref, p_ref, *refs):
    early = refs[:chips]
    late_mine, late_other, att_ref, b_ref, first_ref, cross_ref = refs[chips:]
    c, j = ids[0], ids[1]
    width = bias_ref.shape[2]
    part = width // chips
    cross_ref[...] = jnp.concatenate([b[:, heads * part:(heads + 2) * part] for b in early], axis=1)
    mask = head_mask(rows, heads, width)
    both = range(2)
    gg = [jnp.where(c == e, mine_ref[...], far_ref[...]) for e in both]
    blocks = [spread_heads(gg[e][:, width:], heads, mask) for e in both]
    constant = [jnp.sum(blocks[e] * bias_ref[e][1:2, :], axis=1, keepdims=True) for e in both]
    b_low = [mm(blocks[e].astype(BF), w_buf[e, 2], NT).astype(BF) for e in both]
    probs = [mm(b_low[e], x_buf[e], NT) + constant[e] for e in both]
    att = []
    for e in both:
        b_ref[e] = b_low[e]
        p = p_ref[e]
        att.append((p * (probs[e] - jnp.sum(probs[e] * p, axis=1, keepdims=True))).astype(BF))
        att_ref[e] = att[e]
    y_low = [mm(att[e], x_buf[e]).astype(BF) for e in both]
    gq_low = [(gather_heads(mm(y_low[e], w_buf[e, 1]), heads, rows, mask) * 0.125).astype(BF) for e in both]
    for e in both:
        first_ref[e] = gg[e][:, 0:width] + mm(gq_low[e], w_buf[e, 0], NT)

    def put(e, late_ref):
        for chip in range(chips):
            slot = lax.rem(chip - j + chips, chips)
            cut = slice(chip * part, (chip + 1) * part)
            pieces = [y_low[e][h * rows:(h + 1) * rows, cut] for h in range(heads)] + [gq_low[e]]
            late_ref[slot] = jnp.concatenate(pieces, axis=1)

    @pl.when(c == 0)
    def even():
        put(0, late_mine)
        put(1, late_other)

    @pl.when(c == 1)
    def odd():
        put(1, late_mine)
        put(0, late_other)


def token_grad_kernel(pack, lengths, rows, heads, ids, after_ref, qlen_ref, plen_ref, att_ref, p_ref, a_ref, b_ref, first_ref,
                      gq_ref, gp_ref):
    tile = gq_ref.shape[0]
    at = pl.program_id(0) * tile
    lane = lax.broadcasted_iota(jnp.int32, (rows, tile), 1) + at
    for e in range(2):
        bounds = row_bounds(pack if e else 0, plen_ref if e else qlen_ref, rows, lengths[e])
        pick = jnp.where(lane == column([b[0] for b in bounds], rows), 1.0, 0.0).astype(BF)
        first = first_ref[e]
        high = first.astype(BF)
        rest = first - high.astype(F32)
        middle = rest.astype(BF)
        last = (rest - middle.astype(F32)).astype(BF)
        left = jnp.concatenate([att_ref[e], p_ref[e].astype(BF), pick, pick, pick], axis=0)
        right = jnp.concatenate([a_ref[e] * jnp.asarray(0.125, BF), b_ref[e], high, middle, last], axis=0)
        out = gp_ref if e else gq_ref
        out[...] = mm(left, right, TN)


def head_sums(factor, vectors, heads, part):
    width = vectors.shape[1]
    full = mm(factor, vectors, TN)
    row_head = lax.broadcasted_iota(jnp.int32, full.shape, 0) // part
    col_head = lax.broadcasted_iota(jnp.int32, full.shape, 1) // HEAD_DIM
    kept = jnp.where(row_head == col_head, full, 0.0)
    return jnp.sum(kept.reshape(heads, part, width), axis=0)


def share_kernel(heads, chips, depth, part, ids, *refs):
    late = refs[:chips]
    early = refs[chips:2 * chips]
    plane_ref = refs[2 * chips]
    outs = refs[2 * chips + 2:2 * chips + 2 + depth]
    column_ref, scratch = refs[-2:]
    column_ref[...] = refs[2 * chips + 1][...]
    z = ids[2]
    width = plane_ref.shape[1]
    hp = heads * part
    y = jnp.concatenate([b[:, 0:hp] for b in late], axis=0)
    pooled = jnp.concatenate([b[:, 0:hp] for b in early], axis=0)
    q = jnp.concatenate([b[:, hp + 2 * part:] for b in early], axis=0)
    scratch[:, 0:width] = head_sums(y, q, heads, part) * 0.125
    scratch[:, width:] = head_sums(pooled, plane_ref[...], heads, part)
    span = 2 * width // depth
    for k in range(depth):
        at = pl.multiple_of(lax.rem(z + k, depth) * span, span)
        outs[k][...] = scratch[:, pl.ds(at, span)].astype(BF)


def query_kernel(chips, depth, rows, part, ids, sib_in, near_ref, far_ref, low_chips, high_chips, *refs):
    shares = refs[:depth]
    small_in, gw_ref, keep_ref, send_ref, small_ref, sib_out, x_all, gq_all, q_scr, share_scr = refs[depth:]
    c, j, z = ids[0], ids[1], ids[2]
    for ref, first, lane, place in crossed_blocks((near_ref, far_ref), chips, depth, rows, c, j, z, part, chips * part):
        x_all[pl.ds(place, rows), :] = ref[first:first + rows, lane:lane + part]
    few = chips // 2
    for at_chip, dx in enumerate(doubling(chips, chip_masks(chips))):
        for at_depth, dz in enumerate(doubling(depth, depth_masks(depth))):
            for kc in range(2):
                core = c if kc == 0 else 1 - c
                place = place_of(jnp.bitwise_xor(j, dx), jnp.bitwise_xor(z, dz), core, depth, rows)
                at = (((at_chip % few) * depth + at_depth) * 2 + kc) * rows
                gq_all[pl.ds(place, rows), :] = (low_chips, high_chips)[at_chip // few][at:at + rows, :]
    gq = gq_all[...]
    half = part // 2
    width = gq.shape[1]
    span = shares[0].shape[1]
    bias = jnp.sum(gq.astype(F32), axis=0, keepdims=True)
    small_ref[...] = small_in[...]
    small_ref[7:8, :] = bias
    total = shares[0][...].astype(F32)
    for k in range(1, depth):
        total = total + shares[k][...].astype(F32)
    share_scr[...] = total
    q_scr[...] = mm(x_all[...], gq, TN)
    own = pl.ds(pl.multiple_of(c * half, half), half)
    sib = pl.ds(pl.multiple_of((1 - c) * half, half), half)
    keep_ref[...] = share_scr[own, :].astype(BF)
    gw_ref[...] = q_scr[own, :]
    send_ref[:, 0:span] = share_scr[sib, :].astype(BF)
    send_ref[:, span:] = q_scr[sib, :].astype(BF)


def assemble_kernel(depth, ids, after_ref, *refs):
    shards = refs[:depth]
    own_ref, far_ref, out_ref = refs[depth:]
    c, z = ids[0], ids[2]
    half, width = own_ref.shape
    span = shards[0].shape[1]
    out_ref[c, :, 0:width] = own_ref[...]
    out_ref[1 - c, :, 0:width] = far_ref[:, span:].astype(F32)
    for k in range(depth):
        at = pl.multiple_of(width + lax.rem(z - k + depth, depth) * span, 128)
        out_ref[c, :, pl.ds(at, span)] = shards[k][0:half, :].astype(F32)
        out_ref[1 - c, :, pl.ds(at, span)] = shards[k][half:, :].astype(F32)


def fill_kernel(in_rows, ids, after_ref, in_hbm, back_hbm, out_hbm, sib_ref, own_ref, other_ref, gin_ref, gback_ref, gout_ref,
                qv_ref, outb_ref, gains_ref, shifts_ref, inb_ref, backb_ref):
    c = ids[0]
    half, width = gout_ref.shape[1], gout_ref.shape[2]
    ghalf = gback_ref.shape[1]
    for k in range(in_rows // half):
        gin_ref[0, :, k * width:(k + 1) * width] = sib_ref[k * half:(k + 1) * half, :].astype(F32)
    gback_ref[0] = sib_ref[in_rows:in_rows + ghalf, :].astype(F32)
    gout_ref[0] = sib_ref[in_rows + ghalf:, :].astype(F32)
    for e in range(2):
        small = jnp.where(c == e, own_ref[...], other_ref[...])
        gains_ref[e] = small[0:2]
        shifts_ref[e] = small[2:4]
        outb_ref[e:e + 1, :] = small[4:5]
        backb_ref[e:e + 1, :] = small[5:6]
        qv_ref[e, 0:1, :] = small[7:8]
        qv_ref[e, 1:2, :] = small[6:7]
        for k in range(inb_ref.shape[1] // width):
            inb_ref[e:e + 1, k * width:(k + 1) * width] = small[8 + k:9 + k]


def full_spec(shape):
    return pl.BlockSpec(tuple(shape), lambda *_: (0,) * len(shape))


def shape_of(shape, dtype):
    return jax.ShapeDtypeStruct(tuple(shape), dtype)


ANY = pl.BlockSpec(memory_space=pl.ANY)
SMEM = pl.BlockSpec(memory_space=pltpu.SMEM)


def kernel_call(name, kernel, ids, args, specs, outs, out_specs, scratch=(), grid=(1,), work=(0, 0), aliases=None, vmem=60):
    specs = [full_spec(a.shape) if s is None else s for a, s in zip(args, specs)]
    out_specs = [full_spec(o.shape) if s is None else s for o, s in zip(outs, out_specs)]
    return pl.pallas_call(
        kernel,
        grid_spec=pltpu.PrefetchScalarGridSpec(num_scalar_prefetch=1, grid=grid, in_specs=specs, out_specs=out_specs,
                                               scratch_shapes=list(scratch)),
        out_shape=list(outs),
        input_output_aliases=aliases or {},
        compiler_params=pltpu.CompilerParams(vmem_limit_bytes=vmem * 1024 * 1024),
        cost_estimate=pl.CostEstimate(flops=int(work[0]), bytes_accessed=int(work[1]), transcendentals=0),
        name=name,
    )(ids, *args)


def body(question_tokens, question_lengths, passage_tokens, passage_lengths, positives, w_qkv, qv_bias, w_out, out_bias,
         norm_gains, norm_biases, w_in, in_bias, w_back, back_bias, *, n_dp, depth):
    width = question_tokens.shape[2]
    heads = width // HEAD_DIM
    rows = question_tokens.shape[0]
    pack = passage_lengths.shape[1]
    lengths = (question_tokens.shape[1], passage_tokens.shape[1])
    tokens = rows * lengths[0]
    ff = w_in.shape[2]
    chips = n_dp // 2
    count = n_dp * depth * rows
    part = width // chips
    half = part // 2
    fpart = ff // chips
    hr = heads * rows
    i = lax.axis_index("dp")
    z = lax.axis_index("group")
    c, j = i % 2, i // 2
    ids = jnp.stack([c, j, z]).astype(jnp.int32)
    vm = pltpu.VMEM
    dma = pltpu.SemaphoreType.DMA

    def swap(x):
        return lax.ppermute(x, "dp", [(k, k ^ 1) for k in range(n_dp)])

    def to_chip(x, k):
        return lax.ppermute(x, "dp", [(s, ((s // 2 + k) % chips) * 2 + s % 2) for s in range(n_dp)])

    def to_depth(x, k):
        return lax.ppermute(x, "group", [(s, (s + k) % depth) for s in range(depth)])

    def over_depth(x):
        return [x] + [to_depth(x, k) for k in range(1, depth)]

    def over_plane(x):
        return [x] + [to_chip(x, k) for k in range(1, chips)]

    small_enough = count <= 1024
    kept = pl.BlockSpec(memory_space=pltpu.VMEM) if small_enough else None
    keep_shape = (lambda shape: pltpu.VMEM(shape, BF)) if small_enough else (lambda shape: shape_of(shape, BF))

    xq = question_tokens.reshape(tokens, width)
    xp = passage_tokens.reshape(tokens, width)

    wide = (heads + 2) * part + width
    pack_mine, pack_other, early_mine, early_other, a_low, probs = kernel_call(
        "attend", functools.partial(attend_kernel, pack, lengths, rows, heads, chips, depth), question_lengths,
        [passage_lengths, positives, xq, xp, w_qkv, w_out, qv_bias, out_bias],
        [SMEM, SMEM, ANY, ANY, ANY, ANY, None, None],
        [shape_of((rows, width + EXTRA), BF)] * 2 + [shape_of((chips, rows, wide), BF)] * 2 + [
            shape_of((2, hr, width), BF), shape_of((2, hr, tokens), F32)],
        [None] * 6,
        [vm((2, tokens, width), BF), vm((2, 3, width, width), BF), vm((2, width, width), BF), dma((10,))],
        vmem=60 if count <= 1024 else 60, work=(6e9, 13e6))

    pair = jnp.concatenate([pack_mine, swap(pack_other)], axis=0)
    column_rows = jnp.concatenate(over_depth(pair), axis=0)
    plane = over_plane(column_rows)
    win_kept, wback_kept, wout_kept, x_kept, w_kept = kernel_call(
        "stage", stage_kernel, ids, [column_rows, w_in, w_back, w_out, xq, xp, w_qkv], [ANY] * 7,
        [keep_shape((width, ff)), keep_shape((ff, width)), keep_shape((width, width)), keep_shape((2, tokens, width)),
         keep_shape((2, 3, width, width))], [kept] * 5, [dma((11,))],
        vmem=24 if count <= 1024 else 60, work=(5e9, 10e6))

    fc = max(fpart, 384)
    steps = ff // fc
    tile = count if count <= 1024 else 128
    row = lambda w: full_spec((count, w))
    act, slope, vec, hat2, ex, cut, hat1, early_other = kernel_call(
        "forward", functools.partial(forward_kernel, chips, depth, rows, steps, tile, part), ids,
        plane + [norm_gains, norm_biases, win_kept, in_bias, wback_kept, back_bias, early_other],
        [None] * chips + [None, None, kept, None, kept, None, ANY],
        [shape_of((count, fpart), BF), shape_of((count, ff), BF), shape_of((count, width), BF),
         shape_of((count, width), BF), shape_of((count, EXTRA), F32), shape_of((count, part), BF), shape_of((count, width), BF),
         shape_of(early_other.shape, BF)],
        [None, pl.BlockSpec((count, fc), lambda s, ids: (0, s)), None, None, None, None, None, ANY],
        [vm((count, width), F32), vm((count, width), BF), vm((count, fc), BF)], grid=(steps,), vmem=24 if count <= 1024 else 60, work=(10e9, 18e6),
        aliases={1 + chips + 6: 7})

    vec_other = swap(vec)
    hp = heads * part

    early_far = swap(early_other)
    payload = [jnp.concatenate([early_mine[k], early_far[k]], axis=0) for k in range(chips)]
    early = [payload[0]] + [to_chip(payload[k], k) for k in range(1, chips)]

    chip_block = lambda w: pl.BlockSpec((2 * rows, w), lambda s, ids: (ids[1] * depth + ids[2], 0))
    second, loss, gg_mine, gg_sib, small, q_vectors, p_vectors = kernel_call(
        "loss", functools.partial(loss_kernel, depth, rows, tile), ids,
        [vec, vec_other, ex, hat2, hat1, slope, norm_gains, wback_kept, win_kept, wout_kept],
        [None, None, None, None, chip_block(width), chip_block(ff), None, kept, kept, kept],
        [shape_of((count, width), F32), shape_of((1, rows), F32), shape_of((rows, 2 * width), F32),
         shape_of((rows, 2 * width), F32), shape_of((8, width), F32), shape_of((rows, width), BF), shape_of((rows, width), BF)],
        [None] * 7,
        [vm((count, EXTRA), F32)],
        vmem=24 if count <= 1024 else 60, work=(8e9, 16e6))

    late_mine, late_other, att, b_low, first_rows, crossed = kernel_call(
        "attend_back", functools.partial(attend_back_kernel, rows, heads, chips), ids,
        [gg_mine, swap(gg_sib), x_kept, w_kept, qv_bias, probs] + early,
        [None, None, kept, kept, None, None] + [None] * chips,
        [shape_of((chips, rows, hp + width), BF)] * 2 + [
            shape_of((2, hr, tokens), BF), shape_of((2, hr, width), BF), shape_of((2, rows, width), F32),
            shape_of((2 * rows, 2 * width), BF)],
        [None] * 6,
        vmem=24 if count <= 1024 else 60, work=(6e9, 16e6))

    late_far = swap(late_other)
    payload = [jnp.concatenate([late_mine[k], late_far[k]], axis=0) for k in range(chips)]
    late = [payload[0]] + [to_chip(payload[k], k) for k in range(1, chips)]

    def xor_depth(x, mask):
        return lax.ppermute(x, "group", [(s, s ^ mask) for s in range(depth)])

    def xor_chip(x, mask):
        return lax.ppermute(x, "dp", [(s, s ^ (2 * mask)) for s in range(n_dp)])

    def double(x, step, masks):
        for mask in masks:
            x = jnp.concatenate([x, step(x, mask)], axis=0)
        return x

    near = double(jnp.concatenate([payload[0][:, hp:], crossed], axis=1), xor_depth, depth_masks(depth)[:-1])
    far_z = xor_depth(near, depth_masks(depth)[-1])
    gpl, low, hidden_low, g_plane, small, gq_near = kernel_call(
        "backward", functools.partial(backward_kernel, chips, depth, rows, steps, tile), ids,
        [near, second, ex, hat1, slope, wback_kept, win_kept, norm_gains, wout_kept, small],
        [None, None, None, None, pl.BlockSpec((count, fc), lambda s, ids: (0, s)),
         kept, kept, None, kept, None],
        [shape_of((count, ff), BF), shape_of((count, width), BF), shape_of((count, width), BF),
         shape_of((chips * 2 * rows, width), BF), shape_of((16, width), F32), shape_of((near.shape[0], width), BF)],
        [pl.BlockSpec((count, fc), lambda s, ids: (0, s)), None, None, None, None, None],
        [vm((count, width), F32), vm((count, width), BF)], grid=(steps,), vmem=26 if count <= 1024 else 60, work=(12e9, 18e6))

    gq_column = jnp.concatenate([gq_near, far_z[:, 0:width]], axis=0)

    span = 2 * width // depth
    *shares, gq_first = kernel_call(
        "share", functools.partial(share_kernel, heads, chips, depth, part), ids,
        late + early + [g_plane, gq_column], [None] * (2 * chips + 2),
        [shape_of((part, span), BF)] * depth + [shape_of(gq_column.shape, BF)], [None] * (depth + 1),
        [vm((part, 2 * width), F32)], vmem=24 if count <= 1024 else 60, work=(1e9, 3e6))
    masks = chip_masks(chips)
    gq_low = jnp.concatenate([gq_first, xor_chip(gq_column, masks[0])], axis=0)
    gq_low = double(gq_low, xor_chip, masks[1:-1])
    gq_high = xor_chip(gq_low, masks[-1])
    shares = [shares[0]] + [to_depth(shares[k], k) for k in range(1, depth)]

    ghalf = fpart // 2
    out_block = lambda r, w: pl.BlockSpec((1, r, w), lambda s, ids: (ids[0], 0, 0))
    in_rows = half * ff // width
    gin, gback, gout, sib = kernel_call(
        "weight", functools.partial(weight_kernel, chips, depth, rows, part, steps), ids,
        [shares[0], near, far_z, gpl, low, hidden_low, act, cut],
        [ANY, None, None, pl.BlockSpec((count, fc), lambda s, ids: (0, s)), None, None,
         None, None],
        [shape_of((2, half, ff), F32), shape_of((2, ghalf, width), F32), shape_of((2, half, width), F32),
         shape_of((in_rows + ghalf + half, width), BF)],
        [pl.BlockSpec((1, half, fc), lambda s, ids: (ids[0], 0, s)), out_block(ghalf, width), out_block(half, width), None],
        [vm((count, part), BF), vm((part, fc), F32), vm((fpart, width), F32), vm((part, width), F32)],
        grid=(steps,), vmem=24 if count <= 1024 else 60, work=(4e9, 12e6))
    gw_q, keep, send, small, sib = kernel_call(
        "query", functools.partial(query_kernel, chips, depth, rows, part), ids,
        [sib, near, far_z, gq_low, gq_high] + shares + [small], [ANY] + [None] * (depth + 5),
        [shape_of((half, width), F32), shape_of((half, span), BF), shape_of((half, span + width), BF), shape_of((16, width), F32),
         shape_of(sib.shape, BF)],
        [None] * 4 + [ANY],
        [vm((count, part), BF), vm((count, width), BF), vm((part, width), F32), vm((part, span), F32)], vmem=20 if count <= 1024 else 60, aliases={1: 4}, work=(1e9, 3e6))
    sib_far = swap(sib)
    far = swap(send)
    shards = over_depth(jnp.concatenate([keep, far[:, 0:span]], axis=0))
    gx = kernel_call(
        "token_grad", functools.partial(token_grad_kernel, pack, lengths, rows, heads), ids,
        [far, question_lengths, passage_lengths, att, probs, a_low, b_low, first_rows],
        [ANY, SMEM, SMEM, pl.BlockSpec((2, hr, 256), lambda s, ids: (0, 0, s)),
         pl.BlockSpec((2, hr, 256), lambda s, ids: (0, 0, s)), None, None, None],
        [shape_of((tokens, width), F32)] * 2, [pl.BlockSpec((256, width), lambda s, ids: (s, 0))] * 2,
        grid=(tokens // 256,), vmem=24 if count <= 1024 else 60, work=(2e9, 9e6))

    gin, gback, gout, g_qv, g_outb, g_gains, g_shifts, g_inb, g_backb = kernel_call(
        "fill", functools.partial(fill_kernel, in_rows), ids, [gx[0], gin, gback, gout, sib_far, small, swap(small)],
        [ANY, ANY, ANY, ANY, None, None, None],
        [shape_of(gin.shape, F32), shape_of(gback.shape, F32), shape_of(gout.shape, F32), shape_of((2, 2, width), F32),
         shape_of((2, width), F32), shape_of((2, 2, width), F32), shape_of((2, 2, width), F32), shape_of((2, ff), F32),
         shape_of((2, width), F32)],
        [pl.BlockSpec((1,) + a.shape[1:], lambda s, ids: (1 - ids[0], 0, 0)) for a in (gin, gback, gout)] + [None] * 6,
        aliases={2: 0, 3: 1, 4: 2}, vmem=20 if count <= 1024 else 60, work=(1e6, 8e6))

    (g_qkv,) = kernel_call(
        "assemble", functools.partial(assemble_kernel, depth), ids, [gout] + shards + [gw_q, far], [ANY] + [None] * (depth + 2),
        [shape_of((2, half, 3 * width), F32)], [None], vmem=20 if count <= 1024 else 60, work=(1e6, 3e6))

    return (
        q_vectors,
        p_vectors,
        loss.reshape(rows),
        gx[0].reshape(question_tokens.shape),
        gx[1].reshape(passage_tokens.shape),
        g_qkv,
        g_qv,
        gout,
        g_outb,
        g_gains,
        g_shifts,
        gin,
        g_inb,
        gback,
        g_backb,
    )


def solution(mesh):
    split = P(("dp", "group"))
    return jax.shard_map(
        functools.partial(body, n_dp=mesh.shape["dp"], depth=mesh.shape["group"]),
        mesh=mesh,
        in_specs=(split, split, split, split, split) + (P(),) * 10,
        out_specs=(split, split, split, split, split, P(None, "dp", None), P(), P(None, "dp", None), P(), P(), P(),
                   P(None, "dp", None), P(), P(None, "dp", None), P()),
        check_vma=False,
    )
```

```python
import functools
import math

import jax
import jax.numpy as jnp
from jax import lax
from jax.experimental import pallas as pl
from jax.experimental.pallas import tpu as pltpu
from jax.sharding import PartitionSpec as P

HEAD_DIM = 64
EPSILON = 1e-12
MASKED = -1000000000.0
EXTRA = 128
BF = jnp.bfloat16
F32 = jnp.float32

NT = (((1,), (1,)), ((), ()))
TN = (((0,), (0,)), ((), ()))
NN = (((1,), (0,)), ((), ()))


def mm(left, right, dims=NN):
    return lax.dot_general(left, right, dims, preferred_element_type=F32)


def row_bounds(packed, len_ref, rows, length):
    bounds = []
    for r in range(rows):
        if packed:
            row, k = r // packed, r % packed
            start = row * length
            for earlier in range(k):
                start = start + len_ref[row, earlier]
            bounds.append((start, start + len_ref[row, k]))
        else:
            bounds.append((r * length, r * length + len_ref[r]))
    return bounds


def column(values, rows):
    at = lax.broadcasted_iota(jnp.int32, (rows, 1), 0)
    result = jnp.zeros((rows, 1), jnp.int32)
    for r, value in enumerate(values):
        result = jnp.where(at == r, value, result)
    return result


def head_mask(rows, heads, width):
    row_head = lax.broadcasted_iota(jnp.int32, (rows * heads, width), 0) // rows
    col_head = lax.broadcasted_iota(jnp.int32, (rows * heads, width), 1) // HEAD_DIM
    return row_head == col_head


def spread_heads(values, heads, mask):
    tiled = jnp.concatenate([values] * heads, axis=0)
    return jnp.where(mask, tiled, jnp.zeros_like(tiled))


def gather_heads(full, heads, rows, mask):
    kept = jnp.where(mask, full, jnp.zeros_like(full))
    return jnp.sum(kept.reshape(heads, rows, full.shape[1]), axis=0)


def start_all(copies):
    for copy in copies:
        copy.start()


def order_of(positives, rows, depth):
    owner = positives // rows
    dp = owner // depth
    return ((dp // 2 * depth + owner % depth) * 2 + dp % 2) * rows + positives % rows


def attend_kernel(pack, lengths, rows, heads, chips, depth, qlen_ref, plen_ref, pos_ref, xq_hbm, xp_hbm, w_hbm, wo_hbm,
                  bias_ref, ob_ref, pack_mine, pack_other, early_mine, early_other, a_ref, p_ref, x_buf, w_buf, wo_buf, sems):
    i = lax.axis_index("dp")
    c, j = lax.rem(i, 2), i // 2
    width = wo_buf.shape[2]
    part = width // chips
    tokens = x_buf.shape[1]
    both = range(2)

    def weight_copy(e, k):
        return pltpu.make_async_copy(w_hbm.at[e, :, pl.ds(k * width, width)], w_buf.at[e, k], sems.at[e * 5 + 1 + k])

    copies = []
    for e in both:
        copies += [pltpu.make_async_copy(xq_hbm if e == 0 else xp_hbm, x_buf.at[e], sems.at[e * 5]), weight_copy(e, 0)]
    copies += [weight_copy(e, k) for k in (1, 2) for e in both]
    copies += [pltpu.make_async_copy(wo_hbm.at[e], wo_buf.at[e], sems.at[e * 5 + 4]) for e in both]
    ahead = 10
    start_all(copies[:ahead])

    def arrive(k):
        copies[k].wait()
        if k + ahead < len(copies):
            copies[k + ahead].start()

    mask = head_mask(rows, heads, width)
    pos = order_of(column([pos_ref[r] for r in range(rows)], rows), rows, depth)
    bounds = [row_bounds(pack if e else 0, plen_ref if e else qlen_ref, rows, lengths[e]) for e in both]
    start = [column([b[0] for b in bounds[e]], rows) for e in both]
    stop = [column([b[1] for b in bounds[e]], rows) for e in both]
    lane = lax.broadcasted_iota(jnp.int32, (rows, tokens), 1)
    pick = [jnp.where(lane == start[e], 1.0, 0.0).astype(BF) for e in both]
    x_cls, xc, q = [], [], []
    for e in both:
        arrive(2 * e)
        x_cls.append(mm(pick[e], x_buf[e]))
        xc.append(x_cls[e].astype(BF))
        arrive(2 * e + 1)
        q.append((mm(xc[e], w_buf[e, 0]) + bias_ref[e][0:1, :]).astype(BF))
    arrive(4)
    arrive(5)
    a_low = [mm(spread_heads(q[e], heads, mask), w_buf[e, 1], NT).astype(BF) for e in both]
    scores = [mm(a_low[e], x_buf[e], NT) * 0.125 for e in both]
    p_low, sums = [], []
    for e in both:
        a_ref[e] = a_low[e]
        lane_all = lax.broadcasted_iota(jnp.int32, scores[e].shape, 1)
        starts = jnp.concatenate([start[e]] * heads, axis=0)
        stops = jnp.concatenate([stop[e]] * heads, axis=0)
        allowed = jnp.where((lane_all >= starts) & (lane_all < stops), scores[e], MASKED)
        shifted = jnp.exp(allowed - jnp.max(allowed, axis=1, keepdims=True))
        p = shifted / jnp.sum(shifted, axis=1, keepdims=True)
        p_ref[e] = p
        p_low.append(p.astype(BF))
        sums.append(jnp.sum(p_low[e].astype(F32), axis=1, keepdims=True))
    pooled = [mm(p_low[e], x_buf[e]).astype(BF) for e in both]
    arrive(6)
    arrive(7)
    full = [mm(pooled[e], w_buf[e, 2]) + sums[e] * bias_ref[e][1:2, :] for e in both]
    ctx = [gather_heads(full[e], heads, rows, mask).astype(BF) for e in both]
    arrive(8)
    arrive(9)
    hidden = [x_cls[e] + mm(ctx[e], wo_buf[e]) + ob_ref[e:e + 1, :] for e in both]
    lanes = lax.broadcasted_iota(jnp.int32, (rows, EXTRA), 1)
    hat, extra = [], []
    for e in both:
        centred = hidden[e] - jnp.mean(hidden[e], axis=1, keepdims=True)
        rstd = lax.rsqrt(jnp.mean(centred * centred, axis=1, keepdims=True) + EPSILON)
        hat.append((centred * rstd).astype(BF))
        rstd_high = rstd.astype(BF).astype(F32)
        more = jnp.where(lanes == 0, rstd_high, 0.0)
        more = jnp.where(lanes == 1, rstd - rstd_high, more)
        more = jnp.where(lanes == 2, (pos // 32).astype(F32), more)
        more = jnp.where(lanes == 3, (pos % 32).astype(F32), more)
        for h in range(heads):
            more = jnp.where(lanes == 16 + h, sums[e][h * rows:(h + 1) * rows] - 1.0, more)
        extra.append(more.astype(BF))

    def put(e, pack_ref, early_ref):
        pack_ref[:, 0:width] = hat[e]
        pack_ref[:, width:] = extra[e]
        for chip in range(chips):
            slot = lax.rem(chip - j + chips, chips)
            cut = slice(chip * part, (chip + 1) * part)
            pieces = [pooled[e][h * rows:(h + 1) * rows, cut] for h in range(heads)] + [xc[e][:, cut], ctx[e][:, cut], q[e]]
            early_ref[slot] = jnp.concatenate(pieces, axis=1)

    @pl.when(c == 0)
    def even():
        put(0, pack_mine, early_mine)
        put(1, pack_other, early_other)

    @pl.when(c == 1)
    def odd():
        put(1, pack_mine, early_mine)
        put(0, pack_other, early_other)


def stage_kernel(ids, after_ref, win_hbm, wback_hbm, wout_hbm, xq_hbm, xp_hbm, w_hbm, win, wback, wout, x_buf, w_buf, sems):
    c = ids[0]
    width = wout.shape[0]
    copies = [pltpu.make_async_copy(win_hbm.at[c], win, sems.at[0]), pltpu.make_async_copy(wback_hbm.at[c], wback, sems.at[1]),
              pltpu.make_async_copy(wout_hbm.at[c], wout, sems.at[2]), pltpu.make_async_copy(xq_hbm, x_buf.at[0], sems.at[3]),
              pltpu.make_async_copy(xp_hbm, x_buf.at[1], sems.at[4])]
    for e in range(2):
        for k in range(3):
            copies.append(pltpu.make_async_copy(w_hbm.at[e, :, pl.ds(k * width, width)], w_buf.at[e, k], sems.at[5 + 3 * e + k]))
    start_all(copies)
    for copy in copies:
        copy.wait()


def gelu_parts(x):
    bell = jnp.exp(-0.5 * x * x)
    t = 1.0 / (1.0 + (0.3275911 * math.sqrt(0.5)) * jnp.abs(x))
    tail = 1.061405429 * 0.5
    for factor in (-1.453152027, 1.421413741, -0.284496736, 0.254829592):
        tail = tail * t + factor * 0.5
    tail = tail * t * bell
    cdf = jnp.where(x >= 0.0, 1.0 - tail, tail)
    return x * cdf, cdf + x * bell * (1.0 / math.sqrt(2.0 * math.pi))


def relative_places(chips, depth, rows, c, j, z):
    for kx in range(chips):
        for kz in range(depth):
            for kc in range(2):
                core = c if kc == 0 else 1 - c
                place = ((lax.rem(j - kx + chips, chips) * depth + lax.rem(z - kz + depth, depth)) * 2 + core) * rows
                yield kx, kz, kc, pl.multiple_of(place, rows)


def doubling(n, masks):
    found = [0]
    for mask in masks:
        found = found + [k ^ mask for k in found]
    assert sorted(found) == list(range(n))
    return found


def depth_masks(depth):
    return [(1 << k) - 1 for k in range(1, depth.bit_length())]


def chip_masks(chips):
    return [1 << k for k in range(chips.bit_length() - 1)]


def place_of(chip, deep, core, depth, rows):
    return pl.multiple_of(((chip * depth + deep) * 2 + core) * rows, rows)


def crossed_blocks(refs, chips, depth, rows, c, j, z, part, lead):
    near = depth // 2
    for at, dz in enumerate(doubling(depth, depth_masks(depth))):
        for kc in range(2):
            core = c if kc == 0 else 1 - c
            first = ((at % near) * 2 + kc) * rows
            for kx in range(chips):
                place = place_of(lax.rem(j - kx + chips, chips), jnp.bitwise_xor(z, dz), core, depth, rows)
                yield refs[at // near], first, lead + 2 * kx * part, place


def over_rows(count, tile, work):
    if tile == count:
        work(pl.ds(0, count))
    else:
        def one(t, carry):
            work(pl.ds(pl.multiple_of(t * tile, tile), tile))
            return carry

        lax.fori_loop(0, count // tile, one, 0)


def forward_kernel(chips, depth, rows, steps, tile, part, ids, *refs):
    blocks = refs[:chips]
    gain_ref, shift_ref, win_ref, inb_ref, wback_ref, backb_ref = refs[chips:chips + 6]
    _, act_ref, slope_ref, vec_ref, hat2_ref, ex_ref, cut_ref, hat1_ref, _, total, nl, chunk = refs[chips + 6:]
    c, j, z = ids[0], ids[1], ids[2]
    width = vec_ref.shape[1]
    step = pl.program_id(0)

    @pl.when(step == 0)
    def start():
        for kx, kz, kc, place in relative_places(chips, depth, rows, c, j, z):
            at = (kz * 2 + kc) * rows
            hat1_ref[pl.ds(place, rows), :] = blocks[kx][at:at + rows, 0:width]
            ex_ref[pl.ds(place, rows), :] = blocks[kx][at:at + rows, width:].astype(F32)
        gain = gain_ref[c]
        shift = shift_ref[c]
        normed = hat1_ref[...].astype(F32) * gain[0:1, :] + shift[0:1, :]
        low = normed.astype(BF)
        nl[...] = low
        total[...] = normed + backb_ref[pl.ds(c, 1), :]
        source = lax.broadcasted_iota(jnp.int32, (width, part), 0)
        target = lax.broadcasted_iota(jnp.int32, (width, part), 1) + j * part
        cut_ref[...] = mm(low, jnp.where(source == target, 1.0, 0.0).astype(BF)).astype(BF)

    columns = slope_ref.shape[1]
    at = pl.multiple_of(step * columns, columns)
    fpart = act_ref.shape[1]
    bias = inb_ref[pl.ds(c, 1), pl.ds(at, columns)]
    strips = 2
    strip = nl.shape[0] // strips
    spans = [slice(k * strip, (k + 1) * strip) for k in range(strips)]

    def up(span):
        return mm(nl[span, :], win_ref[:, pl.ds(at, columns)]) + bias

    def down(span, pre):
        active, slope = gelu_parts(pre)
        active = active.astype(BF)
        chunk[span, :] = active
        slope_ref[span, :] = slope.astype(BF)
        total[span, :] += mm(active, wback_ref[pl.ds(at, columns), :])

    pre = up(spans[0])
    for k in range(strips):
        following = up(spans[k + 1]) if k + 1 < strips else None
        down(spans[k], pre)
        pre = following
    for q in range(columns // fpart):
        @pl.when(step * (columns // fpart) + q == j)
        def keep():
            act_ref[...] = chunk[:, q * fpart:(q + 1) * fpart]

    @pl.when(step == steps - 1)
    def finish():
        gain = gain_ref[c]
        shift = shift_ref[c]

        def normalise(part):
            second = total[part, :]
            mean = jnp.mean(second, axis=1, keepdims=True)
            centred = second - mean
            rstd = lax.rsqrt(jnp.mean(centred * centred, axis=1, keepdims=True) + EPSILON)
            hat = centred * rstd
            hat2_ref[part, :] = hat.astype(BF)
            vec_ref[part, :] = (hat * gain[1:2, :] + shift[1:2, :]).astype(BF)
            ex = ex_ref[part, :]
            lanes = lax.broadcasted_iota(jnp.int32, ex.shape, 1)
            pos = ex[:, 2:3] * 32.0 + ex[:, 3:4]
            ex_ref[part, :] = jnp.where(
                lanes == 0, ex[:, 0:1] + ex[:, 1:2], jnp.where(lanes == 1, rstd, jnp.where(lanes == 2, pos, ex)))

        over_rows(total.shape[0], tile, normalise)


def norm_back(grad, hat, rstd, gain):
    scaled = grad * gain
    inner = jnp.mean(scaled * hat, axis=1, keepdims=True)
    return rstd * (scaled - jnp.mean(scaled, axis=1, keepdims=True) - hat * inner)


def loss_kernel(depth, rows, tile, ids, own_ref, other_ref, ex_ref, hat2_ref, hat1_ref, slope_ref, gain_ref,
                wback, win, wout, second_ref, loss_ref, mine_ref, sib_ref, small_ref, qvec_ref, pvec_ref,
                wide_loss):
    c, j, z = ids[0], ids[1], ids[2]
    count, width = own_ref.shape
    scale = 2.0 / math.sqrt(width)
    own_at = pl.multiple_of(((j * depth + z) * 2 + c) * rows, rows)

    def softmax_part(questions, passages, pos):
        scores = mm(questions, passages, NT) * scale
        peak = jnp.max(scores, axis=1, keepdims=True)
        shifted = jnp.exp(scores - peak)
        totals = jnp.sum(shifted, axis=1, keepdims=True)
        hit = lax.broadcasted_iota(jnp.int32, scores.shape, 1) == pos.astype(jnp.int32)
        loss = peak + jnp.log(totals) - jnp.sum(jnp.where(hit, scores, 0.0), axis=1, keepdims=True)
        grad = (shifted / totals - jnp.where(hit, 1.0, 0.0)) * scale
        high = grad.astype(BF)
        return loss, high, (grad - high.astype(F32)).astype(BF)

    @pl.when(c == 0)
    def question_side():
        qvec_ref[...] = own_ref[pl.ds(own_at, rows), :]
        pvec_ref[...] = other_ref[pl.ds(own_at, rows), :]

        def work(part):
            loss, high, low = softmax_part(own_ref[part, :], other_ref[...], ex_ref[part, 2:3])
            wide_loss[part, :] = jnp.broadcast_to(loss, (tile, wide_loss.shape[1]))
            second_ref[part, :] = mm(high, other_ref[...]) + mm(low, other_ref[...])

        over_rows(count, tile, work)

    @pl.when(c == 1)
    def passage_side():
        pvec_ref[...] = own_ref[pl.ds(own_at, rows), :]
        qvec_ref[...] = other_ref[pl.ds(own_at, rows), :]
        if tile < count:
            second_ref[...] = jnp.zeros_like(second_ref)

        def work(part):
            loss, high, low = softmax_part(other_ref[part, :], own_ref[...], ex_ref[part, 2:3])
            wide_loss[part, :] = jnp.broadcast_to(loss, (tile, wide_loss.shape[1]))
            piece = mm(high, other_ref[part, :], TN) + mm(low, other_ref[part, :], TN)
            second_ref[...] = piece if tile == count else second_ref[...] + piece

        over_rows(count, tile, work)

    small_ref[...] = jnp.zeros_like(small_ref)
    losses = wide_loss[pl.ds(own_at, rows), :]
    diagonal = lax.broadcasted_iota(jnp.int32, losses.shape, 0) == lax.broadcasted_iota(jnp.int32, losses.shape, 1)
    loss_ref[...] = jnp.sum(jnp.where(diagonal, losses, 0.0), axis=0, keepdims=True)[:, 0:rows]

    def late_norm(part):
        grad = second_ref[part, :]
        hat = hat2_ref[part, :].astype(F32)
        small_ref[1:2, :] += jnp.sum(grad * hat, axis=0, keepdims=True)
        small_ref[3:4, :] += jnp.sum(grad, axis=0, keepdims=True)
        second = norm_back(grad, hat, ex_ref[part, 1:2], gain_ref[c][1:2, :])
        small_ref[5:6, :] += jnp.sum(second, axis=0, keepdims=True)
        second_ref[part, :] = second

    over_rows(count, tile, late_norm)

    chip_at = pl.multiple_of((j * depth + z) * 2 * rows, 2 * rows)
    second = second_ref[pl.ds(chip_at, 2 * rows), :]
    pre = (mm(second.astype(BF), wback[...], NT) * slope_ref[...].astype(F32)).astype(BF)
    normed = second + mm(pre, win[...], NT)
    hidden = norm_back(normed, hat1_ref[...].astype(F32), ex_ref[pl.ds(chip_at, 2 * rows), 0:1], gain_ref[c][0:1, :])
    ctx = mm(hidden.astype(BF), wout[...], NT).astype(BF).astype(F32)
    both = jnp.concatenate([hidden, ctx], axis=1)
    is_low = c == 0
    mine_ref[...] = jnp.where(is_low, both[:rows], both[rows:])
    sib_ref[...] = jnp.where(is_low, both[rows:], both[:rows])


def split_halves(value, scratch, c, own_ref_set, sib_ref_set):
    half = value.shape[0] // 2
    scratch[...] = value
    own_ref_set(scratch[pl.ds(pl.multiple_of(c * half, half), half), :])
    sib_ref_set(scratch[pl.ds(pl.multiple_of((1 - c) * half, half), half), :].astype(BF))


def backward_kernel(chips, depth, rows, steps, tile, ids, near_ref, second_ref, ex_ref, hat1_ref, slope_ref, wback_ref, win_ref,
                    gain_ref, wout_ref, small_in, gpl_ref, low_ref, hidden_ref, plane_ref, small_ref, column_ref, acc, gfull):
    c, j, z = ids[0], ids[1], ids[2]
    count, width = second_ref.shape
    step = pl.program_id(0)

    @pl.when(step == 0)
    def start():
        acc[...] = second_ref[...]
        low_ref[...] = second_ref[...].astype(BF)
        column_ref[...] = near_ref[:, 0:width]
        small_ref[0:8, :] = small_in[...]
        small_ref[8:, :] = jnp.zeros((8, width), F32)

    columns = slope_ref.shape[1]
    at = pl.multiple_of(step * columns, columns)
    strip = count // 2
    bias = jnp.zeros((1, columns), F32)
    spans = [slice(k * strip, (k + 1) * strip) for k in range(2)]
    rising = [mm(low_ref[span, :], wback_ref[pl.ds(at, columns), :], NT) for span in spans]
    for span, grown in zip(spans, rising):
        pre = grown * slope_ref[span, :].astype(F32)
        bias = bias + jnp.sum(pre, axis=0, keepdims=True)
        pre_low = pre.astype(BF)
        gpl_ref[span, :] = pre_low
        acc[span, :] += mm(pre_low, win_ref[:, pl.ds(at, columns)], NT)
    for s in range(steps):
        @pl.when(step == s)
        def keep_bias():
            line, lane = 8 + s * columns // width, s * columns % width
            small_ref[line:line + 1, lane:lane + columns] = bias

    @pl.when(step == steps - 1)
    def finish():
        lanes = lax.broadcasted_iota(jnp.int32, (EXTRA, width), 0)
        heads_of = lax.broadcasted_iota(jnp.int32, (EXTRA, width), 1) // HEAD_DIM
        expand = jnp.where(lanes == heads_of + 16, 1.0, 0.0).astype(BF)

        def early_norm(part):
            grad = acc[part, :]
            hat = hat1_ref[part, :].astype(F32)
            small_ref[0:1, :] += jnp.sum(grad * hat, axis=0, keepdims=True)
            small_ref[2:3, :] += jnp.sum(grad, axis=0, keepdims=True)
            hidden = norm_back(grad, hat, ex_ref[part, 0:1], gain_ref[c][0:1, :])
            small_ref[4:5, :] += jnp.sum(hidden, axis=0, keepdims=True)
            hidden_low = hidden.astype(BF)
            hidden_ref[part, :] = hidden_low
            ctx = mm(hidden_low, wout_ref[...], NT).astype(BF)
            sums = mm(ex_ref[part, :].astype(BF), expand) + 1.0
            small_ref[6:7, :] += jnp.sum(sums * ctx.astype(F32), axis=0, keepdims=True)
            gfull[part, :] = ctx

        over_rows(count, tile, early_norm)
        for kx in range(chips):
            for kc in range(2):
                core = c if kc == 0 else 1 - c
                place = pl.multiple_of(((lax.rem(j - kx + chips, chips) * depth + z) * 2 + core) * rows, rows)
                at = (kx * 2 + kc) * rows
                plane_ref[at:at + rows, :] = gfull[pl.ds(place, rows), :]


def weight_kernel(chips, depth, rows, part, steps, ids, after_ref, near_ref, far_ref, gpl_ref, low_ref, hidden_ref, act_ref, cut_ref,
                  gin_ref, gback_ref, gout_ref, sib_ref, ctx_all, in_scr, back_scr, out_scr):
    c, j, z = ids[0], ids[1], ids[2]
    step = pl.program_id(0)
    width = low_ref.shape[1]
    half = part // 2
    ghalf = back_scr.shape[0] // 2
    columns = gpl_ref.shape[1]
    in_rows = half * (columns * steps // width)

    def set_own(ref):
        def setter(value):
            ref[0] = value
        return setter

    def set_sib(at, rows, lane, lanes):
        def setter(value):
            sib_ref[at:at + rows, lane:lane + lanes] = value
        return setter

    @pl.when(step == 0)
    def start():
        split_halves(mm(act_ref[...], low_ref[...], TN), back_scr, c, set_own(gback_ref), set_sib(in_rows, ghalf, 0, width))
        for ref, first, lane, place in crossed_blocks((near_ref, far_ref), chips, depth, rows, c, j, z, part, chips * part):
            ctx_all[pl.ds(place, rows), :] = ref[first:first + rows, lane + part:lane + 2 * part]
        split_halves(mm(ctx_all[...], hidden_ref[...], TN), out_scr, c, set_own(gout_ref), set_sib(in_rows + ghalf, half, 0, width))

    piece = mm(cut_ref[...], gpl_ref[...], TN)
    in_scr[...] = piece
    gin_ref[0] = in_scr[pl.ds(pl.multiple_of(c * half, half), half), :]
    other = in_scr[pl.ds(pl.multiple_of((1 - c) * half, half), half), :].astype(BF)
    for s in range(steps):
        @pl.when(step == s)
        def keep():
            set_sib((s * columns // width) * half, half, s * columns % width, columns)(other)


def attend_back_kernel(rows, heads, chips, ids, mine_ref, far_ref, x_buf, w_buf, bias_ref, p_ref, *refs):
    early = refs[:chips]
    late_mine, late_other, att_ref, b_ref, first_ref, cross_ref = refs[chips:]
    c, j = ids[0], ids[1]
    width = bias_ref.shape[2]
    part = width // chips
    cross_ref[...] = jnp.concatenate([b[:, heads * part:(heads + 2) * part] for b in early], axis=1)
    mask = head_mask(rows, heads, width)
    both = range(2)
    gg = [jnp.where(c == e, mine_ref[...], far_ref[...]) for e in both]
    blocks = [spread_heads(gg[e][:, width:], heads, mask) for e in both]
    constant = [jnp.sum(blocks[e] * bias_ref[e][1:2, :], axis=1, keepdims=True) for e in both]
    b_low = [mm(blocks[e].astype(BF), w_buf[e, 2], NT).astype(BF) for e in both]
    probs = [mm(b_low[e], x_buf[e], NT) + constant[e] for e in both]
    att = []
    for e in both:
        b_ref[e] = b_low[e]
        p = p_ref[e]
        att.append((p * (probs[e] - jnp.sum(probs[e] * p, axis=1, keepdims=True))).astype(BF))
        att_ref[e] = att[e]
    y_low = [mm(att[e], x_buf[e]).astype(BF) for e in both]
    gq_low = [(gather_heads(mm(y_low[e], w_buf[e, 1]), heads, rows, mask) * 0.125).astype(BF) for e in both]
    for e in both:
        first_ref[e] = gg[e][:, 0:width] + mm(gq_low[e], w_buf[e, 0], NT)

    def put(e, late_ref):
        for chip in range(chips):
            slot = lax.rem(chip - j + chips, chips)
            cut = slice(chip * part, (chip + 1) * part)
            pieces = [y_low[e][h * rows:(h + 1) * rows, cut] for h in range(heads)] + [gq_low[e]]
            late_ref[slot] = jnp.concatenate(pieces, axis=1)

    @pl.when(c == 0)
    def even():
        put(0, late_mine)
        put(1, late_other)

    @pl.when(c == 1)
    def odd():
        put(1, late_mine)
        put(0, late_other)


def token_grad_kernel(pack, lengths, rows, heads, ids, after_ref, qlen_ref, plen_ref, att_ref, p_ref, a_ref, b_ref, first_ref,
                      gq_ref, gp_ref):
    tile = gq_ref.shape[0]
    at = pl.program_id(0) * tile
    lane = lax.broadcasted_iota(jnp.int32, (rows, tile), 1) + at
    for e in range(2):
        bounds = row_bounds(pack if e else 0, plen_ref if e else qlen_ref, rows, lengths[e])
        pick = jnp.where(lane == column([b[0] for b in bounds], rows), 1.0, 0.0).astype(BF)
        first = first_ref[e]
        high = first.astype(BF)
        rest = first - high.astype(F32)
        middle = rest.astype(BF)
        last = (rest - middle.astype(F32)).astype(BF)
        left = jnp.concatenate([att_ref[e], p_ref[e].astype(BF), pick, pick, pick], axis=0)
        right = jnp.concatenate([a_ref[e] * jnp.asarray(0.125, BF), b_ref[e], high, middle, last], axis=0)
        out = gp_ref if e else gq_ref
        out[...] = mm(left, right, TN)


def head_sums(factor, vectors, heads, part):
    width = vectors.shape[1]
    full = mm(factor, vectors, TN)
    row_head = lax.broadcasted_iota(jnp.int32, full.shape, 0) // part
    col_head = lax.broadcasted_iota(jnp.int32, full.shape, 1) // HEAD_DIM
    kept = jnp.where(row_head == col_head, full, 0.0)
    return jnp.sum(kept.reshape(heads, part, width), axis=0)


def share_kernel(heads, chips, depth, part, ids, *refs):
    late = refs[:chips]
    early = refs[chips:2 * chips]
    plane_ref = refs[2 * chips]
    outs = refs[2 * chips + 2:2 * chips + 2 + depth]
    column_ref, scratch = refs[-2:]
    column_ref[...] = refs[2 * chips + 1][...]
    z = ids[2]
    width = plane_ref.shape[1]
    hp = heads * part
    y = jnp.concatenate([b[:, 0:hp] for b in late], axis=0)
    pooled = jnp.concatenate([b[:, 0:hp] for b in early], axis=0)
    q = jnp.concatenate([b[:, hp + 2 * part:] for b in early], axis=0)
    scratch[:, 0:width] = head_sums(y, q, heads, part) * 0.125
    scratch[:, width:] = head_sums(pooled, plane_ref[...], heads, part)
    span = 2 * width // depth
    for k in range(depth):
        at = pl.multiple_of(lax.rem(z + k, depth) * span, span)
        outs[k][...] = scratch[:, pl.ds(at, span)].astype(BF)


def query_kernel(chips, depth, rows, part, ids, sib_in, near_ref, far_ref, low_chips, high_chips, *refs):
    shares = refs[:depth]
    small_in, gw_ref, keep_ref, send_ref, rows_ref, sib_out, x_all, gq_all, q_scr, share_scr = refs[depth:]
    c, j, z = ids[0], ids[1], ids[2]
    for ref, first, lane, place in crossed_blocks((near_ref, far_ref), chips, depth, rows, c, j, z, part, chips * part):
        x_all[pl.ds(place, rows), :] = ref[first:first + rows, lane:lane + part]
    few = chips // 2
    for at_chip, dx in enumerate(doubling(chips, chip_masks(chips))):
        for at_depth, dz in enumerate(doubling(depth, depth_masks(depth))):
            for kc in range(2):
                core = c if kc == 0 else 1 - c
                place = place_of(jnp.bitwise_xor(j, dx), jnp.bitwise_xor(z, dz), core, depth, rows)
                at = (((at_chip % few) * depth + at_depth) * 2 + kc) * rows
                gq_all[pl.ds(place, rows), :] = (low_chips, high_chips)[at_chip // few][at:at + rows, :]
    gq = gq_all[...]
    half = part // 2
    width = gq.shape[1]
    span = shares[0].shape[1]
    bias = jnp.sum(gq.astype(F32), axis=0, keepdims=True)
    total = shares[0][...].astype(F32)
    for k in range(1, depth):
        total = total + shares[k][...].astype(F32)
    share_scr[...] = total
    q_scr[...] = mm(x_all[...], gq, TN)
    own = pl.ds(pl.multiple_of(c * half, half), half)
    sib = pl.ds(pl.multiple_of((1 - c) * half, half), half)
    keep_ref[...] = share_scr[own, :].astype(BF)
    gw_ref[...] = q_scr[own, :]
    send_ref[...] = share_scr[sib, :].astype(BF)
    rows_ref[0:half, :] = q_scr[sib, :]
    rows_ref[half:, :] = small_in[...]
    rows_ref[half + 7:half + 8, :] = bias


def assemble_kernel(depth, ids, after_ref, *refs):
    shards = refs[:depth]
    own_ref, far_ref, out_ref = refs[depth:]
    c, z = ids[0], ids[2]
    half, width = own_ref.shape
    span = shards[0].shape[1]
    out_ref[c, :, 0:width] = own_ref[...]
    out_ref[1 - c, :, 0:width] = far_ref[0:half, :]
    for k in range(depth):
        at = pl.multiple_of(width + lax.rem(z - k + depth, depth) * span, 128)
        out_ref[c, :, pl.ds(at, span)] = shards[k][0:half, :].astype(F32)
        out_ref[1 - c, :, pl.ds(at, span)] = shards[k][half:, :].astype(F32)


def fill_kernel(in_rows, ids, after_ref, in_hbm, back_hbm, out_hbm, sib_ref, own_ref, other_ref, gin_ref, gback_ref, gout_ref,
                qv_ref, outb_ref, gains_ref, shifts_ref, inb_ref, backb_ref):
    c = ids[0]
    half, width = gout_ref.shape[1], gout_ref.shape[2]
    ghalf = gback_ref.shape[1]
    for k in range(in_rows // half):
        gin_ref[0, :, k * width:(k + 1) * width] = sib_ref[k * half:(k + 1) * half, :].astype(F32)
    gback_ref[0] = sib_ref[in_rows:in_rows + ghalf, :].astype(F32)
    gout_ref[0] = sib_ref[in_rows + ghalf:, :].astype(F32)
    for e in range(2):
        small = jnp.where(c == e, own_ref[half:, :], other_ref[half:, :])
        gains_ref[e] = small[0:2]
        shifts_ref[e] = small[2:4]
        outb_ref[e:e + 1, :] = small[4:5]
        backb_ref[e:e + 1, :] = small[5:6]
        qv_ref[e, 0:1, :] = small[7:8]
        qv_ref[e, 1:2, :] = small[6:7]
        for k in range(inb_ref.shape[1] // width):
            inb_ref[e:e + 1, k * width:(k + 1) * width] = small[8 + k:9 + k]


def full_spec(shape):
    return pl.BlockSpec(tuple(shape), lambda *_: (0,) * len(shape))


def shape_of(shape, dtype):
    return jax.ShapeDtypeStruct(tuple(shape), dtype)


ANY = pl.BlockSpec(memory_space=pl.ANY)
SMEM = pl.BlockSpec(memory_space=pltpu.SMEM)


def kernel_call(name, kernel, ids, args, specs, outs, out_specs, scratch=(), grid=(1,), work=(0, 0), aliases=None, vmem=60):
    specs = [full_spec(a.shape) if s is None else s for a, s in zip(args, specs)]
    out_specs = [full_spec(o.shape) if s is None else s for o, s in zip(outs, out_specs)]
    return pl.pallas_call(
        kernel,
        grid_spec=pltpu.PrefetchScalarGridSpec(num_scalar_prefetch=1, grid=grid, in_specs=specs, out_specs=out_specs,
                                               scratch_shapes=list(scratch)),
        out_shape=list(outs),
        input_output_aliases=aliases or {},
        compiler_params=pltpu.CompilerParams(vmem_limit_bytes=vmem * 1024 * 1024),
        cost_estimate=pl.CostEstimate(flops=int(work[0]), bytes_accessed=int(work[1]), transcendentals=0),
        name=name,
    )(ids, *args)


def body(question_tokens, question_lengths, passage_tokens, passage_lengths, positives, w_qkv, qv_bias, w_out, out_bias,
         norm_gains, norm_biases, w_in, in_bias, w_back, back_bias, *, n_dp, depth):
    width = question_tokens.shape[2]
    heads = width // HEAD_DIM
    rows = question_tokens.shape[0]
    pack = passage_lengths.shape[1]
    lengths = (question_tokens.shape[1], passage_tokens.shape[1])
    tokens = rows * lengths[0]
    ff = w_in.shape[2]
    chips = n_dp // 2
    count = n_dp * depth * rows
    part = width // chips
    half = part // 2
    fpart = ff // chips
    hr = heads * rows
    i = lax.axis_index("dp")
    z = lax.axis_index("group")
    c, j = i % 2, i // 2
    ids = jnp.stack([c, j, z]).astype(jnp.int32)
    vm = pltpu.VMEM
    dma = pltpu.SemaphoreType.DMA

    def swap(x):
        return lax.ppermute(x, "dp", [(k, k ^ 1) for k in range(n_dp)])

    def to_chip(x, k):
        return lax.ppermute(x, "dp", [(s, ((s // 2 + k) % chips) * 2 + s % 2) for s in range(n_dp)])

    def to_depth(x, k):
        return lax.ppermute(x, "group", [(s, (s + k) % depth) for s in range(depth)])

    def over_depth(x):
        return [x] + [to_depth(x, k) for k in range(1, depth)]

    def over_plane(x):
        return [x] + [to_chip(x, k) for k in range(1, chips)]

    small_enough = count <= 1024
    kept = pl.BlockSpec(memory_space=pltpu.VMEM) if small_enough else None
    keep_shape = (lambda shape: pltpu.VMEM(shape, BF)) if small_enough else (lambda shape: shape_of(shape, BF))

    xq = question_tokens.reshape(tokens, width)
    xp = passage_tokens.reshape(tokens, width)

    wide = (heads + 2) * part + width
    pack_mine, pack_other, early_mine, early_other, a_low, probs = kernel_call(
        "attend", functools.partial(attend_kernel, pack, lengths, rows, heads, chips, depth), question_lengths,
        [passage_lengths, positives, xq, xp, w_qkv, w_out, qv_bias, out_bias],
        [SMEM, SMEM, ANY, ANY, ANY, ANY, None, None],
        [shape_of((rows, width + EXTRA), BF)] * 2 + [shape_of((chips, rows, wide), BF)] * 2 + [
            shape_of((2, hr, width), BF), shape_of((2, hr, tokens), F32)],
        [None] * 6,
        [vm((2, tokens, width), BF), vm((2, 3, width, width), BF), vm((2, width, width), BF), dma((10,))],
        vmem=60 if count <= 1024 else 60, work=(6e9, 13e6))

    pair = jnp.concatenate([pack_mine, swap(pack_other)], axis=0)
    column_rows = jnp.concatenate(over_depth(pair), axis=0)
    plane = over_plane(column_rows)
    win_kept, wback_kept, wout_kept, x_kept, w_kept = kernel_call(
        "stage", stage_kernel, ids, [column_rows, w_in, w_back, w_out, xq, xp, w_qkv], [ANY] * 7,
        [keep_shape((width, ff)), keep_shape((ff, width)), keep_shape((width, width)), keep_shape((2, tokens, width)),
         keep_shape((2, 3, width, width))], [kept] * 5, [dma((11,))],
        vmem=24 if count <= 1024 else 60, work=(5e9, 10e6))

    fc = max(fpart, 384)
    steps = ff // fc
    tile = count if count <= 1024 else 128
    row = lambda w: full_spec((count, w))
    act, slope, vec, hat2, ex, cut, hat1, early_other = kernel_call(
        "forward", functools.partial(forward_kernel, chips, depth, rows, steps, tile, part), ids,
        plane + [norm_gains, norm_biases, win_kept, in_bias, wback_kept, back_bias, early_other],
        [None] * chips + [None, None, kept, None, kept, None, ANY],
        [shape_of((count, fpart), BF), shape_of((count, ff), BF), shape_of((count, width), BF),
         shape_of((count, width), BF), shape_of((count, EXTRA), F32), shape_of((count, part), BF), shape_of((count, width), BF),
         shape_of(early_other.shape, BF)],
        [None, pl.BlockSpec((count, fc), lambda s, ids: (0, s)), None, None, None, None, None, ANY],
        [vm((count, width), F32), vm((count, width), BF), vm((count, fc), BF)], grid=(steps,), vmem=24 if count <= 1024 else 60, work=(10e9, 18e6),
        aliases={1 + chips + 6: 7})

    vec_other = swap(vec)
    hp = heads * part

    early_far = swap(early_other)
    payload = [jnp.concatenate([early_mine[k], early_far[k]], axis=0) for k in range(chips)]
    early = [payload[0]] + [to_chip(payload[k], k) for k in range(1, chips)]

    chip_block = lambda w: pl.BlockSpec((2 * rows, w), lambda s, ids: (ids[1] * depth + ids[2], 0))
    second, loss, gg_mine, gg_sib, small, q_vectors, p_vectors = kernel_call(
        "loss", functools.partial(loss_kernel, depth, rows, tile), ids,
        [vec, vec_other, ex, hat2, hat1, slope, norm_gains, wback_kept, win_kept, wout_kept],
        [None, None, None, None, chip_block(width), chip_block(ff), None, kept, kept, kept],
        [shape_of((count, width), F32), shape_of((1, rows), F32), shape_of((rows, 2 * width), F32),
         shape_of((rows, 2 * width), F32), shape_of((8, width), F32), shape_of((rows, width), BF), shape_of((rows, width), BF)],
        [None] * 7,
        [vm((count, EXTRA), F32)],
        vmem=24 if count <= 1024 else 60, work=(8e9, 16e6))

    late_mine, late_other, att, b_low, first_rows, crossed = kernel_call(
        "attend_back", functools.partial(attend_back_kernel, rows, heads, chips), ids,
        [gg_mine, swap(gg_sib), x_kept, w_kept, qv_bias, probs] + early,
        [None, None, kept, kept, None, None] + [None] * chips,
        [shape_of((chips, rows, hp + width), BF)] * 2 + [
            shape_of((2, hr, tokens), BF), shape_of((2, hr, width), BF), shape_of((2, rows, width), F32),
            shape_of((2 * rows, 2 * width), BF)],
        [None] * 6,
        vmem=24 if count <= 1024 else 60, work=(6e9, 16e6))

    late_far = swap(late_other)
    payload = [jnp.concatenate([late_mine[k], late_far[k]], axis=0) for k in range(chips)]
    late = [payload[0]] + [to_chip(payload[k], k) for k in range(1, chips)]

    def xor_depth(x, mask):
        return lax.ppermute(x, "group", [(s, s ^ mask) for s in range(depth)])

    def xor_chip(x, mask):
        return lax.ppermute(x, "dp", [(s, s ^ (2 * mask)) for s in range(n_dp)])

    def double(x, step, masks):
        for mask in masks:
            x = jnp.concatenate([x, step(x, mask)], axis=0)
        return x

    near = double(jnp.concatenate([payload[0][:, hp:], crossed], axis=1), xor_depth, depth_masks(depth)[:-1])
    far_z = xor_depth(near, depth_masks(depth)[-1])
    gpl, low, hidden_low, g_plane, small, gq_near = kernel_call(
        "backward", functools.partial(backward_kernel, chips, depth, rows, steps, tile), ids,
        [near, second, ex, hat1, slope, wback_kept, win_kept, norm_gains, wout_kept, small],
        [None, None, None, None, pl.BlockSpec((count, fc), lambda s, ids: (0, s)),
         kept, kept, None, kept, None],
        [shape_of((count, ff), BF), shape_of((count, width), BF), shape_of((count, width), BF),
         shape_of((chips * 2 * rows, width), BF), shape_of((16, width), F32), shape_of((near.shape[0], width), BF)],
        [pl.BlockSpec((count, fc), lambda s, ids: (0, s)), None, None, None, None, None],
        [vm((count, width), F32), vm((count, width), BF)], grid=(steps,), vmem=26 if count <= 1024 else 60, work=(12e9, 18e6))

    gq_column = jnp.concatenate([gq_near, far_z[:, 0:width]], axis=0)

    span = 2 * width // depth
    *shares, gq_first = kernel_call(
        "share", functools.partial(share_kernel, heads, chips, depth, part), ids,
        late + early + [g_plane, gq_column], [None] * (2 * chips + 2),
        [shape_of((part, span), BF)] * depth + [shape_of(gq_column.shape, BF)], [None] * (depth + 1),
        [vm((part, 2 * width), F32)], vmem=24 if count <= 1024 else 60, work=(1e9, 3e6))
    masks = chip_masks(chips)
    gq_low = jnp.concatenate([gq_first, xor_chip(gq_column, masks[0])], axis=0)
    gq_low = double(gq_low, xor_chip, masks[1:-1])
    gq_high = xor_chip(gq_low, masks[-1])
    shares = [shares[0]] + [to_depth(shares[k], k) for k in range(1, depth)]

    ghalf = fpart // 2
    out_block = lambda r, w: pl.BlockSpec((1, r, w), lambda s, ids: (ids[0], 0, 0))
    in_rows = half * ff // width
    gin, gback, gout, sib = kernel_call(
        "weight", functools.partial(weight_kernel, chips, depth, rows, part, steps), ids,
        [shares[0], near, far_z, gpl, low, hidden_low, act, cut],
        [ANY, None, None, pl.BlockSpec((count, fc), lambda s, ids: (0, s)), None, None,
         None, None],
        [shape_of((2, half, ff), F32), shape_of((2, ghalf, width), F32), shape_of((2, half, width), F32),
         shape_of((in_rows + ghalf + half, width), BF)],
        [pl.BlockSpec((1, half, fc), lambda s, ids: (ids[0], 0, s)), out_block(ghalf, width), out_block(half, width), None],
        [vm((count, part), BF), vm((part, fc), F32), vm((fpart, width), F32), vm((part, width), F32)],
        grid=(steps,), vmem=24 if count <= 1024 else 60, work=(4e9, 12e6))
    gw_q, keep, send, rows_q, sib = kernel_call(
        "query", functools.partial(query_kernel, chips, depth, rows, part), ids,
        [sib, near, far_z, gq_low, gq_high] + shares + [small], [ANY] + [None] * (depth + 5),
        [shape_of((half, width), F32), shape_of((half, span), BF), shape_of((half, span), BF), shape_of((half + 16, width), F32),
         shape_of(sib.shape, BF)],
        [None] * 4 + [ANY],
        [vm((count, part), BF), vm((count, width), BF), vm((part, width), F32), vm((part, span), F32)], vmem=20 if count <= 1024 else 60, aliases={1: 4}, work=(1e9, 3e6))
    far = swap(send)
    sib_far = swap(sib)
    far_q = swap(rows_q)
    shards = over_depth(jnp.concatenate([keep, far], axis=0))
    gx = kernel_call(
        "token_grad", functools.partial(token_grad_kernel, pack, lengths, rows, heads), ids,
        [far, question_lengths, passage_lengths, att, probs, a_low, b_low, first_rows],
        [ANY, SMEM, SMEM, pl.BlockSpec((2, hr, 256), lambda s, ids: (0, 0, s)),
         pl.BlockSpec((2, hr, 256), lambda s, ids: (0, 0, s)), None, None, None],
        [shape_of((tokens, width), F32)] * 2, [pl.BlockSpec((256, width), lambda s, ids: (s, 0))] * 2,
        grid=(tokens // 256,), vmem=24 if count <= 1024 else 60, work=(2e9, 9e6))

    gin, gback, gout, g_qv, g_outb, g_gains, g_shifts, g_inb, g_backb = kernel_call(
        "fill", functools.partial(fill_kernel, in_rows), ids, [gx[0], gin, gback, gout, sib_far, rows_q, far_q],
        [ANY, ANY, ANY, ANY, None, None, None],
        [shape_of(gin.shape, F32), shape_of(gback.shape, F32), shape_of(gout.shape, F32), shape_of((2, 2, width), F32),
         shape_of((2, width), F32), shape_of((2, 2, width), F32), shape_of((2, 2, width), F32), shape_of((2, ff), F32),
         shape_of((2, width), F32)],
        [pl.BlockSpec((1,) + a.shape[1:], lambda s, ids: (1 - ids[0], 0, 0)) for a in (gin, gback, gout)] + [None] * 6,
        aliases={2: 0, 3: 1, 4: 2}, vmem=20 if count <= 1024 else 60, work=(1e6, 8e6))

    (g_qkv,) = kernel_call(
        "assemble", functools.partial(assemble_kernel, depth), ids, [gout] + shards + [gw_q, far_q], [ANY] + [None] * (depth + 2),
        [shape_of((2, half, 3 * width), F32)], [None], vmem=20 if count <= 1024 else 60, work=(1e6, 3e6))

    return (
        q_vectors,
        p_vectors,
        loss.reshape(rows),
        gx[0].reshape(question_tokens.shape),
        gx[1].reshape(passage_tokens.shape),
        g_qkv,
        g_qv,
        gout,
        g_outb,
        g_gains,
        g_shifts,
        gin,
        g_inb,
        gback,
        g_backb,
    )


def solution(mesh):
    split = P(("dp", "group"))
    return jax.shard_map(
        functools.partial(body, n_dp=mesh.shape["dp"], depth=mesh.shape["group"]),
        mesh=mesh,
        in_specs=(split, split, split, split, split) + (P(),) * 10,
        out_specs=(split, split, split, split, split, P(None, "dp", None), P(), P(None, "dp", None), P(), P(), P(),
                   P(None, "dp", None), P(), P(None, "dp", None), P()),
        check_vma=False,
    )
```
